128 devices in a mesh: seed: 8 (over y, z_hi), tok: 16 (over z_lo, x, core).
Axes of the slice: x: 4, y: 4, z: 4 (z_hi: 2, z_lo: 2; z = z_hi * 2 + z_lo), core: 2. Of those that a mesh axis runs over, the one named last changes fastest.
Arguments:
- atom_feats: bfloat16 [16384, 16, 128], P('tok', 'seed'), may hold values from -6 to 6
- atom_index: int32 [16384], P('tok'), may hold values from 0 to 2047, as said below
- token_cond: bfloat16 [2048, 768], P('tok'), may hold values from -6 to 6
- pair_bias: bfloat16 [16, 2048, 2048], P('seed', 'tok'), may hold values from -8 to 248
- atom_bias_enc: bfloat16 [16384, 4, 128], P('tok'), may hold values from -8 to 248
- atom_bias_dec: bfloat16 [16384, 4, 128], P('tok'), may hold values from -8 to 248
- enc_project: bfloat16 [128, 384], replicated, may hold values from -0.5 to 0.5
- enc_mix: bfloat16 [128, 128], replicated, may hold values from -0.5 to 0.5
- pool_weight: bfloat16 [128, 768], replicated, may hold values from -0.5 to 0.5
- token_project: bfloat16 [768, 3072], replicated, may hold values from -0.21875 to 0.21875
- token_mix: bfloat16 [768, 768], replicated, may hold values from -0.21875 to 0.21875
- swiglu_in: bfloat16 [768, 3072], replicated, may hold values from -0.21875 to 0.21875
- swiglu_out: bfloat16 [1536, 768], replicated, may hold values from -0.15625 to 0.15625
- spread_weight: bfloat16 [768, 128], replicated, may hold values from -0.21875 to 0.21875
- dec_project: bfloat16 [128, 384], replicated, may hold values from -0.5 to 0.5
- dec_mix: bfloat16 [128, 128], replicated, may hold values from -0.5 to 0.5
Outputs:
- token_state: bfloat16 [2048, 16, 768], P('tok', 'seed')
- atom_update: bfloat16 [16384, 16, 128], P('tok', 'seed')
The draws below stay inside these ranges and needn't reach their ends.
Inputs may be any that keep to these rules, and one draw needn't show every extreme that they name: `atom_index`: Nondecreasing. The atoms of token t are rows 8 t + e(t) to 8 (t + 1) + e(t + 1) - 1, every e between -3 and 3, e(0) = e(2048) = 0, and e(t) between -3 and -2 for every other t that is a multiple of 128; so every token has 2 to 14 atoms.
All inputs are finite; a program needn't handle non-finite values.
Results may differ from the reference program's by a relative error of at most 0.015.
Values may be sent and summed in bfloat16 or wider, within the bound.
No kernel may reach another device: no remote copies, remote signals or barrier semaphores. Data moves between devices by JAX's collectives and lax.ppermute only.
A program may use at most 192 MiB of HBM per device.

```python
import jax
import jax.numpy as jnp
from jax import lax

CT = 768
HEADS = 16
CA = 128
ATOM_HEADS = 4
QUERY_BLOCK = 32
KEY_WINDOW = 128
ATOMS_PER_TOKEN = 8
TOK_DEV = 128
HEAD_SIZE = 48
ATOM_HEAD_SIZE = 32
TRANS = 1536
TOKENS = 2048
ATOMS = 16384
SEEDS = 16


def clipped_normal(key, shape):
    return jnp.clip(jax.random.normal(jax.random.fold_in(key, 1), shape, jnp.float32), -4.0, 4.0)


def draw_atom_index(key, part):
    key = jax.random.fold_in(key, 5)
    bounds = jnp.arange(TOKENS + 1, dtype=jnp.int32)
    offsets = jax.random.randint(key, (TOKENS + 1,), -3, 4)
    edge_offsets = jax.random.randint(jax.random.fold_in(key, 9), (TOKENS + 1,), -3, -1)
    offsets = jnp.where(bounds % TOK_DEV == 0, edge_offsets, offsets)
    offsets = jnp.where((bounds == 0) | (bounds == TOKENS), 0, offsets)
    starts = ATOMS_PER_TOKEN * bounds + offsets
    atoms = jnp.arange(ATOMS, dtype=jnp.int32)
    guess = atoms // ATOMS_PER_TOKEN
    here = jnp.take(starts, guess)
    after = jnp.take(starts, jnp.minimum(guess + 1, TOKENS))
    found = guess - 1 + (here <= atoms).astype(jnp.int32) + (after <= atoms).astype(jnp.int32)
    return found.astype(jnp.int32)


def draw_pair_bias(key, part):
    key = jax.random.fold_in(key, 11)
    shape = (HEADS, TOKENS, TOKENS)
    base = clipped_normal(key, shape)
    return base.astype(jnp.bfloat16)


def draw_atom_bias_enc(key, part):
    key = jax.random.fold_in(key, 12)
    shape = (ATOMS, ATOM_HEADS, KEY_WINDOW)
    base = clipped_normal(key, shape)
    return base.astype(jnp.bfloat16)


def draw_atom_bias_dec(key, part):
    key = jax.random.fold_in(key, 13)
    shape = (ATOMS, ATOM_HEADS, KEY_WINDOW)
    base = clipped_normal(key, shape)
    return base.astype(jnp.bfloat16)


def steps_of(stream_key, dims, split, low, largest):
    level = 1.0
    for dim, shards_of in split:
        steps = jax.random.uniform(jax.random.fold_in(jax.random.fold_in(stream_key, 6), dim), (shards_of,), jnp.float32, low / len(split), largest / len(split))
        level = level * jnp.repeat(jnp.exp(steps), dims[dim] // shards_of).reshape((-1,) + (1,) * (len(dims) - 1 - dim))
    return level


def gaussian(own_key, shape, scale, bound, shards=(), kind=jnp.bfloat16):
    loudness = steps_of(own_key, shape, shards, -0.22, 0.18) if shards else 1.0
    values = jax.random.normal(own_key, shape, jnp.float32) * scale * loudness
    return jnp.minimum(jnp.maximum(values, -bound), bound).astype(kind)


def setup_inputs(seed: int = 0) -> dict:
    seeds = jax.random.split(jax.random.key(seed), 17)
    atom_feats = gaussian(seeds[0], (ATOMS, SEEDS, CA), 1.0, 6.0, ((0, 16), (1, 8)))
    atom_index = draw_atom_index(jax.random.fold_in(seeds[16], 71), 0)
    token_cond = gaussian(seeds[2], (TOKENS, CT), 1.0, 6.0, ((0, 16),))
    pair_bias = draw_pair_bias(jax.random.fold_in(seeds[16], 71), 0)
    atom_bias_enc = draw_atom_bias_enc(jax.random.fold_in(seeds[16], 71), 0)
    atom_bias_dec = draw_atom_bias_dec(jax.random.fold_in(seeds[16], 71), 0)
    enc_project = gaussian(seeds[6], (CA, 3 * CA), CA ** -0.5, 0.5)
    enc_mix = gaussian(seeds[7], (CA, CA), CA ** -0.5, 0.5)
    pool_weight = gaussian(seeds[8], (CA, CT), CA ** -0.5, 0.5)
    token_project = gaussian(seeds[9], (CT, 4 * CT), CT ** -0.5, 0.21875)
    token_mix = gaussian(seeds[10], (CT, CT), CT ** -0.5, 0.21875)
    swiglu_in = gaussian(seeds[11], (CT, 2 * TRANS), CT ** -0.5, 0.21875)
    swiglu_out = gaussian(seeds[12], (TRANS, CT), TRANS ** -0.5, 0.15625)
    spread_weight = gaussian(seeds[13], (CT, CA), CT ** -0.5, 0.21875)
    dec_project = gaussian(seeds[14], (CA, 3 * CA), CA ** -0.5, 0.5)
    dec_mix = gaussian(seeds[15], (CA, CA), CA ** -0.5, 0.5)
    return {"atom_feats": atom_feats, "atom_index": atom_index, "token_cond": token_cond, "pair_bias": pair_bias, "atom_bias_enc": atom_bias_enc, "atom_bias_dec": atom_bias_dec, "enc_project": enc_project, "enc_mix": enc_mix, "pool_weight": pool_weight, "token_project": token_project, "token_mix": token_mix, "swiglu_in": swiglu_in, "swiglu_out": swiglu_out, "spread_weight": spread_weight, "dec_project": dec_project, "dec_mix": dec_mix}


EPS = 1e-05
NEGATIVE = -1000000000.0

def layer_norm(values):
    centre = values - lax.optimization_barrier(jnp.mean(values, axis=-1, keepdims=True))
    variance = lax.optimization_barrier(jnp.mean(centre * centre, axis=-1, keepdims=True))
    return centre * lax.rsqrt(variance + EPS)

def window_attend(packed, bias):
    atom_total = packed.shape[0]
    block_count = atom_total // QUERY_BLOCK
    margin = (KEY_WINDOW - QUERY_BLOCK) // 2
    extra_tiles = KEY_WINDOW // QUERY_BLOCK - 1
    queries = packed[:, :CA].astype(jnp.float32).reshape(block_count, QUERY_BLOCK, ATOM_HEADS, ATOM_HEAD_SIZE)
    padded = jnp.pad(packed[:, CA:], ((margin, margin), (0, 0)))
    key_tiles = padded.reshape(block_count + extra_tiles, QUERY_BLOCK, 2 * CA)
    windows = jnp.concatenate([key_tiles[offset:offset + block_count] for offset in range(extra_tiles + 1)], axis=1)
    key_rows = windows[:, :, :CA].astype(jnp.float32).reshape(block_count, KEY_WINDOW, ATOM_HEADS, ATOM_HEAD_SIZE)
    value_rows = windows[:, :, CA:].astype(jnp.float32).reshape(block_count, KEY_WINDOW, ATOM_HEADS, ATOM_HEAD_SIZE)
    scores = jnp.einsum('bqhd,bkhd->bhqk', queries, key_rows) * ATOM_HEAD_SIZE ** (-0.5)
    scores = scores + bias.astype(jnp.float32).reshape(block_count, QUERY_BLOCK, ATOM_HEADS, KEY_WINDOW).transpose(0, 2, 1, 3)
    position = QUERY_BLOCK * jnp.arange(block_count, dtype=jnp.int32)[:, None] - margin + jnp.arange(KEY_WINDOW, dtype=jnp.int32)[None, :]
    in_range = (position >= 0) & (position < atom_total)
    scores = jnp.where(in_range[:, None, None, :], scores, NEGATIVE)
    row_max = lax.optimization_barrier(jnp.max(scores, axis=-1, keepdims=True))
    weights = jnp.exp(scores - row_max)
    rounded = lax.optimization_barrier(weights.astype(jnp.bfloat16)).astype(jnp.float32)
    attended_atoms = jnp.einsum('bhqk,bkhd->bqhd', rounded, value_rows)
    attended_atoms = attended_atoms / lax.optimization_barrier(jnp.sum(weights, axis=-1)).transpose(0, 2, 1)[..., None]
    return attended_atoms.reshape(atom_total, CA).astype(jnp.bfloat16)

def atom_block(inputs, bias, project, mix):
    normed = layer_norm(inputs.astype(jnp.float32)).astype(jnp.bfloat16)
    packed = jnp.dot(normed, project, preferred_element_type=jnp.float32).astype(jnp.bfloat16)
    attended_atoms = window_attend(packed, bias)
    return (inputs.astype(jnp.float32) + jnp.dot(attended_atoms, mix, preferred_element_type=jnp.float32)).astype(jnp.bfloat16)

def head_attend(operands):
    head_query, head_key, head_value, head_bias = operands
    scores = jnp.dot(head_query, head_key.T, preferred_element_type=jnp.float32) * HEAD_SIZE ** (-0.5)
    scores = scores + head_bias.astype(jnp.float32)
    row_max = lax.optimization_barrier(jnp.max(scores, axis=-1, keepdims=True))
    weights = jnp.exp(scores - row_max)
    rounded = lax.optimization_barrier(weights.astype(jnp.bfloat16))
    summed = jnp.dot(rounded, head_value, preferred_element_type=jnp.float32)
    return summed / lax.optimization_barrier(jnp.sum(weights, axis=-1, keepdims=True))

def split_heads(values):
    return values.reshape(TOKENS, HEADS, HEAD_SIZE).transpose(1, 0, 2)

def reference(atom_feats, atom_index, token_cond, pair_bias, atom_bias_enc, atom_bias_dec, enc_project, enc_mix, pool_weight, token_project, token_mix, swiglu_in, swiglu_out, spread_weight, dec_project, dec_mix):
    counts = jax.ops.segment_sum(jnp.ones(atom_index.shape, jnp.float32), atom_index, num_segments=TOKENS)

    def one_seed(atoms):
        encoded = atom_block(atoms, atom_bias_enc, enc_project, enc_mix)
        lifted = jnp.maximum(jnp.dot(encoded, pool_weight, preferred_element_type=jnp.float32), 0.0).astype(jnp.bfloat16)
        pooled_sum = jax.ops.segment_sum(lifted.astype(jnp.float32), atom_index, num_segments=TOKENS)
        residual = token_cond.astype(jnp.float32) + pooled_sum / counts[:, None]
        normed = layer_norm(residual).astype(jnp.bfloat16)
        projected = jnp.dot(normed, token_project, preferred_element_type=jnp.float32)
        queries = projected[:, :CT].astype(jnp.bfloat16)
        key_rows = projected[:, CT:2 * CT].astype(jnp.bfloat16)
        value_rows = projected[:, 2 * CT:3 * CT].astype(jnp.bfloat16)
        gate_open = jax.nn.sigmoid(projected[:, 3 * CT:])
        attended = lax.map(head_attend, (split_heads(queries), split_heads(key_rows), split_heads(value_rows), pair_bias))
        attended = attended.transpose(1, 0, 2).reshape(TOKENS, CT)
        gated_out = (attended * gate_open).astype(jnp.bfloat16)
        residual = residual + jnp.dot(gated_out, token_mix, preferred_element_type=jnp.float32)
        widened = jnp.dot(layer_norm(residual).astype(jnp.bfloat16), swiglu_in, preferred_element_type=jnp.float32)
        hidden = (jax.nn.silu(widened[:, :TRANS]) * widened[:, TRANS:]).astype(jnp.bfloat16)
        token_state = (residual + jnp.dot(hidden, swiglu_out, preferred_element_type=jnp.float32)).astype(jnp.bfloat16)
        spread = jnp.dot(token_state, spread_weight, preferred_element_type=jnp.float32).astype(jnp.bfloat16)
        decoded_in = (encoded.astype(jnp.float32) + spread[atom_index].astype(jnp.float32)).astype(jnp.bfloat16)
        atom_update = atom_block(decoded_in, atom_bias_dec, dec_project, dec_mix)
        return (token_state, atom_update)
    token_state, atom_update = lax.map(one_seed, atom_feats.transpose(1, 0, 2))
    return (token_state.transpose(1, 0, 2), atom_update.transpose(1, 0, 2))
```

```python
import functools

import jax
import jax.numpy as jnp
from jax import lax
from jax.experimental import pallas as pl
from jax.experimental.pallas import tpu as pltpu
from jax.sharding import PartitionSpec as P

EPS = 1e-05
NEG = -1000000000.0
F32 = jnp.float32
BF16 = jnp.bfloat16

SEEDS = 2
ATOMS = 1024
TOKS = 128
CA = 128
CT = 768
HEADS = 16
HEAD = 48
PAIR = 96
GROUPS = 8
QB = 32
WIN = 128
MARGIN = 48
LOWER = 80
EXT = 1152
EDGE = 16
TRANS = 1536
ALL_TOKS = 2048
ALL_ATOMS = 16384


def params(limit_mb, **more):
    return pltpu.CompilerParams(vmem_limit_bytes=limit_mb * 1024 * 1024, **more)


def vmem(n):
    return [pl.BlockSpec(memory_space=pltpu.VMEM)] * n


def layer_norm(values):
    centre = values - jnp.mean(values, axis=-1, keepdims=True)
    variance = jnp.mean(centre * centre, axis=-1, keepdims=True)
    return centre * lax.rsqrt(variance + EPS)


def dot(a, b):
    return jnp.dot(a, b, preferred_element_type=F32)


def dot_t(a, b):
    return lax.dot_general(a, b, (((1,), (1,)), ((), ())), preferred_element_type=F32)


def window_blocks(packed, bias, mixed, blocks, first_atom, unroll):
    lane_head = lax.broadcasted_iota(jnp.int32, (QB, CA), 1) // 32
    lane = lax.broadcasted_iota(jnp.int32, (1, WIN), 1)

    def body(b, carry):
        rows = pl.multiple_of(b * QB, QB)
        query_rows = pl.multiple_of(b * QB + MARGIN, 16)
        bias_rows = pl.multiple_of(b * 4 * QB, 4 * QB)
        added = jnp.concatenate(
            [bias[pl.ds(bias_rows + h, QB, stride=4), :] for h in range(4)], axis=0
        )
        position = lane + (first_atom + b * QB)
        inside = (position >= 0) & (position < ALL_ATOMS)
        added = jnp.where(inside, added, NEG)
        for seed in range(SEEDS):
            query = packed[seed, pl.ds(query_rows, QB), 0:CA]
            key = packed[seed, pl.ds(rows, WIN), CA : 2 * CA]
            value = packed[seed, pl.ds(rows, WIN), 2 * CA : 3 * CA]
            stacked = jnp.concatenate(
                [jnp.where(lane_head == h, query, jnp.zeros_like(query)) for h in range(4)], axis=0
            )
            scores = dot_t(stacked, key) * (32**-0.5)
            scores = jnp.where(inside, scores + added, NEG)
            top = jnp.max(scores, axis=-1, keepdims=True)
            weights = jnp.exp(scores - top)
            total = jnp.sum(weights, axis=-1, keepdims=True)
            out = dot(weights.astype(BF16), value) / total
            joined = jnp.zeros((QB, CA), F32)
            for h in range(4):
                joined = joined + jnp.where(lane_head == h, out[h * QB : (h + 1) * QB], 0.0)
            mixed[seed, pl.ds(rows, QB), :] = joined.astype(BF16)
        return carry

    lax.fori_loop(0, blocks, body, 0, unroll=unroll)


def encode_kernel(
    tok, feats, low, high, bias, index, cond, project, mix, pool,
    encoded, residual, normed,
    rows, bias32, packed, mixed, ext,
):
    rows[0 : 2 * LOWER] = low[0 : 2 * LOWER].astype(F32)
    rows[2 * LOWER : 2 * (LOWER + ATOMS)] = feats[...].astype(F32)
    rows[2 * (LOWER + ATOMS) : 2 * EXT] = high[0 : 2 * MARGIN].astype(F32)
    bias32[0 : 4 * QB] = low[2 * LOWER : 2 * LOWER + 4 * QB].astype(F32)
    bias32[4 * QB :] = bias[...].astype(F32)
    for seed in range(SEEDS):
        values = rows[pl.ds(seed, EXT, stride=2), :]
        packed[seed] = dot(layer_norm(values).astype(BF16), project[...]).astype(BF16)
    window_blocks(packed, bias32, mixed, 33, tok[0] * ATOMS - QB - MARGIN, 3)
    chosen = (index[...] == lax.broadcasted_iota(jnp.int32, (TOKS, EXT), 0).astype(F32)).astype(F32)
    counts = jnp.sum(chosen, axis=1, keepdims=True)
    chosen = chosen.astype(BF16)
    for seed in range(SEEDS):
        values = rows[pl.ds(2 * MARGIN + seed, QB + ATOMS, stride=2), :]
        ext[0 : QB + ATOMS] = (values + dot(mixed[seed], mix[...])).astype(BF16)
        ext[QB + ATOMS :] = jnp.zeros((EXT - QB - ATOMS, CA), BF16)
        encoded[seed] = ext[QB : QB + ATOMS]
        lifted = jnp.maximum(dot(ext[...], pool[...]), 0.0).astype(BF16)
        state = cond[...].astype(F32) + dot(chosen, lifted) / counts
        residual[seed] = state
        normed[seed] = layer_norm(state).astype(BF16)


def encode(tok, feats, low, high, bias, index, cond, project, mix, pool):
    return pl.pallas_call(
        encode_kernel,
        out_shape=(
            jax.ShapeDtypeStruct((SEEDS, ATOMS, CA), BF16),
            jax.ShapeDtypeStruct((SEEDS, TOKS, CT), F32),
            jax.ShapeDtypeStruct((SEEDS, TOKS, CT), BF16),
        ),
        in_specs=[pl.BlockSpec(memory_space=pltpu.SMEM)] + vmem(9),
        out_specs=tuple(vmem(3)),
        scratch_shapes=[
            pltpu.VMEM((2 * EXT, CA), F32),
            pltpu.VMEM((33 * 4 * QB, WIN), F32),
            pltpu.VMEM((SEEDS, EXT, 3 * CA), BF16),
            pltpu.VMEM((SEEDS, QB + ATOMS, CA), BF16),
            pltpu.VMEM((EXT, CA), BF16),
        ],
        compiler_params=params(40),
        cost_estimate=pl.CostEstimate(flops=2 * 10**9, bytes_accessed=6 * 10**6, transcendentals=10**6),
        name="encode",
    )(tok, feats, low, high, bias, index, cond, project, mix, pool)


def decode_kernel(
    tok, enc, enc_low, enc_high, spread, spread_low, spread_high, bias, index, project, mix,
    update,
    rows, bias32, packed, mixed, decoded, tokens,
):
    bias32[...] = bias[...].astype(F32)
    chosen = (
        index[...] == lax.broadcasted_iota(jnp.int32, (TOKS + 2 * EDGE, EXT), 0).astype(F32)
    ).astype(BF16)
    for seed in range(SEEDS):
        tokens[0:EDGE] = spread_low[seed]
        tokens[EDGE : EDGE + TOKS] = spread[seed]
        tokens[EDGE + TOKS :] = spread_high[seed]
        carried = lax.dot_general(
            chosen, tokens[...], (((0,), (0,)), ((), ())), preferred_element_type=F32
        )
        decoded[0:MARGIN] = enc_low[seed]
        decoded[MARGIN : MARGIN + ATOMS] = enc[seed]
        decoded[MARGIN + ATOMS : 2 * MARGIN + ATOMS] = enc_high[seed]
        decoded[2 * MARGIN + ATOMS :] = jnp.zeros((EXT - 2 * MARGIN - ATOMS, CA), BF16)
        values = (decoded[...].astype(F32) + carried).astype(BF16).astype(F32)
        rows[pl.ds(seed, EXT, stride=2), :] = values
        packed[seed] = dot(layer_norm(values).astype(BF16), project[...]).astype(BF16)
    window_blocks(packed, bias32, mixed, 32, tok[0] * ATOMS - MARGIN, 4)
    for seed in range(SEEDS):
        place = pl.ds(2 * MARGIN + seed, ATOMS, stride=2)
        rows[place, :] = rows[place, :] + dot(mixed[seed], mix[...])
    update[...] = rows[2 * MARGIN : 2 * (MARGIN + ATOMS)].astype(BF16)


def decode(*args):
    return pl.pallas_call(
        decode_kernel,
        out_shape=jax.ShapeDtypeStruct((SEEDS * ATOMS, CA), BF16),
        in_specs=[pl.BlockSpec(memory_space=pltpu.SMEM)] + vmem(10),
        out_specs=vmem(1)[0],
        scratch_shapes=[
            pltpu.VMEM((2 * EXT, CA), F32),
            pltpu.VMEM((32 * 4 * QB, WIN), F32),
            pltpu.VMEM((SEEDS, EXT, 3 * CA), BF16),
            pltpu.VMEM((SEEDS, ATOMS, CA), BF16),
            pltpu.VMEM((EXT, CA), BF16),
            pltpu.VMEM((TOKS + 2 * EDGE, CA), BF16),
        ],
        compiler_params=params(40),
        cost_estimate=pl.CostEstimate(flops=10**9, bytes_accessed=4 * 10**6, transcendentals=10**6),
        name="decode",
    )(*args)


def spaced_kernel(weight, out):
    for group in range(4):
        start = PAIR * group // 128 * 128
        shift = PAIR * group - start
        width = min(256, 384 - start)
        row = lax.broadcasted_iota(jnp.int32, (width, 128), 0)
        lane = lax.broadcasted_iota(jnp.int32, (width, 128), 1)
        pick = ((row == lane + shift) & (lane < PAIR)).astype(F32).astype(BF16)
        out[0, group] = dot(weight[:, start : start + width], pick).astype(BF16)


def spaced(weight):
    return pl.pallas_call(
        spaced_kernel,
        grid=(8,),
        out_shape=jax.ShapeDtypeStruct((2, GROUPS, CT, 256), BF16),
        in_specs=[pl.BlockSpec((CT, 384), lambda i: (0, i))],
        out_specs=pl.BlockSpec(
            (1, 4, CT, 128),
            lambda i: (((i >= 2) & (i < 6)).astype(jnp.int32), i % 2, 0, (i >= 4).astype(jnp.int32)),
        ),
        compiler_params=params(32),
        cost_estimate=pl.CostEstimate(flops=10**9, bytes_accessed=11 * 10**6, transcendentals=0),
        name="spaced",
    )(weight)


def keys_kernel(tokens, weight, out):
    count = tokens.shape[0]
    values = jnp.concatenate([tokens[i].reshape(SEEDS * TOKS, CT) for i in range(count)], axis=0)
    ones = (lax.broadcasted_iota(jnp.int32, (1, 256), 1) == 128 + PAIR).astype(F32)
    for group in range(GROUPS):
        product = (dot(values, weight[0, group]) + ones).astype(BF16)
        for i in range(count):
            for seed in range(SEEDS):
                start = (i * SEEDS + seed) * TOKS
                out[group, seed, i * TOKS : (i + 1) * TOKS] = product[start : start + TOKS]


def keys(tokens, weight):
    step = 2
    return pl.pallas_call(
        keys_kernel,
        grid=(tokens.shape[0] // step,),
        out_shape=jax.ShapeDtypeStruct((GROUPS, SEEDS, ALL_TOKS, 256), BF16),
        in_specs=[
            pl.BlockSpec((step, SEEDS, TOKS, CT), lambda i: (i, 0, 0, 0)),
            pl.BlockSpec((1, GROUPS, CT, 256), lambda i: (1, 0, 0, 0)),
        ],
        out_specs=pl.BlockSpec((GROUPS, SEEDS, step * TOKS, 256), lambda i: (0, 0, i, 0)),
        compiler_params=params(40),
        cost_estimate=pl.CostEstimate(flops=13 * 10**9, bytes_accessed=26 * 10**6, transcendentals=0),
        name="keys",
    )(tokens, weight)


def attend_kernel(count, pieces, group_ids, normed, weight, key_value, mix, start, *rest):
    biases, (out, bias, scores, weights) = rest[:-4], rest[-4:]
    step = pl.program_id(0)
    seed = step % 2

    @pl.when(step == 0)
    def _():
        out[...] = start[...]

    at = 0
    for i, parts in enumerate(pieces):
        refs = biases[at : at + parts]
        at += parts

        @pl.when(step == 2 * i)
        def _(refs=refs):
            place = 0
            for ref in refs:
                size = ref.shape[1]
                for j in range(2):
                    bias[j * TOKS + place : j * TOKS + place + size] = ref[j]
                place += size

    query_gate = dot(normed[0], weight[0, 0])
    lane = lax.broadcasted_iota(jnp.int32, (TOKS, 128), 1)
    query = query_gate[:, :128] * (HEAD**-0.5)
    gate = jax.nn.sigmoid(query_gate[:, 128:])
    stacked = jnp.concatenate(
        [jnp.where(lane < HEAD, query, 0.0), jnp.where(lane < HEAD, 0.0, query)], axis=0
    ).astype(BF16)
    width = 512
    peak = None
    for c in range(ALL_TOKS // width):
        cols = slice(c * width, (c + 1) * width)
        part = dot_t(stacked, key_value[0, 0, cols, 0:128]) + bias[:, cols].astype(F32)
        scores[:, cols] = part
        for w in range(width // 128):
            tile = part[:, w * 128 : (w + 1) * 128]
            peak = tile if peak is None else jnp.maximum(peak, tile)
    top = jnp.max(peak, axis=-1, keepdims=True)
    for c in range(ALL_TOKS // width):
        cols = slice(c * width, (c + 1) * width)
        weights[:, cols] = jnp.exp(scores[:, cols] - top).astype(BF16)
    total = dot(weights[...], key_value[0, 0, :, 128:256])
    joined = total / total[:, PAIR : PAIR + 1]
    joined = jnp.where(lane < HEAD, joined[:TOKS], joined[TOKS:])
    gated = (joined * gate).astype(BF16)
    out[seed] = out[seed] + dot(gated[:, :PAIR], mix[0])


def attend(group_ids, normed, weight, key_value, mix, start, pieces):
    count = len(pieces)
    flat = [ref for parts in pieces for ref in parts]
    grid_spec = pltpu.PrefetchScalarGridSpec(
        num_scalar_prefetch=1,
        grid=(2 * count,),
        in_specs=[
            pl.BlockSpec((1, TOKS, CT), lambda i, ids: (i % 2, 0, 0)),
            pl.BlockSpec((1, 1, CT, 256), lambda i, ids: (0, ids[i // 2], 0, 0)),
            pl.BlockSpec((1, 1, ALL_TOKS, 256), lambda i, ids: (ids[i // 2], i % 2, 0, 0)),
            pl.BlockSpec((1, PAIR, CT), lambda i, ids: (ids[i // 2], 0, 0)),
            pl.BlockSpec((SEEDS, TOKS, CT), lambda i, ids: (0, 0, 0)),
        ]
        + vmem(len(flat)),
        out_specs=pl.BlockSpec((SEEDS, TOKS, CT), lambda i, ids: (0, 0, 0)),
        scratch_shapes=[
            pltpu.VMEM((2 * TOKS, ALL_TOKS), BF16),
            pltpu.VMEM((2 * TOKS, ALL_TOKS), F32),
            pltpu.VMEM((2 * TOKS, ALL_TOKS), BF16),
        ],
    )
    return pl.pallas_call(
        functools.partial(attend_kernel, count, tuple(len(parts) for parts in pieces)),
        grid_spec=grid_spec,
        out_shape=jax.ShapeDtypeStruct((SEEDS, TOKS, CT), F32),
        compiler_params=params(40),
        cost_estimate=pl.CostEstimate(
            flops=count * 10**9, bytes_accessed=count * 4 * 10**6, transcendentals=count * 10**6
        ),
        name="attend",
    )(group_ids, normed, weight, key_value, mix, start, *flat)


def transition_kernel(residual, wide, narrow, spread_weight, state, spread):
    values = residual[...].reshape(SEEDS * TOKS, CT)
    normed = layer_norm(values).astype(BF16)
    total = values
    step = 512
    for c in range(TRANS // step):
        gate = dot(normed, wide[:, c * step : (c + 1) * step])
        up = dot(normed, wide[:, TRANS + c * step : TRANS + (c + 1) * step])
        hidden = (jax.nn.silu(gate) * up).astype(BF16)
        total = total + dot(hidden, narrow[c * step : (c + 1) * step, :])
    rounded = total.astype(BF16)
    state[...] = rounded.reshape(SEEDS, TOKS, CT)
    spread[...] = dot(rounded, spread_weight[...]).astype(BF16).reshape(SEEDS, TOKS, CA)


def transition(residual, wide, narrow, spread_weight):
    return pl.pallas_call(
        transition_kernel,
        out_shape=(
            jax.ShapeDtypeStruct((SEEDS, TOKS, CT), BF16),
            jax.ShapeDtypeStruct((SEEDS, TOKS, CA), BF16),
        ),
        in_specs=vmem(4),
        out_specs=tuple(vmem(2)),
        compiler_params=params(40),
        cost_estimate=pl.CostEstimate(flops=2 * 10**9, bytes_accessed=9 * 10**6, transcendentals=4 * 10**5),
        name="transition",
    )(residual, wide, narrow, spread_weight)


def along_tok(values, by):
    return lax.ppermute(values, "tok", [(i, (i + by) % 16) for i in range(16)])


def along_y(values, by):
    return lax.ppermute(values, "seed", [(i, (i + 2 * by) % 8) for i in range(8)])


def along_z(values):
    return lax.ppermute(values, "seed", [(i, i ^ 1) for i in range(8)])


def y_ring(own):
    below = along_y(own, 1)
    above = along_y(own, -1)
    half = own.shape[1] // 2
    far = (along_y(below[:, :half], 1), along_y(above[:, half:], -1))
    return below, above, far


def per_device(
    atom_feats, atom_index, token_cond, pair_bias, atom_bias_enc, atom_bias_dec,
    enc_project, enc_mix, pool_weight, token_project, token_mix, swiglu_in, swiglu_out,
    spread_weight, dec_project, dec_mix,
):
    tok = lax.axis_index("tok")
    seed = lax.axis_index("seed")
    tok_ref = tok.astype(jnp.int32).reshape(1)
    feats = atom_feats.reshape(SEEDS * ATOMS, CA)
    bias_enc = atom_bias_enc.reshape(4 * ATOMS, WIN)
    bias_dec = atom_bias_dec.reshape(4 * ATOMS, WIN)

    place = (atom_index - tok * TOKS).astype(F32)
    tail = jnp.pad((place[-MARGIN:] - TOKS).astype(BF16)[None], ((0, 15), (0, WIN - MARGIN)))
    head = jnp.pad(place[:MARGIN].astype(BF16)[None], ((0, 15), (0, WIN - MARGIN)))
    low = along_tok(jnp.concatenate([feats[-2 * LOWER :], bias_enc[-4 * QB :], tail], axis=0), 1)
    high = along_tok(jnp.concatenate([feats[: 2 * MARGIN], head], axis=0), -1)

    below, above, far = y_ring(pair_bias)
    other = along_z(pair_bias)
    other_below, other_above, other_far = y_ring(other)

    place_low = low[2 * LOWER + 4 * QB, :MARGIN].astype(F32)
    place_high = high[2 * MARGIN, :MARGIN].astype(F32) + TOKS
    place_low = jnp.where(tok == 0, -1000.0, place_low)
    place_high = jnp.where(tok == 15, 1000.0, place_high)
    pool_index = jnp.concatenate(
        [place_low[-QB:], place, jnp.full((EXT - QB - ATOMS,), -1000.0, F32)]
    )[None]
    spread_index = (
        jnp.concatenate(
            [place_low, place, place_high, jnp.full((EXT - 2 * MARGIN - ATOMS,), -1000.0, F32)]
        )
        + EDGE
    )[None]

    weights = spaced(token_project)
    encoded, residual, normed = encode(
        tok_ref, feats, low, high, bias_enc, pool_index, token_cond, enc_project, enc_mix, pool_weight
    )
    enc_low = along_tok(encoded[:, -MARGIN:], 1)
    enc_high = along_tok(encoded[:, :MARGIN], -1)

    everyone = lax.all_gather(normed, "tok", axis=0)
    key_value = keys(everyone, weights)

    level, side = seed // 2, seed % 2

    def ids(*offsets):
        return jnp.stack([(level + dy) % 4 * 2 + (side ^ dz) for dy, dz in offsets]).astype(jnp.int32)

    mix = token_mix.reshape(GROUPS, PAIR, CT)
    residual = attend(
        ids((0, 0), (3, 0), (1, 0), (2, 0), (0, 1)), normed, weights, key_value, mix, residual,
        ((pair_bias,), (below,), (above,), far, (other,)),
    )
    residual = attend(
        ids((3, 1), (1, 1), (2, 1)), normed, weights, key_value, mix, residual,
        ((other_below,), (other_above,), other_far),
    )
    state, spread = transition(residual, swiglu_in, swiglu_out, spread_weight)
    spread_low = along_tok(spread[:, -EDGE:], 1)
    spread_high = along_tok(spread[:, :EDGE], -1)
    update = decode(
        tok_ref, encoded, enc_low, enc_high, spread, spread_low, spread_high, bias_dec,
        spread_index, dec_project, dec_mix,
    )
    return state.transpose(1, 0, 2), update.reshape(ATOMS, SEEDS, CA)


def solution(mesh):
    placed = (
        P("tok", "seed", None),
        P("tok"),
        P("tok", None),
        P("seed", "tok", None),
        P("tok", None, None),
        P("tok", None, None),
    ) + (P(),) * 10
    return jax.shard_map(
        per_device,
        mesh=mesh,
        in_specs=placed,
        out_specs=(P("tok", "seed", None), P("tok", "seed", None)),
        check_vma=False,
    )
```

```python
import functools

import jax
import jax.numpy as jnp
from jax import lax
from jax.experimental import pallas as pl
from jax.experimental.pallas import tpu as pltpu
from jax.sharding import PartitionSpec as P

EPS = 1e-05
NEG = -1000000000.0
F32 = jnp.float32
BF16 = jnp.bfloat16

SEEDS = 2
ATOMS = 1024
TOKS = 128
CA = 128
CT = 768
HEADS = 16
HEAD = 48
PAIR = 96
GROUPS = 8
QB = 32
WIN = 128
MARGIN = 48
LOWER = 80
EXT = 1152
EDGE = 16
TRANS = 1536
ALL_TOKS = 2048
ALL_ATOMS = 16384


SMALL = pl.CostEstimate(flops=10**6, bytes_accessed=10**4, transcendentals=0)


def params(limit_mb, **more):
    return pltpu.CompilerParams(vmem_limit_bytes=limit_mb * 1024 * 1024, **more)


def vmem(n):
    return [pl.BlockSpec(memory_space=pltpu.VMEM)] * n


def anywhere(n):
    return [pl.BlockSpec(memory_space=pl.ANY)] * n


def layer_norm(values):
    centre = values - jnp.mean(values, axis=-1, keepdims=True)
    variance = jnp.mean(centre * centre, axis=-1, keepdims=True)
    return centre * lax.rsqrt(variance + EPS)


def dot(a, b):
    return jnp.dot(a, b, preferred_element_type=F32)


def dot_t(a, b):
    return lax.dot_general(a, b, (((1,), (1,)), ((), ())), preferred_element_type=F32)


def window_blocks(packed, bias, mixed, blocks, first_atom, unroll):
    lane_head = lax.broadcasted_iota(jnp.int32, (QB, CA), 1) // 32
    head_mask = [(lane_head == h).astype(BF16) for h in range(4)]
    lane = lax.broadcasted_iota(jnp.int32, (1, WIN), 1)
    ones = jnp.ones((WIN, CA), BF16)
    for b in (0, 1, 2, blocks - 2, blocks - 1):
        position = lane + (first_atom + b * QB)
        inside = (position >= 0) & (position < ALL_ATOMS)
        place = slice(b * 4 * QB, (b + 1) * 4 * QB)
        bias[place] = jnp.where(inside, bias[place], NEG)

    def body(i, carry):
        work = []
        for u in range(unroll):
            b = i * unroll + u
            rows = pl.multiple_of(b * QB, QB)
            query_rows = pl.multiple_of(b * QB + MARGIN, 16)
            bias_rows = pl.multiple_of(b * 4 * QB, 4 * QB)
            added = jnp.concatenate(
                [bias[pl.ds(bias_rows + h, QB, stride=4), :] for h in range(4)], axis=0
            )
            for seed in range(SEEDS):
                work.append((rows, query_rows, added, seed))
        scores = []
        for rows, query_rows, added, seed in work:
            query = packed[seed, pl.ds(query_rows, QB), 0:CA]
            key = packed[seed, pl.ds(rows, WIN), CA : 2 * CA]
            stacked = jnp.concatenate([query * head_mask[h] for h in range(4)], axis=0)
            scores.append(dot_t(stacked, key) * (32**-0.5) + added)
        weights = [jnp.exp(s - jnp.max(s, axis=-1, keepdims=True)).astype(BF16) for s in scores]
        for (rows, _, _, seed), w in zip(work, weights):
            value = jnp.concatenate([packed[seed, pl.ds(rows, WIN), 2 * CA : 3 * CA], ones], axis=1)
            out = dot(w, value)
            joined = out[3 * QB :]
            for h in range(3):
                joined = jnp.where(jnp.concatenate([lane_head, lane_head], axis=1) == h, out[h * QB : (h + 1) * QB], joined)
            mixed[seed, pl.ds(rows, QB), :] = (joined[:, :CA] / joined[:, CA:]).astype(BF16)
        return carry

    lax.fori_loop(0, blocks // unroll, body, 0)


def encode_kernel(
    tok, feats, low, high, bias, index, cond, project, mix, pool,
    encoded, residual, normed,
    rows, bias32, packed, mixed, ext,
):
    rows[0 : 2 * LOWER] = low[0 : 2 * LOWER].astype(F32)
    rows[2 * LOWER : 2 * (LOWER + ATOMS)] = feats[...].astype(F32)
    rows[2 * (LOWER + ATOMS) : 2 * EXT] = high[0 : 2 * MARGIN].astype(F32)
    bias32[0 : 4 * QB] = low[2 * LOWER : 2 * LOWER + 4 * QB].astype(F32)
    bias32[4 * QB :] = bias[...].astype(F32)
    for seed in range(SEEDS):
        values = rows[pl.ds(seed, EXT, stride=2), :]
        packed[seed] = dot(layer_norm(values).astype(BF16), project[...]).astype(BF16)
    window_blocks(packed, bias32, mixed, 33, tok[0] * ATOMS - QB - MARGIN, 11)
    chosen = (index[...] == lax.broadcasted_iota(jnp.int32, (TOKS, EXT), 0).astype(F32)).astype(F32)
    counts = jnp.sum(chosen, axis=1, keepdims=True)
    chosen = chosen.astype(BF16)
    for seed in range(SEEDS):
        values = rows[pl.ds(2 * MARGIN + seed, QB + ATOMS, stride=2), :]
        ext[0 : QB + ATOMS] = (values + dot(mixed[seed], mix[...])).astype(BF16)
        ext[QB + ATOMS :] = jnp.zeros((EXT - QB - ATOMS, CA), BF16)
        encoded[seed] = ext[QB : QB + ATOMS]
        lifted = jnp.maximum(dot(ext[...], pool[...]), 0.0).astype(BF16)
        state = cond[...].astype(F32) + dot(chosen, lifted) / counts
        residual[seed] = state
        normed[seed] = layer_norm(state).astype(BF16)


def encode(tok, feats, low, high, bias, index, cond, project, mix, pool):
    return pl.pallas_call(
        encode_kernel,
        out_shape=(
            jax.ShapeDtypeStruct((SEEDS, ATOMS, CA), BF16),
            jax.ShapeDtypeStruct((SEEDS, TOKS, CT), F32),
            jax.ShapeDtypeStruct((SEEDS, TOKS, CT), BF16),
        ),
        in_specs=[pl.BlockSpec(memory_space=pltpu.SMEM)] + vmem(9),
        out_specs=tuple(vmem(3)),
        scratch_shapes=[
            pltpu.VMEM((2 * EXT, CA), F32),
            pltpu.VMEM((33 * 4 * QB, WIN), F32),
            pltpu.VMEM((SEEDS, EXT, 3 * CA), BF16),
            pltpu.VMEM((SEEDS, QB + ATOMS, CA), BF16),
            pltpu.VMEM((EXT, CA), BF16),
        ],
        compiler_params=params(58),
        cost_estimate=SMALL,
        name="encode",
    )(tok, feats, low, high, bias, index, cond, project, mix, pool)


def decode_kernel(
    tok, enc, enc_low, enc_high, spread, spread_low, spread_high, bias, index, project, mix,
    update,
    rows, bias32, packed, mixed, decoded, tokens,
):
    bias32[...] = bias[...].astype(F32)
    chosen = (
        index[...] == lax.broadcasted_iota(jnp.int32, (TOKS + 2 * EDGE, EXT), 0).astype(F32)
    ).astype(BF16)
    for seed in range(SEEDS):
        tokens[0:EDGE] = spread_low[seed]
        tokens[EDGE : EDGE + TOKS] = spread[seed]
        tokens[EDGE + TOKS :] = spread_high[seed]
        carried = lax.dot_general(
            chosen, tokens[...], (((0,), (0,)), ((), ())), preferred_element_type=F32
        )
        decoded[0:MARGIN] = enc_low[seed]
        decoded[MARGIN : MARGIN + ATOMS] = enc[seed]
        decoded[MARGIN + ATOMS : 2 * MARGIN + ATOMS] = enc_high[seed]
        decoded[2 * MARGIN + ATOMS :] = jnp.zeros((EXT - 2 * MARGIN - ATOMS, CA), BF16)
        values = (decoded[...].astype(F32) + carried).astype(BF16).astype(F32)
        rows[pl.ds(seed, EXT, stride=2), :] = values
        packed[seed] = dot(layer_norm(values).astype(BF16), project[...]).astype(BF16)
    window_blocks(packed, bias32, mixed, 32, tok[0] * ATOMS - MARGIN, 8)
    for seed in range(SEEDS):
        place = pl.ds(2 * MARGIN + seed, ATOMS, stride=2)
        rows[place, :] = rows[place, :] + dot(mixed[seed], mix[...])
    update[...] = rows[2 * MARGIN : 2 * (MARGIN + ATOMS)].astype(BF16)


def decode(*args):
    return pl.pallas_call(
        decode_kernel,
        out_shape=jax.ShapeDtypeStruct((SEEDS * ATOMS, CA), BF16),
        in_specs=[pl.BlockSpec(memory_space=pltpu.SMEM)] + vmem(10),
        out_specs=vmem(1)[0],
        scratch_shapes=[
            pltpu.VMEM((2 * EXT, CA), F32),
            pltpu.VMEM((32 * 4 * QB, WIN), F32),
            pltpu.VMEM((SEEDS, EXT, 3 * CA), BF16),
            pltpu.VMEM((SEEDS, ATOMS, CA), BF16),
            pltpu.VMEM((EXT, CA), BF16),
            pltpu.VMEM((TOKS + 2 * EDGE, CA), BF16),
        ],
        compiler_params=params(58),
        cost_estimate=SMALL,
        name="decode",
    )(*args)


def spaced_kernel(weight, out):
    for group in range(4):
        start = PAIR * group // 128 * 128
        shift = PAIR * group - start
        width = min(256, 384 - start)
        row = lax.broadcasted_iota(jnp.int32, (width, 128), 0)
        lane = lax.broadcasted_iota(jnp.int32, (width, 128), 1)
        pick = ((row == lane + shift) & (lane < PAIR)).astype(F32).astype(BF16)
        out[0, group] = dot(weight[:, start : start + width], pick).astype(BF16)


def spaced(weight):
    return pl.pallas_call(
        spaced_kernel,
        grid=(8,),
        out_shape=jax.ShapeDtypeStruct((2, GROUPS, CT, 256), BF16),
        in_specs=[pl.BlockSpec((CT, 384), lambda i: (0, i))],
        out_specs=pl.BlockSpec(
            (1, 4, CT, 128),
            lambda i: (((i >= 2) & (i < 6)).astype(jnp.int32), i % 2, 0, (i >= 4).astype(jnp.int32)),
        ),
        compiler_params=params(58),
        cost_estimate=SMALL,
        name="spaced",
    )(weight)


def keys_kernel(pieces, passed, at, *refs):
    count = sum(a + b for a, b in pieces)
    chunks, weight = refs[:count], refs[count]
    out, both = refs[-2 - passed], refs[-1]
    step = pl.program_id(0)
    core = at[0]
    first = 0
    for i, sizes in enumerate(pieces):
        sides = (chunks[first : first + sizes[0]], chunks[first + sizes[0] : first + sum(sizes)])
        first += sum(sizes)

        @pl.when(step == i)
        def _(sides=sides):
            for side, parts in zip((core, 1 - core), sides):
                seed = 0
                for part in parts:
                    for j in range(part.shape[0]):
                        both[side, seed] = part[j]
                        seed += 1

    values = both[...].reshape(2 * SEEDS * TOKS, CT)
    ones = (lax.broadcasted_iota(jnp.int32, (1, 256), 1) == 128 + PAIR).astype(F32)
    for group in range(GROUPS):
        product = (dot(values, weight[0, group]) + ones).astype(BF16)
        for side in range(2):
            for seed in range(SEEDS):
                start = (side * SEEDS + seed) * TOKS
                out[group, seed, side * TOKS : (side + 1) * TOKS] = product[start : start + TOKS]


def keys(core, chips, pieces, weight, before, passed=()):
    flat = [part for sides in pieces for parts in sides for part in parts]
    at = jnp.concatenate([core, chips])
    more = ([] if before is None else [before]) + list(passed)
    aliases = {} if before is None else {len(flat) + 2: 0}
    for i in range(len(passed)):
        aliases[len(flat) + 2 + len(more) - len(passed) + i] = 1 + i
    grid_spec = pltpu.PrefetchScalarGridSpec(
        num_scalar_prefetch=1,
        grid=(len(pieces),),
        in_specs=vmem(len(flat))
        + [pl.BlockSpec((1, GROUPS, CT, 256), lambda i, at: (1, 0, 0, 0))]
        + anywhere(len(more)),
        out_specs=tuple(
            [pl.BlockSpec((GROUPS, SEEDS, 2 * TOKS, 256), lambda i, at: (0, 0, at[1 + i], 0))]
            + anywhere(len(passed))
        ),
        scratch_shapes=[pltpu.VMEM((2, SEEDS, TOKS, CT), BF16)],
    )
    sizes = tuple((len(same), len(other)) for same, other in pieces)
    return pl.pallas_call(
        functools.partial(keys_kernel, sizes, len(passed)),
        grid_spec=grid_spec,
        out_shape=tuple(
            [jax.ShapeDtypeStruct((GROUPS, SEEDS, ALL_TOKS, 256), BF16)]
            + [jax.ShapeDtypeStruct(array.shape, array.dtype) for array in passed]
        ),
        input_output_aliases=aliases,
        compiler_params=params(50),
        cost_estimate=SMALL,
        name="keys",
    )(at, *flat, weight, *more)


def attend_kernel(pieces, group_ids, normed, weight, key_value, mix, start, *rest):
    biases, (out, bias, scores) = rest[: sum(pieces)], rest[-3:]
    step = pl.program_id(0)

    @pl.when(step == 0)
    def _():
        out[...] = start[...]

    at = 0
    for i, parts in enumerate(pieces):
        refs = biases[at : at + parts]
        at += parts

        @pl.when(step == i)
        def _(refs=refs):
            place = 0
            for ref in refs:
                size = ref.shape[1]
                for j in range(2):
                    bias[j * TOKS + place : j * TOKS + place + size] = ref[j]
                place += size

    lane = lax.broadcasted_iota(jnp.int32, (TOKS, 128), 1)
    query_gate = dot(normed[...].reshape(SEEDS * TOKS, CT), weight[0, 0])
    gate = jax.nn.sigmoid(query_gate[:, 128:])
    width = 512
    tops = []
    for seed in range(SEEDS):
        query = query_gate[seed * TOKS : (seed + 1) * TOKS, :128] * (HEAD**-0.5)
        stacked = jnp.concatenate(
            [jnp.where(lane < HEAD, query, 0.0), jnp.where(lane < HEAD, 0.0, query)], axis=0
        ).astype(BF16)
        peak = None
        for c in range(ALL_TOKS // width):
            cols = slice(c * width, (c + 1) * width)
            part = dot_t(stacked, key_value[0, seed, cols, 0:128]) + bias[:, cols].astype(F32)
            scores[seed, :, cols] = part
            for w in range(width // 128):
                tile = part[:, w * 128 : (w + 1) * 128]
                peak = tile if peak is None else jnp.maximum(peak, tile)
        tops.append(jnp.max(peak, axis=-1, keepdims=True))
    for seed in range(SEEDS):
        total = None
        for c in range(ALL_TOKS // width):
            cols = slice(c * width, (c + 1) * width)
            part = dot(
                jnp.exp(scores[seed, :, cols] - tops[seed]).astype(BF16),
                key_value[0, seed, cols, 128:256],
            )
            total = part if total is None else total + part
        joined = total / total[:, PAIR : PAIR + 1]
        joined = jnp.where(lane < HEAD, joined[:TOKS], joined[TOKS:])
        gated = (joined * gate[seed * TOKS : (seed + 1) * TOKS]).astype(BF16)
        out[seed] = out[seed] + dot(gated[:, :PAIR], mix[0])


def attend(group_ids, normed, weight, key_value, mix, start, pieces):
    count = len(pieces)
    flat = [ref for parts in pieces for ref in parts]
    grid_spec = pltpu.PrefetchScalarGridSpec(
        num_scalar_prefetch=1,
        grid=(count,),
        in_specs=[
            pl.BlockSpec((SEEDS, TOKS, CT), lambda i, ids: (0, 0, 0)),
            pl.BlockSpec((1, 1, CT, 256), lambda i, ids: (0, ids[i], 0, 0)),
            pl.BlockSpec((1, SEEDS, ALL_TOKS, 256), lambda i, ids: (ids[i], 0, 0, 0)),
            pl.BlockSpec((1, PAIR, CT), lambda i, ids: (ids[i], 0, 0)),
            pl.BlockSpec((SEEDS, TOKS, CT), lambda i, ids: (0, 0, 0)),
        ]
        + vmem(len(flat)),
        out_specs=pl.BlockSpec((SEEDS, TOKS, CT), lambda i, ids: (0, 0, 0)),
        scratch_shapes=[
            pltpu.VMEM((2 * TOKS, ALL_TOKS), BF16),
            pltpu.VMEM((SEEDS, 2 * TOKS, ALL_TOKS), F32),
        ],
    )
    return pl.pallas_call(
        functools.partial(attend_kernel, tuple(len(parts) for parts in pieces)),
        grid_spec=grid_spec,
        out_shape=jax.ShapeDtypeStruct((SEEDS, TOKS, CT), F32),
        compiler_params=params(50),
        cost_estimate=SMALL,
        name="attend",
    )(group_ids, normed, weight, key_value, mix, start, *flat)


def transition_kernel(residual, wide_hbm, narrow_hbm, spread_weight, state, spread, wide, narrow, sems):
    step = 512
    count = TRANS // step
    copies = []
    for c in range(count):
        gate_cols = pl.ds(c * step, step)
        up_cols = pl.ds(TRANS + c * step, step)
        copies.append(
            [
                pltpu.make_async_copy(wide_hbm.at[:, gate_cols], wide.at[:, gate_cols], sems.at[c, 0]),
                pltpu.make_async_copy(wide_hbm.at[:, up_cols], wide.at[:, up_cols], sems.at[c, 1]),
                pltpu.make_async_copy(narrow_hbm.at[gate_cols], narrow.at[gate_cols], sems.at[c, 2]),
            ]
        )
    for group in copies:
        for copy in group:
            copy.start()
    values = residual[...].reshape(SEEDS * TOKS, CT)
    normed = layer_norm(values).astype(BF16)
    total = values
    for c in range(count):
        for copy in copies[c]:
            copy.wait()
        gate = dot(normed, wide[:, c * step : (c + 1) * step])
        up = dot(normed, wide[:, TRANS + c * step : TRANS + (c + 1) * step])
        hidden = (jax.nn.silu(gate) * up).astype(BF16)
        total = total + dot(hidden, narrow[c * step : (c + 1) * step, :])
    rounded = total.astype(BF16)
    state[...] = rounded.reshape(SEEDS, TOKS, CT)
    spread[...] = dot(rounded, spread_weight[...]).astype(BF16).reshape(SEEDS, TOKS, CA)


def transition(residual, wide, narrow, spread_weight):
    return pl.pallas_call(
        transition_kernel,
        out_shape=(
            jax.ShapeDtypeStruct((SEEDS, TOKS, CT), BF16),
            jax.ShapeDtypeStruct((SEEDS, TOKS, CA), BF16),
        ),
        in_specs=vmem(1) + anywhere(2) + vmem(1),
        out_specs=tuple(vmem(2)),
        scratch_shapes=[
            pltpu.VMEM((CT, 2 * TRANS), BF16),
            pltpu.VMEM((TRANS, CT), BF16),
            pltpu.SemaphoreType.DMA((3, 3)),
        ],
        compiler_params=params(58),
        cost_estimate=SMALL,
        name="transition",
    )(residual, wide, narrow, spread_weight)


def along_tok(values, by):
    return lax.ppermute(values, "tok", [(i, (i + by) % 16) for i in range(16)])


def along_x(values, by):
    return lax.ppermute(values, "tok", [(i, i // 8 * 8 + (i + 2 * by) % 8) for i in range(16)])


def across_z(values):
    return lax.ppermute(values, "tok", [(i, i ^ 8) for i in range(16)])


def across_core(values):
    return lax.ppermute(values, "tok", [(i, i ^ 1) for i in range(16)])


def along_y(values, by):
    return lax.ppermute(values, "seed", [(i, (i + 2 * by) % 8) for i in range(8)])


def along_z(values):
    return lax.ppermute(values, "seed", [(i, i ^ 1) for i in range(8)])


def per_device(
    atom_feats, atom_index, token_cond, pair_bias, atom_bias_enc, atom_bias_dec,
    enc_project, enc_mix, pool_weight, token_project, token_mix, swiglu_in, swiglu_out,
    spread_weight, dec_project, dec_mix,
):
    tok = lax.axis_index("tok")
    seed = lax.axis_index("seed")
    tok_ref = tok.astype(jnp.int32).reshape(1)
    feats = atom_feats.reshape(SEEDS * ATOMS, CA)
    bias_enc = atom_bias_enc.reshape(4 * ATOMS, WIN)
    bias_dec = atom_bias_dec.reshape(4 * ATOMS, WIN)

    place = (atom_index - tok * TOKS).astype(F32)
    tail = jnp.pad((place[-MARGIN:] - TOKS).astype(BF16)[None], ((0, 15), (0, WIN - MARGIN)))
    head = jnp.pad(place[:MARGIN].astype(BF16)[None], ((0, 15), (0, WIN - MARGIN)))
    low = along_tok(jnp.concatenate([feats[-2 * LOWER :], bias_enc[-4 * QB :], tail], axis=0), 1)
    high = along_tok(jnp.concatenate([feats[: 2 * MARGIN], head], axis=0), -1)

    below = along_y(pair_bias, 1)
    above = along_y(pair_bias, -1)
    other = along_z(pair_bias)

    place_low = low[2 * LOWER + 4 * QB, :MARGIN].astype(F32)
    place_high = high[2 * MARGIN, :MARGIN].astype(F32) + TOKS
    place_low = jnp.where(tok == 0, -1000.0, place_low)
    place_high = jnp.where(tok == 15, 1000.0, place_high)
    pool_index = jnp.concatenate(
        [place_low[-QB:], place, jnp.full((EXT - QB - ATOMS,), -1000.0, F32)]
    )[None]
    spread_index = (
        jnp.concatenate(
            [place_low, place, place_high, jnp.full((EXT - 2 * MARGIN - ATOMS,), -1000.0, F32)]
        )
        + EDGE
    )[None]

    weights = spaced(token_project)
    encoded, residual, normed = encode(
        tok_ref, feats, low, high, bias_enc, pool_index, token_cond, enc_project, enc_mix, pool_weight
    )
    enc_low = along_tok(encoded[:, -MARGIN:], 1)
    enc_high = along_tok(encoded[:, :MARGIN], -1)

    core = (tok % 2).astype(jnp.int32).reshape(1)
    column, floor = tok // 2 % 4, tok // 8

    def chips(*offsets):
        return jnp.stack([(floor ^ dz) * 4 + (column + dx) % 4 for dx, dz in offsets]).astype(jnp.int32)

    def chip(*parts):
        return parts, tuple(across_core(part) for part in parts)

    x_below = along_x(normed, 1)
    x_above = along_x(normed, -1)
    z_own = across_z(normed)
    key_value, below, above, other, x_below, x_above, z_own = keys(
        core, chips((0, 0)), (chip(normed),), weights, None,
        (below, above, other, x_below, x_above, z_own),
    )
    x_far = (along_x(x_below[:1], 1), along_x(x_above[1:], -1))
    z_below = along_x(z_own, 1)
    z_above = along_x(z_own, -1)
    half = TOKS // 2
    far = (along_y(below[:, :half], 1), along_y(above[:, half:], -1))
    other_below = along_y(other, 1)
    other_above = along_y(other, -1)
    key_value, z_below, z_above = keys(
        core, chips((3, 0), (1, 0), (0, 1)), (chip(x_below), chip(x_above), chip(z_own)),
        weights, key_value, (z_below, z_above),
    )
    z_far = (along_x(z_below[:1], 1), along_x(z_above[1:], -1))
    key_value, other_below, other_above = keys(
        core, chips((2, 0), (3, 1), (1, 1), (2, 1)),
        (chip(*x_far), chip(z_below), chip(z_above), chip(*z_far)),
        weights, key_value, (other_below, other_above),
    )
    other_far = (along_y(other_below[:, :half], 1), along_y(other_above[:, half:], -1))

    level, side = seed // 2, seed % 2

    def ids(*offsets):
        return jnp.stack([(level + dy) % 4 * 2 + (side ^ dz) for dy, dz in offsets]).astype(jnp.int32)

    mix = token_mix.reshape(GROUPS, PAIR, CT)
    residual = attend(
        ids((0, 0), (3, 0), (1, 0), (2, 0), (0, 1)), normed, weights, key_value, mix, residual,
        ((pair_bias,), (below,), (above,), far, (other,)),
    )
    residual = attend(
        ids((3, 1), (1, 1)), normed, weights, key_value, mix, residual,
        ((other_below,), (other_above,)),
    )
    residual = attend(ids((2, 1)), normed, weights, key_value, mix, residual, (other_far,))
    state, spread = transition(residual, swiglu_in, swiglu_out, spread_weight)
    spread_low = along_tok(spread[:, -EDGE:], 1)
    spread_high = along_tok(spread[:, :EDGE], -1)
    update = decode(
        tok_ref, encoded, enc_low, enc_high, spread, spread_low, spread_high, bias_dec,
        spread_index, dec_project, dec_mix,
    )
    return state.transpose(1, 0, 2), update.reshape(ATOMS, SEEDS, CA)


def solution(mesh):
    placed = (
        P("tok", "seed", None),
        P("tok"),
        P("tok", None),
        P("seed", "tok", None),
        P("tok", None, None),
        P("tok", None, None),
    ) + (P(),) * 10
    return jax.shard_map(
        per_device,
        mesh=mesh,
        in_specs=placed,
        out_specs=(P("tok", "seed", None), P("tok", "seed", None)),
        check_vma=False,
    )
```

```python
import functools

import jax
import jax.numpy as jnp
from jax import lax
from jax.experimental import pallas as pl
from jax.experimental.pallas import tpu as pltpu
from jax.sharding import PartitionSpec as P

EPS = 1e-05
NEG = -1000000000.0
F32 = jnp.float32
BF16 = jnp.bfloat16

SEEDS = 2
ATOMS = 1024
TOKS = 128
CA = 128
CT = 768
HEADS = 16
HEAD = 48
PAIR = 96
GROUPS = 8
QB = 32
WIN = 128
MARGIN = 48
LOWER = 80
EXT = 1152
EDGE = 16
TRANS = 1536
ALL_TOKS = 2048
ALL_ATOMS = 16384
UP_ROWS = 2 * LOWER + 4 * QB + 16
DOWN_ROWS = 2 * MARGIN + 16


SMALL = pl.CostEstimate(flops=10**6, bytes_accessed=10**4, transcendentals=0)
LARGE = pl.CostEstimate(flops=10**11, bytes_accessed=10**4, transcendentals=0)


def params(limit_mb, **more):
    return pltpu.CompilerParams(vmem_limit_bytes=limit_mb * 1024 * 1024, **more)


def vmem(n):
    return [pl.BlockSpec(memory_space=pltpu.VMEM)] * n


def anywhere(n):
    return [pl.BlockSpec(memory_space=pltpu.HBM)] * n


def layer_norm(values):
    centre = values - jnp.mean(values, axis=-1, keepdims=True)
    variance = jnp.mean(centre * centre, axis=-1, keepdims=True)
    return centre * lax.rsqrt(variance + EPS)


def dot(a, b):
    return jnp.dot(a, b, preferred_element_type=F32)


def dot_t(a, b):
    return lax.dot_general(a, b, (((1,), (1,)), ((), ())), preferred_element_type=F32)


def window_blocks(packed, bias, mixed, blocks, first_atom, unroll):
    lane_head = lax.broadcasted_iota(jnp.int32, (QB, CA), 1) // 32
    head_mask = [(lane_head == h).astype(BF16) for h in range(4)]
    lane = lax.broadcasted_iota(jnp.int32, (1, WIN), 1)
    ones = jnp.ones((WIN, CA), BF16)
    for b in (0, 1, 2, blocks - 2, blocks - 1):
        position = lane + (first_atom + b * QB)
        inside = (position >= 0) & (position < ALL_ATOMS)
        place = slice(b * 4 * QB, (b + 1) * 4 * QB)
        bias[place] = jnp.where(inside, bias[place], NEG)

    def body(i, carry):
        work = []
        for u in range(unroll):
            b = i * unroll + u
            rows = pl.multiple_of(b * QB, QB)
            query_rows = pl.multiple_of(b * QB + MARGIN, 16)
            bias_rows = pl.multiple_of(b * 4 * QB, 4 * QB)
            added = jnp.concatenate(
                [bias[pl.ds(bias_rows + h, QB, stride=4), :] for h in range(4)], axis=0
            )
            for seed in range(SEEDS):
                work.append((rows, query_rows, added, seed))
        scores = []
        for rows, query_rows, added, seed in work:
            query = packed[seed, pl.ds(query_rows, QB), 0:CA]
            key = packed[seed, pl.ds(rows, WIN), CA : 2 * CA]
            stacked = jnp.concatenate([query * head_mask[h] for h in range(4)], axis=0)
            scores.append(dot_t(stacked, key) * (32**-0.5) + added)
        weights = [jnp.exp(s - jnp.max(s, axis=-1, keepdims=True)).astype(BF16) for s in scores]
        for (rows, _, _, seed), w in zip(work, weights):
            value = jnp.concatenate([packed[seed, pl.ds(rows, WIN), 2 * CA : 3 * CA], ones], axis=1)
            out = dot(w, value)
            joined = out[3 * QB :]
            for h in range(3):
                joined = jnp.where(jnp.concatenate([lane_head, lane_head], axis=1) == h, out[h * QB : (h + 1) * QB], joined)
            mixed[seed, pl.ds(rows, QB), :] = (joined[:, :CA] / joined[:, CA:]).astype(BF16)
        return carry

    lax.fori_loop(0, blocks // unroll, body, 0)


def pack_kernel(place, feats, bias, index, pair_bias, up, down, send, joined, rows, sems):
    base, core = place[0] * TOKS, place[1]
    rows[0:16] = jnp.broadcast_to((index[7:8] - (base + TOKS)).astype(F32).astype(BF16), (16, CA))
    rows[16:32] = jnp.broadcast_to((index[0:1] - base).astype(F32).astype(BF16), (16, CA))
    moves = (
        (pair_bias.at[1 - core], send),
        (pair_bias.at[core], joined.at[pl.ds(0, TOKS)]),
        (feats.at[pl.ds(2 * (ATOMS - LOWER), 2 * LOWER)], up.at[pl.ds(0, 2 * LOWER)]),
        (bias.at[pl.ds(4 * (ATOMS - QB), 4 * QB)], up.at[pl.ds(2 * LOWER, 4 * QB)]),
        (rows.at[pl.ds(0, 16)], up.at[pl.ds(2 * LOWER + 4 * QB, 16)]),
        (feats.at[pl.ds(0, 2 * MARGIN)], down.at[pl.ds(0, 2 * MARGIN)]),
        (rows.at[pl.ds(16, 16)], down.at[pl.ds(2 * MARGIN, 16)]),
    )
    copies = [pltpu.make_async_copy(a, b, sems.at[i]) for i, (a, b) in enumerate(moves)]
    for copy in copies:
        copy.start()
    for copy in copies:
        copy.wait()


def pack(place, feats, bias, index, pair_bias):
    return pl.pallas_call(
        pack_kernel,
        out_shape=(
            jax.ShapeDtypeStruct((UP_ROWS, CA), BF16),
            jax.ShapeDtypeStruct((DOWN_ROWS, CA), BF16),
            jax.ShapeDtypeStruct((TOKS, ALL_TOKS), BF16),
            jax.ShapeDtypeStruct((2 * TOKS, ALL_TOKS), BF16),
        ),
        in_specs=[pl.BlockSpec(memory_space=pltpu.SMEM)] + anywhere(2) + vmem(1) + anywhere(1),
        out_specs=tuple(anywhere(4)),
        scratch_shapes=[pltpu.VMEM((32, CA), BF16), pltpu.SemaphoreType.DMA((7,))],
        compiler_params=params(58),
        cost_estimate=SMALL,
        name="pack",
    )(place, feats, bias, index, pair_bias)


def join_kernel(joined, received, out, sem):
    copy = pltpu.make_async_copy(received, out.at[pl.ds(TOKS, TOKS)], sem)
    copy.start()
    copy.wait()


def join(joined, received):
    return pl.pallas_call(
        join_kernel,
        out_shape=jax.ShapeDtypeStruct(joined.shape, BF16),
        in_specs=anywhere(2),
        out_specs=anywhere(1)[0],
        input_output_aliases={0: 0},
        scratch_shapes=[pltpu.SemaphoreType.DMA],
        compiler_params=params(58),
        cost_estimate=SMALL,
        name="join",
    )(joined, received)


def hold_kernel(*refs):
    del refs


def hold(*arrays):
    return pl.pallas_call(
        hold_kernel,
        out_shape=tuple(jax.ShapeDtypeStruct(array.shape, array.dtype) for array in arrays),
        in_specs=anywhere(len(arrays)),
        out_specs=tuple(anywhere(len(arrays))),
        input_output_aliases={i: i for i in range(len(arrays))},
        compiler_params=params(58),
        cost_estimate=SMALL,
        name="hold",
    )(*arrays)


def encode_kernel(
    place, feats, low, high, bias, index, cond, project, mix, pool, fence,
    encoded, first, last, residual, normed,
    rows, bias32, packed, mixed, ext,
):
    rows[0 : 2 * LOWER] = low[0 : 2 * LOWER].astype(F32)
    rows[2 * LOWER : 2 * (LOWER + ATOMS)] = feats[...].astype(F32)
    rows[2 * (LOWER + ATOMS) : 2 * EXT] = high[0 : 2 * MARGIN].astype(F32)
    bias32[0 : 4 * QB] = low[2 * LOWER : 2 * LOWER + 4 * QB].astype(F32)
    bias32[4 * QB :] = bias[...].astype(F32)
    for seed in range(SEEDS):
        values = rows[pl.ds(seed, EXT, stride=2), :]
        packed[seed] = dot(layer_norm(values).astype(BF16), project[...]).astype(BF16)
    window_blocks(packed, bias32, mixed, 33, place[0] * ATOMS - QB - MARGIN, 11)
    token = lax.broadcasted_iota(jnp.int32, (TOKS, CA), 0)
    below = low[2 * LOWER + 4 * QB :].astype(F32)[0:1].astype(jnp.int32)
    below = jnp.where(place[0] == 0, -1000, below)
    base = place[0] * TOKS
    chosen = jnp.concatenate(
        [(index[i : i + 1] - base == token).astype(F32) for i in range(8)]
        + [(below == token).astype(F32)],
        axis=1,
    )
    counts = jnp.sum(chosen, axis=1, keepdims=True)
    chosen = chosen.astype(BF16)
    for seed in range(SEEDS):
        values = rows[pl.ds(2 * MARGIN + seed, QB + ATOMS, stride=2), :]
        result = (values + dot(mixed[seed], mix[...])).astype(BF16)
        ext[0:ATOMS] = result[QB:]
        ext[ATOMS : EXT - QB] = jnp.zeros((EXT - QB - ATOMS, CA), BF16)
        ext[EXT - QB :] = result[0:QB]
        encoded[seed] = ext[0:ATOMS]
        first[seed] = ext[0:MARGIN]
        last[seed] = ext[ATOMS - MARGIN : ATOMS]
        lifted = jnp.maximum(dot(ext[...], pool[...]), 0.0).astype(BF16)
        state = cond[...].astype(F32) + dot(chosen, lifted) / counts
        residual[seed] = state
        normed[seed] = layer_norm(state).astype(BF16)


def encode(*args):
    return pl.pallas_call(
        encode_kernel,
        out_shape=(
            jax.ShapeDtypeStruct((SEEDS, ATOMS, CA), BF16),
            jax.ShapeDtypeStruct((SEEDS, MARGIN, CA), BF16),
            jax.ShapeDtypeStruct((SEEDS, MARGIN, CA), BF16),
            jax.ShapeDtypeStruct((SEEDS, TOKS, CT), F32),
            jax.ShapeDtypeStruct((SEEDS, TOKS, CT), BF16),
        ),
        in_specs=[pl.BlockSpec(memory_space=pltpu.SMEM)] + vmem(9) + anywhere(1),
        out_specs=tuple(vmem(5)),
        scratch_shapes=[
            pltpu.VMEM((2 * EXT, CA), F32),
            pltpu.VMEM((33 * 4 * QB, WIN), F32),
            pltpu.VMEM((SEEDS, EXT, 3 * CA), BF16),
            pltpu.VMEM((SEEDS, QB + ATOMS, CA), BF16),
            pltpu.VMEM((EXT, CA), BF16),
        ],
        compiler_params=params(58),
        cost_estimate=SMALL,
        name="encode",
    )(*args)


def decode_kernel(
    place, enc, enc_low, enc_high, spread, spread_low, spread_high, bias, index, low, high,
    project, mix,
    update,
    rows, bias32, packed, mixed, decoded, tokens, moved,
):
    bias32[...] = bias[...].astype(F32)
    token = lax.broadcasted_iota(jnp.int32, (TOKS + 2 * EDGE, CA), 0) - EDGE
    below = low[2 * LOWER + 4 * QB :].astype(F32)[0:1].astype(jnp.int32)
    above = high[2 * MARGIN :].astype(F32)[0:1].astype(jnp.int32) + TOKS
    base = place[0] * TOKS
    chosen = jnp.concatenate(
        [(index[i : i + 1] - base == token).astype(F32) for i in range(8)]
        + [(below == token).astype(F32), (above == token).astype(F32)],
        axis=1,
    ).astype(BF16)
    end = MARGIN + ATOMS
    for seed in range(SEEDS):
        tokens[0:EDGE] = spread_low[seed]
        tokens[EDGE : EDGE + TOKS] = spread[seed]
        tokens[EDGE + TOKS :] = spread_high[seed]
        moved[...] = lax.dot_general(
            chosen, tokens[...], (((0,), (0,)), ((), ())), preferred_element_type=F32
        )
        decoded[0:MARGIN] = enc_low[seed].astype(F32) + moved[ATOMS + CA - MARGIN : ATOMS + CA]
        decoded[MARGIN:end] = enc[seed].astype(F32) + moved[0:ATOMS]
        decoded[end : end + MARGIN] = (
            enc_high[seed].astype(F32) + moved[ATOMS + CA : ATOMS + CA + MARGIN]
        )
        decoded[end + MARGIN :] = jnp.zeros((EXT - end - MARGIN, CA), F32)
        values = decoded[...].astype(BF16).astype(F32)
        rows[pl.ds(seed, EXT, stride=2), :] = values
        packed[seed] = dot(layer_norm(values).astype(BF16), project[...]).astype(BF16)
    window_blocks(packed, bias32, mixed, 32, place[0] * ATOMS - MARGIN, 8)
    for seed in range(SEEDS):
        at = pl.ds(2 * MARGIN + seed, ATOMS, stride=2)
        rows[at, :] = rows[at, :] + dot(mixed[seed], mix[...])
    update[...] = rows[2 * MARGIN : 2 * (MARGIN + ATOMS)].astype(BF16)


def decode(*args):
    return pl.pallas_call(
        decode_kernel,
        out_shape=jax.ShapeDtypeStruct((SEEDS * ATOMS, CA), BF16),
        in_specs=[pl.BlockSpec(memory_space=pltpu.SMEM)] + vmem(12),
        out_specs=vmem(1)[0],
        scratch_shapes=[
            pltpu.VMEM((2 * EXT, CA), F32),
            pltpu.VMEM((32 * 4 * QB, WIN), F32),
            pltpu.VMEM((SEEDS, EXT, 3 * CA), BF16),
            pltpu.VMEM((SEEDS, ATOMS, CA), BF16),
            pltpu.VMEM((EXT, CA), F32),
            pltpu.VMEM((TOKS + 2 * EDGE, CA), BF16),
            pltpu.VMEM((ATOMS + 2 * CA, CA), F32),
        ],
        compiler_params=params(58),
        cost_estimate=SMALL,
        name="decode",
    )(*args)


def spaced_kernel(place, first, second, fence, out):
    core = place[1]
    for group in range(4):
        start = PAIR * group // 128 * 128
        shift = PAIR * group - start + HEAD * core
        width = min(256, 384 - start)
        row = lax.broadcasted_iota(jnp.int32, (width, 128), 0) - shift
        lane = lax.broadcasted_iota(jnp.int32, (width, 128), 1)

        def pick(side):
            at = lane - HEAD * side
            return ((row == at) & (at >= 0) & (at < HEAD)).astype(F32).astype(BF16)

        block = dot(first[:, start : start + width], pick(1 - core)) + dot(
            second[:, start : start + width], pick(core)
        )
        out[0, group // 2, :, group % 2 * 128 : group % 2 * 128 + 128] = block.astype(BF16)


def spaced(place, weight, fence):
    return pl.pallas_call(
        spaced_kernel,
        grid=(4,),
        out_shape=jax.ShapeDtypeStruct((2, GROUPS // 2, CT, 256), BF16),
        in_specs=[
            pl.BlockSpec(memory_space=pltpu.SMEM),
            pl.BlockSpec((CT, 384), lambda i: (0, i)),
            pl.BlockSpec((CT, 384), lambda i: (0, jnp.where(i < 2, 6 + i, 2 + i))),
        ]
        + anywhere(1),
        out_specs=pl.BlockSpec((1, 2, CT, 256), lambda i: (i // 2, i % 2, 0, 0)),
        compiler_params=params(58),
        cost_estimate=SMALL,
        name="spaced",
    )(place, weight, weight, fence)


def queries_kernel(place, normed, other, weight, fence, query, gate):
    core = place[1]
    lane = lax.broadcasted_iota(jnp.int32, (1, 128), 1)
    in_query = (lane // HEAD == 1 - core) & (lane < PAIR)
    in_gate = (lane // HEAD == core) & (lane < PAIR)
    values = jnp.concatenate([normed[0], other[0], normed[1], other[1]], axis=0)
    for pair in range(GROUPS // 2):
        product = dot(values, weight[0, pair])
        for side in range(2):
            part = product[:, side * 128 : side * 128 + 128]
            group = 2 * pair + side
            queried = jnp.where(in_query, part * (HEAD**-0.5), 0.0).astype(BF16)
            opened = jnp.where(in_gate, jax.nn.sigmoid(part), 0.0)
            for seed in range(SEEDS):
                at = slice(seed * 2 * TOKS, (seed + 1) * 2 * TOKS)
                query[group, seed] = queried[at]
                gate[group, seed] = opened[at]


def queries(place, normed, other, weight, fence):
    return pl.pallas_call(
        queries_kernel,
        grid=(1,),
        out_shape=(
            jax.ShapeDtypeStruct((GROUPS, SEEDS, 2 * TOKS, 128), BF16),
            jax.ShapeDtypeStruct((GROUPS, SEEDS, 2 * TOKS, 128), F32),
        ),
        in_specs=[pl.BlockSpec(memory_space=pltpu.SMEM)]
        + vmem(2)
        + [pl.BlockSpec((1, GROUPS // 2, CT, 256), lambda i: (0, 0, 0, 0))]
        + anywhere(1),
        out_specs=tuple(vmem(2)),
        compiler_params=params(50),
        cost_estimate=LARGE,
        name="queries",
    )(place, normed, other, weight, fence)


def keys_kernel(tokens, weight, out):
    count = tokens.shape[0]
    values = jnp.concatenate([tokens[i].reshape(SEEDS * TOKS, CT) for i in range(count)], axis=0)
    ones = (lax.broadcasted_iota(jnp.int32, (1, 256), 1) % 128 == PAIR).astype(F32)
    for pair in range(GROUPS // 2):
        product = (dot(values, weight[0, pair]) + ones).astype(BF16)
        for side in range(2):
            for i in range(count):
                for seed in range(SEEDS):
                    start = (i * SEEDS + seed) * TOKS
                    out[2 * pair + side, seed, i * TOKS : (i + 1) * TOKS] = product[
                        start : start + TOKS, side * 128 : side * 128 + 128
                    ]


def keys(tokens, weight):
    step = 4
    return pl.pallas_call(
        keys_kernel,
        grid=(tokens.shape[0] // step,),
        out_shape=jax.ShapeDtypeStruct((GROUPS, SEEDS, ALL_TOKS, 128), BF16),
        in_specs=[
            pl.BlockSpec((step, SEEDS, TOKS, CT), lambda i: (i, 0, 0, 0)),
            pl.BlockSpec((1, GROUPS // 2, CT, 256), lambda i: (1, 0, 0, 0)),
        ],
        out_specs=pl.BlockSpec((GROUPS, SEEDS, step * TOKS, 128), lambda i: (0, 0, i, 0)),
        compiler_params=params(50),
        cost_estimate=SMALL,
        name="keys",
    )(tokens, weight)


def attend_kernel(pieces, extra, group_ids, query, gate, key_value, *rest):
    biases = rest[: sum(pieces)]
    own, sent, bias, scores = rest[sum(pieces) + extra :]
    step = pl.program_id(0)
    at = 0
    for i, parts in enumerate(pieces):
        refs = biases[at : at + parts]
        at += parts

        @pl.when(step == i)
        def _(refs=refs):
            place = 0
            for ref in refs:
                size = ref.shape[0]
                bias[place : place + size] = ref[...]
                place += size

    width = 512
    tops = []
    for seed in range(SEEDS):
        peak = None
        for c in range(ALL_TOKS // width):
            cols = slice(c * width, (c + 1) * width)
            part = dot_t(query[0, seed], key_value[0, seed, cols, :]) + bias[:, cols].astype(F32)
            scores[seed, :, cols] = part
            for w in range(width // 128):
                tile = part[:, w * 128 : (w + 1) * 128]
                peak = tile if peak is None else jnp.maximum(peak, tile)
        tops.append(jnp.max(peak, axis=-1, keepdims=True))
    for seed in range(SEEDS):
        total = None
        for c in range(ALL_TOKS // width):
            cols = slice(c * width, (c + 1) * width)
            part = dot(
                jnp.exp(scores[seed, :, cols] - tops[seed]).astype(BF16), key_value[0, seed, cols, :]
            )
            total = part if total is None else total + part
        gated = (total / total[:, PAIR : PAIR + 1] * gate[0, seed]).astype(BF16)
        own[0, seed] = gated[:TOKS]
        sent[0, seed] = gated[TOKS:]


def attend(group_ids, query, gate, key_value, before, pieces):
    flat = [ref for parts in pieces for ref in parts]
    shape = jax.ShapeDtypeStruct((GROUPS, SEEDS, TOKS, 128), BF16)

    def by_group(*block):
        return pl.BlockSpec((1,) + block, lambda i, ids: (ids[i],) + (0,) * len(block))

    grid_spec = pltpu.PrefetchScalarGridSpec(
        num_scalar_prefetch=1,
        grid=(len(pieces),),
        in_specs=[
            by_group(SEEDS, 2 * TOKS, 128),
            by_group(SEEDS, 2 * TOKS, 128),
            by_group(SEEDS, ALL_TOKS, 128),
        ]
        + vmem(len(flat))
        + anywhere(len(before)),
        out_specs=(by_group(SEEDS, TOKS, 128),) * 2,
        scratch_shapes=[
            pltpu.VMEM((2 * TOKS, ALL_TOKS), BF16),
            pltpu.VMEM((SEEDS, 2 * TOKS, ALL_TOKS), F32),
        ],
    )
    return pl.pallas_call(
        functools.partial(attend_kernel, tuple(len(parts) for parts in pieces), len(before)),
        grid_spec=grid_spec,
        out_shape=(shape, shape),
        input_output_aliases={4 + len(flat) + i: i for i in range(len(before))},
        compiler_params=params(50),
        cost_estimate=SMALL,
        name="attend",
    )(group_ids, query, gate, key_value, *flat, *before)


def finish_kernel(
    residual, own, received, mix, wide_hbm, narrow_hbm, spread_weight,
    state, spread, first, last,
    wide, narrow, mix_tile, total, hidden, sems,
):
    step = 512
    count = TRANS // step
    copies = []
    for c in range(count):
        gate_cols = pl.ds(c * step, step)
        up_cols = pl.ds(TRANS + c * step, step)
        copies.append(
            [
                pltpu.make_async_copy(wide_hbm.at[:, gate_cols], wide.at[:, gate_cols], sems.at[c, 0]),
                pltpu.make_async_copy(wide_hbm.at[:, up_cols], wide.at[:, up_cols], sems.at[c, 1]),
                pltpu.make_async_copy(narrow_hbm.at[gate_cols], narrow.at[gate_cols], sems.at[c, 2]),
            ]
        )
    for group in copies:
        for copy in group:
            copy.start()
    values = residual[...].reshape(SEEDS * TOKS, CT)
    for group in range(GROUPS):
        gated = (own[group] + received[group]).reshape(SEEDS * TOKS, 128)
        mix_tile[group, 0:PAIR] = mix[group]
        mix_tile[group, PAIR:128] = jnp.zeros((128 - PAIR, CT), BF16)
        values = values + dot(gated, mix_tile[group])
    total[...] = values
    normed = layer_norm(values).astype(BF16)
    for c in range(count):
        for copy in copies[c]:
            copy.wait()
        gate = dot(normed, wide[:, c * step : (c + 1) * step])
        up = dot(normed, wide[:, TRANS + c * step : TRANS + (c + 1) * step])
        hidden[:, c * step : (c + 1) * step] = (jax.nn.silu(gate) * up).astype(BF16)
    rounded = (total[...] + dot(hidden[...], narrow[...])).astype(BF16)
    state[...] = rounded.reshape(SEEDS, TOKS, CT)
    carried = dot(rounded, spread_weight[...]).astype(BF16).reshape(SEEDS, TOKS, CA)
    spread[...] = carried
    first[...] = carried[:, :EDGE]
    last[...] = carried[:, TOKS - EDGE :]


def finish(residual, own, received, mix, wide, narrow, spread_weight):
    return pl.pallas_call(
        finish_kernel,
        out_shape=(
            jax.ShapeDtypeStruct((SEEDS, TOKS, CT), BF16),
            jax.ShapeDtypeStruct((SEEDS, TOKS, CA), BF16),
            jax.ShapeDtypeStruct((SEEDS, EDGE, CA), BF16),
            jax.ShapeDtypeStruct((SEEDS, EDGE, CA), BF16),
        ),
        in_specs=vmem(4) + anywhere(2) + vmem(1),
        out_specs=tuple(vmem(4)),
        scratch_shapes=[
            pltpu.VMEM((CT, 2 * TRANS), BF16),
            pltpu.VMEM((TRANS, CT), BF16),
            pltpu.VMEM((GROUPS, 128, CT), BF16),
            pltpu.VMEM((SEEDS * TOKS, CT), F32),
            pltpu.VMEM((SEEDS * TOKS, TRANS), BF16),
            pltpu.SemaphoreType.DMA((3, 3)),
        ],
        compiler_params=params(58),
        cost_estimate=SMALL,
        name="finish",
    )(residual, own, received, mix, wide, narrow, spread_weight)


def along_tok(values, by):
    return lax.ppermute(values, "tok", [(i, (i + by) % 16) for i in range(16)])


def across_core(values):
    return lax.ppermute(values, "tok", [(i, i ^ 1) for i in range(16)])


def along_y(values, by):
    return lax.ppermute(values, "seed", [(i, (i + 2 * by) % 8) for i in range(8)])


def along_z(values):
    return lax.ppermute(values, "seed", [(i, i ^ 1) for i in range(8)])


def per_device(
    atom_feats, atom_index, token_cond, pair_bias, atom_bias_enc, atom_bias_dec,
    enc_project, enc_mix, pool_weight, token_project, token_mix, swiglu_in, swiglu_out,
    spread_weight, dec_project, dec_mix,
):
    tok = lax.axis_index("tok")
    seed = lax.axis_index("seed")
    place = jnp.stack([tok, tok % 2]).astype(jnp.int32)
    feats = atom_feats.reshape(SEEDS * ATOMS, CA)
    bias_enc = atom_bias_enc.reshape(4 * ATOMS, WIN)
    bias_dec = atom_bias_dec.reshape(4 * ATOMS, WIN)
    index = atom_index.reshape(8, CA)

    up, down, send, joined = pack(place, feats, bias_enc, index, pair_bias)
    mine = join(joined, across_core(send))
    low = along_tok(up, 1)
    high = along_tok(down, -1)
    below = along_y(mine, 1)
    above = along_y(mine, -1)
    other = along_z(mine)

    encoded, first, last, residual, normed = encode(
        place, feats, low, high, bias_enc, index, token_cond, enc_project, enc_mix, pool_weight,
        mine,
    )
    everyone = lax.all_gather(normed, "tok", axis=0)
    below, above, other, first, last = hold(below, above, other, first, last)
    far = (along_y(below[:TOKS], 1), along_y(above[TOKS:], -1))
    other_below = along_y(other, 1)
    other_above = along_y(other, -1)
    enc_low = along_tok(last, 1)
    enc_high = along_tok(first, -1)
    weights = spaced(place, token_project, below)
    query, gate = queries(place, normed, across_core(normed), weights, below)

    everyone, other_below, other_above, query, enc_low, enc_high = hold(
        everyone, other_below, other_above, query, enc_low, enc_high
    )
    other_far = (along_y(other_below[:TOKS], 1), along_y(other_above[TOKS:], -1))
    key_value = keys(everyone, weights)

    level, side = seed // 2, seed % 2

    def ids(*offsets):
        return jnp.stack([(level + dy) % 4 * 2 + (side ^ dz) for dy, dz in offsets]).astype(jnp.int32)

    done = attend(
        ids((0, 0), (3, 0), (1, 0), (2, 0), (0, 1)), query, gate, key_value, (),
        ((mine,), (below,), (above,), far, (other,)),
    )
    done = attend(
        ids((3, 1), (1, 1)), query, gate, key_value, done, ((other_below,), (other_above,))
    )
    own, sent = attend(ids((2, 1)), query, gate, key_value, done, (other_far,))

    state, spread, spread_first, spread_last = finish(
        residual, own, across_core(sent), token_mix.reshape(GROUPS, PAIR, CT), swiglu_in,
        swiglu_out, spread_weight,
    )
    update = decode(
        place, encoded, enc_low, enc_high, spread, along_tok(spread_last, 1),
        along_tok(spread_first, -1), bias_dec, index, low, high, dec_project, dec_mix,
    )
    return state.transpose(1, 0, 2), update.reshape(ATOMS, SEEDS, CA)


def solution(mesh):
    placed = (
        P("tok", "seed", None),
        P("tok"),
        P("tok", None),
        P("seed", "tok", None),
        P("tok", None, None),
        P("tok", None, None),
    ) + (P(),) * 10
    return jax.shard_map(
        per_device,
        mesh=mesh,
        in_specs=placed,
        out_specs=(P("tok", "seed", None), P("tok", "seed", None)),
        check_vma=False,
    )
```

```python
import functools

import jax
import jax.numpy as jnp
from jax import lax
from jax.experimental import pallas as pl
from jax.experimental.pallas import tpu as pltpu
from jax.sharding import PartitionSpec as P

EPS = 1e-05
NEG = -1000000000.0
F32 = jnp.float32
BF16 = jnp.bfloat16

SEEDS = 2
ATOMS = 1024
TOKS = 128
CA = 128
CT = 768
HEADS = 16
HEAD = 48
PAIR = 96
GROUPS = 8
QB = 32
WIN = 128
MARGIN = 48
LOWER = 80
EXT = 1152
EDGE = 16
TRANS = 1536
ALL_TOKS = 2048
ALL_ATOMS = 16384
UP_ROWS = 2 * LOWER + 4 * QB + 16
DOWN_ROWS = 2 * MARGIN + 16


SMALL = pl.CostEstimate(flops=10**6, bytes_accessed=10**4, transcendentals=0)
LARGE = pl.CostEstimate(flops=7 * 10**10, bytes_accessed=10**4, transcendentals=0)


def params(limit_mb, **more):
    return pltpu.CompilerParams(vmem_limit_bytes=limit_mb * 1024 * 1024, **more)


def vmem(n):
    return [pl.BlockSpec(memory_space=pltpu.VMEM)] * n


def anywhere(n):
    return [pl.BlockSpec(memory_space=pltpu.HBM)] * n


def layer_norm(values):
    centre = values - jnp.mean(values, axis=-1, keepdims=True)
    variance = jnp.mean(centre * centre, axis=-1, keepdims=True)
    return centre * lax.rsqrt(variance + EPS)


def dot(a, b):
    return jnp.dot(a, b, preferred_element_type=F32)


def dot_t(a, b):
    return lax.dot_general(a, b, (((1,), (1,)), ((), ())), preferred_element_type=F32)


def window_blocks(packed, bias, mixed, blocks, first_atom, unroll):
    lane_head = lax.broadcasted_iota(jnp.int32, (QB, CA), 1) // 32
    head_mask = [(lane_head == h).astype(BF16) for h in range(4)]
    lane = lax.broadcasted_iota(jnp.int32, (1, WIN), 1)
    ones = jnp.ones((WIN, CA), BF16)
    for b in (0, 1, 2, blocks - 2, blocks - 1):
        position = lane + (first_atom + b * QB)
        inside = (position >= 0) & (position < ALL_ATOMS)
        place = slice(b * 4 * QB, (b + 1) * 4 * QB)
        bias[place] = jnp.where(inside, bias[place], NEG)

    def body(i, carry):
        work = []
        for u in range(unroll):
            b = i * unroll + u
            rows = pl.multiple_of(b * QB, QB)
            query_rows = pl.multiple_of(b * QB + MARGIN, 16)
            bias_rows = pl.multiple_of(b * 4 * QB, 4 * QB)
            added = jnp.concatenate(
                [bias[pl.ds(bias_rows + h, QB, stride=4), :] for h in range(4)], axis=0
            )
            for seed in range(SEEDS):
                work.append((rows, query_rows, added, seed))
        scores = []
        for rows, query_rows, added, seed in work:
            query = packed[seed, pl.ds(query_rows, QB), 0:CA]
            key = packed[seed, pl.ds(rows, WIN), CA : 2 * CA]
            stacked = jnp.concatenate([query * head_mask[h] for h in range(4)], axis=0)
            scores.append(dot_t(stacked, key) * (32**-0.5) + added)
        weights = [jnp.exp(s - jnp.max(s, axis=-1, keepdims=True)).astype(BF16) for s in scores]
        for (rows, _, _, seed), w in zip(work, weights):
            value = jnp.concatenate([packed[seed, pl.ds(rows, WIN), 2 * CA : 3 * CA], ones], axis=1)
            out = dot(w, value)
            joined = out[3 * QB :]
            for h in range(3):
                joined = jnp.where(jnp.concatenate([lane_head, lane_head], axis=1) == h, out[h * QB : (h + 1) * QB], joined)
            mixed[seed, pl.ds(rows, QB), :] = (joined[:, :CA] / joined[:, CA:]).astype(BF16)
        return carry

    lax.fori_loop(0, blocks // unroll, body, 0)


def pack_kernel(place, feats, bias, index, pair_bias, up, down, send, joined, heads, rows, sems):
    base, core = place[0] * TOKS, place[1]
    low_rows, high_rows = UP_ROWS - 16, DOWN_ROWS - 16
    loads = (
        (pair_bias, heads),
        (feats.at[pl.ds(2 * (ATOMS - LOWER), 2 * LOWER)], rows.at[pl.ds(0, 2 * LOWER)]),
        (bias.at[pl.ds(4 * (ATOMS - QB), 4 * QB)], rows.at[pl.ds(2 * LOWER, 4 * QB)]),
        (feats.at[pl.ds(0, 2 * MARGIN)], rows.at[pl.ds(UP_ROWS, 2 * MARGIN)]),
    )
    loads = [pltpu.make_async_copy(a, b, sems.at[i]) for i, (a, b) in enumerate(loads)]
    for copy in loads:
        copy.start()
    tail = (index[7:8] - (base + TOKS)).astype(F32)
    head = (index[0:1] - base).astype(F32)
    rows[low_rows:UP_ROWS] = jnp.broadcast_to(tail, (16, CA)).astype(BF16)
    rows[UP_ROWS + high_rows :] = jnp.broadcast_to(head, (16, CA)).astype(BF16)
    for copy in loads:
        copy.wait()
    stores = (
        (rows.at[pl.ds(0, UP_ROWS)], up),
        (rows.at[pl.ds(UP_ROWS, DOWN_ROWS)], down),
        (heads.at[1 - core], send),
        (heads.at[core], joined.at[pl.ds(0, TOKS)]),
    )
    stores = [pltpu.make_async_copy(a, b, sems.at[4 + i]) for i, (a, b) in enumerate(stores)]
    for copy in stores:
        copy.start()
    for copy in stores:
        copy.wait()


def pack(place, feats, bias, index, pair_bias):
    return pl.pallas_call(
        pack_kernel,
        out_shape=(
            jax.ShapeDtypeStruct((UP_ROWS, CA), BF16),
            jax.ShapeDtypeStruct((DOWN_ROWS, CA), BF16),
            jax.ShapeDtypeStruct((TOKS, ALL_TOKS), BF16),
            jax.ShapeDtypeStruct((2 * TOKS, ALL_TOKS), BF16),
        ),
        in_specs=[pl.BlockSpec(memory_space=pltpu.SMEM)] + anywhere(2) + vmem(1) + anywhere(1),
        out_specs=tuple(anywhere(4)),
        scratch_shapes=[
            pltpu.VMEM((2, TOKS, ALL_TOKS), BF16),
            pltpu.VMEM((UP_ROWS + DOWN_ROWS, CA), BF16),
            pltpu.SemaphoreType.DMA((8,)),
        ],
        compiler_params=params(58),
        cost_estimate=SMALL,
        name="pack",
    )(place, feats, bias, index, pair_bias)


def join_kernel(joined, received, out, rows, sems):
    load = pltpu.make_async_copy(received, rows, sems.at[0])
    load.start()
    load.wait()
    store = pltpu.make_async_copy(rows, out.at[pl.ds(TOKS, TOKS)], sems.at[1])
    store.start()
    store.wait()


def join(joined, received):
    return pl.pallas_call(
        join_kernel,
        out_shape=jax.ShapeDtypeStruct(joined.shape, BF16),
        in_specs=anywhere(2),
        out_specs=anywhere(1)[0],
        input_output_aliases={0: 0},
        scratch_shapes=[pltpu.VMEM((TOKS, ALL_TOKS), BF16), pltpu.SemaphoreType.DMA((2,))],
        compiler_params=params(58),
        cost_estimate=SMALL,
        name="join",
    )(joined, received)


def hold_kernel(*refs):
    del refs


def hold(*arrays, cost=SMALL):
    return pl.pallas_call(
        hold_kernel,
        out_shape=tuple(jax.ShapeDtypeStruct(array.shape, array.dtype) for array in arrays),
        in_specs=anywhere(len(arrays)),
        out_specs=tuple(anywhere(len(arrays))),
        input_output_aliases={i: i for i in range(len(arrays))},
        compiler_params=params(58),
        cost_estimate=cost,
        name="hold",
    )(*arrays)


def encode_kernel(
    place, feats, low, high, bias, index, cond, project, mix, pool, fence,
    encoded, first, last, residual, normed, again,
    rows, bias32, packed, mixed, ext,
):
    rows[0 : 2 * LOWER] = low[0 : 2 * LOWER].astype(F32)
    rows[2 * LOWER : 2 * (LOWER + ATOMS)] = feats[...].astype(F32)
    rows[2 * (LOWER + ATOMS) : 2 * EXT] = high[0 : 2 * MARGIN].astype(F32)
    bias32[0 : 4 * QB] = low[2 * LOWER : 2 * LOWER + 4 * QB].astype(F32)
    bias32[4 * QB :] = bias[...].astype(F32)
    for seed in range(SEEDS):
        values = rows[pl.ds(seed, EXT, stride=2), :]
        packed[seed] = dot(layer_norm(values).astype(BF16), project[...]).astype(BF16)
    window_blocks(packed, bias32, mixed, 33, place[0] * ATOMS - QB - MARGIN, 11)
    token = lax.broadcasted_iota(jnp.int32, (TOKS, CA), 0)
    below = low[2 * LOWER + 4 * QB :].astype(F32)[0:1].astype(jnp.int32)
    below = jnp.where(place[0] == 0, -1000, below)
    base = place[0] * TOKS
    chosen = jnp.concatenate(
        [(index[i : i + 1] - base == token).astype(F32) for i in range(8)]
        + [(below == token).astype(F32)],
        axis=1,
    )
    counts = jnp.sum(chosen, axis=1, keepdims=True)
    chosen = chosen.astype(BF16)
    for seed in range(SEEDS):
        values = rows[pl.ds(2 * MARGIN + seed, QB + ATOMS, stride=2), :]
        result = (values + dot(mixed[seed], mix[...])).astype(BF16)
        ext[0:ATOMS] = result[QB:]
        ext[ATOMS : EXT - QB] = jnp.zeros((EXT - QB - ATOMS, CA), BF16)
        ext[EXT - QB :] = result[0:QB]
        encoded[seed] = ext[0:ATOMS]
        first[seed] = ext[0:MARGIN]
        last[seed] = ext[ATOMS - MARGIN : ATOMS]
        lifted = jnp.maximum(dot(ext[...], pool[...]), 0.0).astype(BF16)
        state = cond[...].astype(F32) + dot(chosen, lifted) / counts
        residual[seed] = state
        normed[seed] = layer_norm(state).astype(BF16)
        again[seed] = normed[seed]


def encode(*args):
    return pl.pallas_call(
        encode_kernel,
        out_shape=(
            jax.ShapeDtypeStruct((SEEDS, ATOMS, CA), BF16),
            jax.ShapeDtypeStruct((SEEDS, MARGIN, CA), BF16),
            jax.ShapeDtypeStruct((SEEDS, MARGIN, CA), BF16),
            jax.ShapeDtypeStruct((SEEDS, TOKS, CT), F32),
            jax.ShapeDtypeStruct((SEEDS, TOKS, CT), BF16),
            jax.ShapeDtypeStruct((SEEDS, TOKS, CT), BF16),
        ),
        in_specs=[pl.BlockSpec(memory_space=pltpu.SMEM)] + vmem(9) + anywhere(1),
        out_specs=tuple(vmem(6)),
        scratch_shapes=[
            pltpu.VMEM((2 * EXT, CA), F32),
            pltpu.VMEM((33 * 4 * QB, WIN), F32),
            pltpu.VMEM((SEEDS, EXT, 3 * CA), BF16),
            pltpu.VMEM((SEEDS, QB + ATOMS, CA), BF16),
            pltpu.VMEM((EXT, CA), BF16),
        ],
        compiler_params=params(58),
        cost_estimate=SMALL,
        name="encode",
    )(*args)


def decode_kernel(
    place, enc, enc_low, enc_high, spread, spread_low, spread_high, bias, index, low, high,
    project, mix,
    update,
    rows, bias32, packed, mixed, decoded, tokens, moved,
):
    bias32[...] = bias[...].astype(F32)
    token = lax.broadcasted_iota(jnp.int32, (TOKS + 2 * EDGE, CA), 0) - EDGE
    below = low[2 * LOWER + 4 * QB :].astype(F32)[0:1].astype(jnp.int32)
    above = high[2 * MARGIN :].astype(F32)[0:1].astype(jnp.int32) + TOKS
    base = place[0] * TOKS
    chosen = jnp.concatenate(
        [(index[i : i + 1] - base == token).astype(F32) for i in range(8)]
        + [(below == token).astype(F32), (above == token).astype(F32)],
        axis=1,
    ).astype(BF16)
    end = MARGIN + ATOMS
    for seed in range(SEEDS):
        tokens[0:EDGE] = spread_low[seed]
        tokens[EDGE : EDGE + TOKS] = spread[seed]
        tokens[EDGE + TOKS :] = spread_high[seed]
        moved[...] = lax.dot_general(
            chosen, tokens[...], (((0,), (0,)), ((), ())), preferred_element_type=F32
        )
        decoded[0:MARGIN] = enc_low[seed].astype(F32) + moved[ATOMS + CA - MARGIN : ATOMS + CA]
        decoded[MARGIN:end] = enc[seed].astype(F32) + moved[0:ATOMS]
        decoded[end : end + MARGIN] = (
            enc_high[seed].astype(F32) + moved[ATOMS + CA : ATOMS + CA + MARGIN]
        )
        decoded[end + MARGIN :] = jnp.zeros((EXT - end - MARGIN, CA), F32)
        values = decoded[...].astype(BF16).astype(F32)
        rows[pl.ds(seed, EXT, stride=2), :] = values
        packed[seed] = dot(layer_norm(values).astype(BF16), project[...]).astype(BF16)
    window_blocks(packed, bias32, mixed, 32, place[0] * ATOMS - MARGIN, 8)
    for seed in range(SEEDS):
        at = pl.ds(2 * MARGIN + seed, ATOMS, stride=2)
        rows[at, :] = rows[at, :] + dot(mixed[seed], mix[...])
    update[...] = rows[2 * MARGIN : 2 * (MARGIN + ATOMS)].astype(BF16)


def decode(*args):
    return pl.pallas_call(
        decode_kernel,
        out_shape=jax.ShapeDtypeStruct((SEEDS * ATOMS, CA), BF16),
        in_specs=[pl.BlockSpec(memory_space=pltpu.SMEM)] + vmem(12),
        out_specs=vmem(1)[0],
        scratch_shapes=[
            pltpu.VMEM((2 * EXT, CA), F32),
            pltpu.VMEM((32 * 4 * QB, WIN), F32),
            pltpu.VMEM((SEEDS, EXT, 3 * CA), BF16),
            pltpu.VMEM((SEEDS, ATOMS, CA), BF16),
            pltpu.VMEM((EXT, CA), F32),
            pltpu.VMEM((TOKS + 2 * EDGE, CA), BF16),
            pltpu.VMEM((ATOMS + 2 * CA, CA), F32),
        ],
        compiler_params=params(58),
        cost_estimate=SMALL,
        name="decode",
    )(*args)


def spaced_kernel(place, first, second, fence, out):
    core = place[1]
    for group in range(4):
        start = PAIR * group // 128 * 128
        shift = PAIR * group - start + HEAD * core
        width = min(256, 384 - start)
        row = lax.broadcasted_iota(jnp.int32, (width, 128), 0) - shift
        lane = lax.broadcasted_iota(jnp.int32, (width, 128), 1)

        def pick(side):
            at = lane - HEAD * side
            return ((row == at) & (at >= 0) & (at < HEAD)).astype(F32).astype(BF16)

        block = dot(first[:, start : start + width], pick(1 - core)) + dot(
            second[:, start : start + width], pick(core)
        )
        out[0, group // 2, :, group % 2 * 128 : group % 2 * 128 + 128] = block.astype(BF16)


def spaced(place, weight, fence):
    return pl.pallas_call(
        spaced_kernel,
        grid=(4,),
        out_shape=jax.ShapeDtypeStruct((2, GROUPS // 2, CT, 256), BF16),
        in_specs=[
            pl.BlockSpec(memory_space=pltpu.SMEM),
            pl.BlockSpec((CT, 384), lambda i: (0, i)),
            pl.BlockSpec((CT, 384), lambda i: (0, jnp.where(i < 2, 6 + i, 2 + i))),
        ]
        + anywhere(1),
        out_specs=pl.BlockSpec((1, 2, CT, 256), lambda i: (i // 2, i % 2, 0, 0)),
        compiler_params=params(58),
        cost_estimate=SMALL,
        name="spaced",
    )(place, weight, weight, fence)


def queries_kernel(place, normed, other, weight, fence, query, gate):
    core = place[1]
    lane = lax.broadcasted_iota(jnp.int32, (1, 128), 1)
    in_query = (lane // HEAD == 1 - core) & (lane < PAIR)
    in_gate = (lane // HEAD == core) & (lane < PAIR)
    values = jnp.concatenate([normed[0], other[0], normed[1], other[1]], axis=0)
    for pair in range(GROUPS // 2):
        product = dot(values, weight[0, pair])
        for side in range(2):
            part = product[:, side * 128 : side * 128 + 128]
            group = 2 * pair + side
            queried = jnp.where(in_query, part * (HEAD**-0.5), 0.0).astype(BF16)
            opened = jnp.where(in_gate, jax.nn.sigmoid(part), 0.0)
            for seed in range(SEEDS):
                at = slice(seed * 2 * TOKS, (seed + 1) * 2 * TOKS)
                query[group, seed] = queried[at]
                gate[group, seed] = opened[at]


def queries(place, normed, other, weight, fence):
    return pl.pallas_call(
        queries_kernel,
        grid=(1,),
        out_shape=(
            jax.ShapeDtypeStruct((GROUPS, SEEDS, 2 * TOKS, 128), BF16),
            jax.ShapeDtypeStruct((GROUPS, SEEDS, 2 * TOKS, 128), F32),
        ),
        in_specs=[pl.BlockSpec(memory_space=pltpu.SMEM)]
        + vmem(2)
        + [pl.BlockSpec((1, GROUPS // 2, CT, 256), lambda i: (0, 0, 0, 0))]
        + anywhere(1),
        out_specs=tuple(vmem(2)),
        compiler_params=params(50),
        cost_estimate=LARGE,
        name="queries",
    )(place, normed, other, weight, fence)


def keys_kernel(tokens, weight, out):
    count = tokens.shape[0]
    values = jnp.concatenate([tokens[i].reshape(SEEDS * TOKS, CT) for i in range(count)], axis=0)
    ones = (lax.broadcasted_iota(jnp.int32, (1, 256), 1) % 128 == PAIR).astype(F32)
    for pair in range(GROUPS // 2):
        product = (dot(values, weight[0, pair]) + ones).astype(BF16)
        for side in range(2):
            for i in range(count):
                for seed in range(SEEDS):
                    start = (i * SEEDS + seed) * TOKS
                    out[2 * pair + side, seed, i * TOKS : (i + 1) * TOKS] = product[
                        start : start + TOKS, side * 128 : side * 128 + 128
                    ]


def keys(tokens, weight):
    step = 4
    return pl.pallas_call(
        keys_kernel,
        grid=(tokens.shape[0] // step,),
        out_shape=jax.ShapeDtypeStruct((GROUPS, SEEDS, ALL_TOKS, 128), BF16),
        in_specs=[
            pl.BlockSpec((step, SEEDS, TOKS, CT), lambda i: (i, 0, 0, 0)),
            pl.BlockSpec((1, GROUPS // 2, CT, 256), lambda i: (1, 0, 0, 0)),
        ],
        out_specs=pl.BlockSpec((GROUPS, SEEDS, step * TOKS, 128), lambda i: (0, 0, i, 0)),
        compiler_params=params(50),
        cost_estimate=SMALL,
        name="keys",
    )(tokens, weight)


def attend_kernel(pieces, extra, group_ids, query, gate, key_value, *rest):
    biases = rest[: sum(pieces)]
    own, sent, bias, scores = rest[sum(pieces) + extra :]
    step = pl.program_id(0)
    at = 0
    for i, parts in enumerate(pieces):
        refs = biases[at : at + parts]
        at += parts

        @pl.when(step == i)
        def _(refs=refs):
            place = 0
            for ref in refs:
                size = ref.shape[0]
                bias[place : place + size] = ref[...]
                place += size

    width = 512
    tops = []
    for seed in range(SEEDS):
        peak = None
        for c in range(ALL_TOKS // width):
            cols = slice(c * width, (c + 1) * width)
            part = dot_t(query[0, seed], key_value[0, seed, cols, :]) + bias[:, cols].astype(F32)
            scores[seed, :, cols] = part
            for w in range(width // 128):
                tile = part[:, w * 128 : (w + 1) * 128]
                peak = tile if peak is None else jnp.maximum(peak, tile)
        tops.append(jnp.max(peak, axis=-1, keepdims=True))
    for seed in range(SEEDS):
        total = None
        for c in range(ALL_TOKS // width):
            cols = slice(c * width, (c + 1) * width)
            part = dot(
                jnp.exp(scores[seed, :, cols] - tops[seed]).astype(BF16), key_value[0, seed, cols, :]
            )
            total = part if total is None else total + part
        gated = (total / total[:, PAIR : PAIR + 1] * gate[0, seed]).astype(BF16)
        own[0, seed] = gated[:TOKS]
        sent[0, seed] = gated[TOKS:]


def attend(group_ids, query, gate, key_value, before, pieces):
    flat = [ref for parts in pieces for ref in parts]
    shape = jax.ShapeDtypeStruct((GROUPS, SEEDS, TOKS, 128), BF16)

    def by_group(*block):
        return pl.BlockSpec((1,) + block, lambda i, ids: (ids[i],) + (0,) * len(block))

    grid_spec = pltpu.PrefetchScalarGridSpec(
        num_scalar_prefetch=1,
        grid=(len(pieces),),
        in_specs=[
            by_group(SEEDS, 2 * TOKS, 128),
            by_group(SEEDS, 2 * TOKS, 128),
            by_group(SEEDS, ALL_TOKS, 128),
        ]
        + vmem(len(flat))
        + anywhere(len(before)),
        out_specs=(by_group(SEEDS, TOKS, 128),) * 2,
        scratch_shapes=[
            pltpu.VMEM((2 * TOKS, ALL_TOKS), BF16),
            pltpu.VMEM((SEEDS, 2 * TOKS, ALL_TOKS), F32),
        ],
    )
    return pl.pallas_call(
        functools.partial(attend_kernel, tuple(len(parts) for parts in pieces), len(before)),
        grid_spec=grid_spec,
        out_shape=(shape, shape),
        input_output_aliases={4 + len(flat) + i: i for i in range(len(before))},
        compiler_params=params(50),
        cost_estimate=SMALL,
        name="attend",
    )(group_ids, query, gate, key_value, *flat, *before)


def finish_kernel(
    residual, own, received, mix, wide_hbm, narrow_hbm, spread_weight,
    state, spread, first, last,
    wide, narrow, mix_tile, total, hidden, sems,
):
    step = 512
    count = TRANS // step
    copies = []
    for c in range(count):
        gate_cols = pl.ds(c * step, step)
        up_cols = pl.ds(TRANS + c * step, step)
        copies.append(
            [
                pltpu.make_async_copy(wide_hbm.at[:, gate_cols], wide.at[:, gate_cols], sems.at[c, 0]),
                pltpu.make_async_copy(wide_hbm.at[:, up_cols], wide.at[:, up_cols], sems.at[c, 1]),
                pltpu.make_async_copy(narrow_hbm.at[gate_cols], narrow.at[gate_cols], sems.at[c, 2]),
            ]
        )
    for group in copies:
        for copy in group:
            copy.start()
    values = residual[...].reshape(SEEDS * TOKS, CT)
    for group in range(GROUPS):
        gated = (own[group] + received[group]).reshape(SEEDS * TOKS, 128)
        mix_tile[group, 0:PAIR] = mix[group]
        mix_tile[group, PAIR:128] = jnp.zeros((128 - PAIR, CT), BF16)
        values = values + dot(gated, mix_tile[group])
    total[...] = values
    normed = layer_norm(values).astype(BF16)
    for c in range(count):
        for copy in copies[c]:
            copy.wait()
        gate = dot(normed, wide[:, c * step : (c + 1) * step])
        up = dot(normed, wide[:, TRANS + c * step : TRANS + (c + 1) * step])
        hidden[:, c * step : (c + 1) * step] = (jax.nn.silu(gate) * up).astype(BF16)
    rounded = (total[...] + dot(hidden[...], narrow[...])).astype(BF16)
    state[...] = rounded.reshape(SEEDS, TOKS, CT)
    carried = dot(rounded, spread_weight[...]).astype(BF16).reshape(SEEDS, TOKS, CA)
    spread[...] = carried
    first[...] = carried[:, :EDGE]
    last[...] = carried[:, TOKS - EDGE :]


def finish(residual, own, received, mix, wide, narrow, spread_weight):
    return pl.pallas_call(
        finish_kernel,
        out_shape=(
            jax.ShapeDtypeStruct((SEEDS, TOKS, CT), BF16),
            jax.ShapeDtypeStruct((SEEDS, TOKS, CA), BF16),
            jax.ShapeDtypeStruct((SEEDS, EDGE, CA), BF16),
            jax.ShapeDtypeStruct((SEEDS, EDGE, CA), BF16),
        ),
        in_specs=vmem(4) + anywhere(2) + vmem(1),
        out_specs=tuple(vmem(4)),
        scratch_shapes=[
            pltpu.VMEM((CT, 2 * TRANS), BF16),
            pltpu.VMEM((TRANS, CT), BF16),
            pltpu.VMEM((GROUPS, 128, CT), BF16),
            pltpu.VMEM((SEEDS * TOKS, CT), F32),
            pltpu.VMEM((SEEDS * TOKS, TRANS), BF16),
            pltpu.SemaphoreType.DMA((3, 3)),
        ],
        compiler_params=params(58),
        cost_estimate=SMALL,
        name="finish",
    )(residual, own, received, mix, wide, narrow, spread_weight)


def along_tok(values, by):
    return lax.ppermute(values, "tok", [(i, (i + by) % 16) for i in range(16)])


def across_core(values):
    return lax.ppermute(values, "tok", [(i, i ^ 1) for i in range(16)])


def along_y(values, by):
    return lax.ppermute(values, "seed", [(i, (i + 2 * by) % 8) for i in range(8)])


def along_z(values):
    return lax.ppermute(values, "seed", [(i, i ^ 1) for i in range(8)])


def per_device(
    atom_feats, atom_index, token_cond, pair_bias, atom_bias_enc, atom_bias_dec,
    enc_project, enc_mix, pool_weight, token_project, token_mix, swiglu_in, swiglu_out,
    spread_weight, dec_project, dec_mix,
):
    tok = lax.axis_index("tok")
    seed = lax.axis_index("seed")
    place = jnp.stack([tok, tok % 2]).astype(jnp.int32)
    feats = atom_feats.reshape(SEEDS * ATOMS, CA)
    bias_enc = atom_bias_enc.reshape(4 * ATOMS, WIN)
    bias_dec = atom_bias_dec.reshape(4 * ATOMS, WIN)
    index = atom_index.reshape(8, CA)

    up, down, send, joined = pack(place, feats, bias_enc, index, pair_bias)
    mine = join(joined, across_core(send))
    low = along_tok(up, 1)
    high = along_tok(down, -1)
    below = along_y(mine, 1)
    above = along_y(mine, -1)
    other = along_z(mine)

    encoded, first, last, residual, normed, again = encode(
        place, feats, low, high, bias_enc, index, token_cond, enc_project, enc_mix, pool_weight,
        mine,
    )
    everyone = lax.all_gather(normed, "tok", axis=0)
    below, above, other, first, last, again = hold(
        below, above, other, first, last, again, cost=LARGE
    )
    far = along_y(mine, 2)
    other_below = along_y(other, 1)
    other_above = along_y(other, -1)
    other_far = along_y(other, 2)
    enc_low = along_tok(last, 1)
    enc_high = along_tok(first, -1)
    weights = spaced(place, token_project, below)
    query, gate = queries(place, again, across_core(again), weights, below)
    everyone, query, enc_low, enc_high = hold(everyone, query, enc_low, enc_high)
    key_value = keys(everyone, weights)

    level, side = seed // 2, seed % 2

    def ids(*offsets):
        return jnp.stack([(level + dy) % 4 * 2 + (side ^ dz) for dy, dz in offsets]).astype(jnp.int32)

    done = attend(
        ids((0, 0), (3, 0), (1, 0), (2, 0), (0, 1)), query, gate, key_value, (),
        ((mine,), (below,), (above,), (far,), (other,)),
    )
    done = attend(
        ids((3, 1), (1, 1)), query, gate, key_value, done, ((other_below,), (other_above,))
    )
    own, sent = attend(ids((2, 1)), query, gate, key_value, done, ((other_far,),))

    state, spread, spread_first, spread_last = finish(
        residual, own, across_core(sent), token_mix.reshape(GROUPS, PAIR, CT), swiglu_in,
        swiglu_out, spread_weight,
    )
    update = decode(
        place, encoded, enc_low, enc_high, spread, along_tok(spread_last, 1),
        along_tok(spread_first, -1), bias_dec, index, low, high, dec_project, dec_mix,
    )
    return state.transpose(1, 0, 2), update.reshape(ATOMS, SEEDS, CA)


def solution(mesh):
    placed = (
        P("tok", "seed", None),
        P("tok"),
        P("tok", None),
        P("seed", "tok", None),
        P("tok", None, None),
        P("tok", None, None),
    ) + (P(),) * 10
    return jax.shard_map(
        per_device,
        mesh=mesh,
        in_specs=placed,
        out_specs=(P("tok", "seed", None), P("tok", "seed", None)),
        check_vma=False,
    )
```

```python
import functools

import jax
import jax.numpy as jnp
from jax import lax
from jax.experimental import pallas as pl
from jax.experimental.pallas import tpu as pltpu
from jax.sharding import PartitionSpec as P

EPS = 1e-05
NEG = -1000000000.0
F32 = jnp.float32
BF16 = jnp.bfloat16

SEEDS = 2
ATOMS = 1024
TOKS = 128
CA = 128
CT = 768
HEADS = 16
HEAD = 48
PAIR = 96
GROUPS = 8
QB = 32
WIN = 128
MARGIN = 48
LOWER = 80
EXT = 1152
EDGE = 16
TRANS = 1536
ALL_TOKS = 2048
ALL_ATOMS = 16384
UP_ROWS = 2 * LOWER + 4 * QB + 16
DOWN_ROWS = 2 * MARGIN + 16


SMALL = pl.CostEstimate(flops=10**6, bytes_accessed=10**4, transcendentals=0)
LARGE = pl.CostEstimate(flops=7 * 10**10, bytes_accessed=10**4, transcendentals=0)


def params(limit_mb, **more):
    return pltpu.CompilerParams(vmem_limit_bytes=limit_mb * 1024 * 1024, **more)


def vmem(n):
    return [pl.BlockSpec(memory_space=pltpu.VMEM)] * n


def anywhere(n):
    return [pl.BlockSpec(memory_space=pltpu.HBM)] * n


def layer_norm(values):
    centre = values - jnp.mean(values, axis=-1, keepdims=True)
    variance = jnp.mean(centre * centre, axis=-1, keepdims=True)
    return centre * lax.rsqrt(variance + EPS)


def dot(a, b):
    return jnp.dot(a, b, preferred_element_type=F32)


def dot_t(a, b):
    return lax.dot_general(a, b, (((1,), (1,)), ((), ())), preferred_element_type=F32)


def window_blocks(packed, bias, mixed, blocks, first_atom, unroll):
    lane_head = lax.broadcasted_iota(jnp.int32, (QB, CA), 1) // 32
    head_mask = [(lane_head == h).astype(BF16) for h in range(4)]
    lane = lax.broadcasted_iota(jnp.int32, (1, WIN), 1)
    ones = jnp.ones((WIN, CA), BF16)
    for b in (0, 1, 2, blocks - 2, blocks - 1):
        position = lane + (first_atom + b * QB)
        inside = (position >= 0) & (position < ALL_ATOMS)
        place = slice(b * 4 * QB, (b + 1) * 4 * QB)
        bias[place] = jnp.where(inside, bias[place], NEG)

    def body(i, carry):
        work = []
        for u in range(unroll):
            b = i * unroll + u
            rows = pl.multiple_of(b * QB, QB)
            query_rows = pl.multiple_of(b * QB + MARGIN, 16)
            bias_rows = pl.multiple_of(b * 4 * QB, 4 * QB)
            added = jnp.concatenate(
                [bias[pl.ds(bias_rows + h, QB, stride=4), :] for h in range(4)], axis=0
            )
            for seed in range(SEEDS):
                work.append((rows, query_rows, added, seed))
        scores = []
        for rows, query_rows, added, seed in work:
            query = packed[seed, pl.ds(query_rows, QB), 0:CA]
            key = packed[seed, pl.ds(rows, WIN), CA : 2 * CA]
            stacked = jnp.concatenate([query * head_mask[h] for h in range(4)], axis=0)
            scores.append(dot_t(stacked, key) * (32**-0.5) + added)
        weights = [jnp.exp(s - jnp.max(s, axis=-1, keepdims=True)).astype(BF16) for s in scores]
        for (rows, _, _, seed), w in zip(work, weights):
            value = jnp.concatenate([packed[seed, pl.ds(rows, WIN), 2 * CA : 3 * CA], ones], axis=1)
            out = dot(w, value)
            joined = out[3 * QB :]
            for h in range(3):
                joined = jnp.where(jnp.concatenate([lane_head, lane_head], axis=1) == h, out[h * QB : (h + 1) * QB], joined)
            mixed[seed, pl.ds(rows, QB), :] = (joined[:, :CA] / joined[:, CA:]).astype(BF16)
        return carry

    lax.fori_loop(0, blocks // unroll, body, 0)


def pack_kernel(place, feats, bias, index, pair_bias, up, down, send, joined, heads, rows, sems):
    base, core = place[0] * TOKS, place[1]
    low_rows, high_rows = UP_ROWS - 16, DOWN_ROWS - 16
    loads = (
        (pair_bias, heads),
        (feats.at[pl.ds(2 * (ATOMS - LOWER), 2 * LOWER)], rows.at[pl.ds(0, 2 * LOWER)]),
        (bias.at[pl.ds(4 * (ATOMS - QB), 4 * QB)], rows.at[pl.ds(2 * LOWER, 4 * QB)]),
        (feats.at[pl.ds(0, 2 * MARGIN)], rows.at[pl.ds(UP_ROWS, 2 * MARGIN)]),
    )
    loads = [pltpu.make_async_copy(a, b, sems.at[i]) for i, (a, b) in enumerate(loads)]
    for copy in loads:
        copy.start()
    tail = (index[7:8] - (base + TOKS)).astype(F32)
    head = (index[0:1] - base).astype(F32)
    rows[low_rows:UP_ROWS] = jnp.broadcast_to(tail, (16, CA)).astype(BF16)
    rows[UP_ROWS + high_rows :] = jnp.broadcast_to(head, (16, CA)).astype(BF16)
    for copy in loads:
        copy.wait()
    stores = (
        (rows.at[pl.ds(0, UP_ROWS)], up),
        (rows.at[pl.ds(UP_ROWS, DOWN_ROWS)], down),
        (heads.at[1 - core], send),
        (heads.at[core], joined.at[pl.ds(0, TOKS)]),
    )
    stores = [pltpu.make_async_copy(a, b, sems.at[4 + i]) for i, (a, b) in enumerate(stores)]
    for copy in stores:
        copy.start()
    for copy in stores:
        copy.wait()


def pack(place, feats, bias, index, pair_bias):
    return pl.pallas_call(
        pack_kernel,
        out_shape=(
            jax.ShapeDtypeStruct((UP_ROWS, CA), BF16),
            jax.ShapeDtypeStruct((DOWN_ROWS, CA), BF16),
            jax.ShapeDtypeStruct((TOKS, ALL_TOKS), BF16),
            jax.ShapeDtypeStruct((2 * TOKS, ALL_TOKS), BF16),
        ),
        in_specs=[pl.BlockSpec(memory_space=pltpu.SMEM)] + anywhere(2) + vmem(1) + anywhere(1),
        out_specs=tuple(anywhere(4)),
        scratch_shapes=[
            pltpu.VMEM((2, TOKS, ALL_TOKS), BF16),
            pltpu.VMEM((UP_ROWS + DOWN_ROWS, CA), BF16),
            pltpu.SemaphoreType.DMA((8,)),
        ],
        compiler_params=params(58),
        cost_estimate=SMALL,
        name="pack",
    )(place, feats, bias, index, pair_bias)


def join_kernel(joined, received, low, high, out, rows, sems):
    load = pltpu.make_async_copy(received, rows, sems.at[0])
    load.start()
    load.wait()
    store = pltpu.make_async_copy(rows, out.at[pl.ds(TOKS, TOKS)], sems.at[1])
    store.start()
    store.wait()


def join(joined, received, low, high):
    return pl.pallas_call(
        join_kernel,
        out_shape=jax.ShapeDtypeStruct(joined.shape, BF16),
        in_specs=anywhere(4),
        out_specs=anywhere(1)[0],
        input_output_aliases={0: 0},
        scratch_shapes=[pltpu.VMEM((TOKS, ALL_TOKS), BF16), pltpu.SemaphoreType.DMA((2,))],
        compiler_params=params(58),
        cost_estimate=SMALL,
        name="join",
    )(joined, received, low, high)


def hold_kernel(*refs):
    del refs


def hold(*arrays, cost=SMALL):
    return pl.pallas_call(
        hold_kernel,
        out_shape=tuple(jax.ShapeDtypeStruct(array.shape, array.dtype) for array in arrays),
        in_specs=anywhere(len(arrays)),
        out_specs=tuple(anywhere(len(arrays))),
        input_output_aliases={i: i for i in range(len(arrays))},
        compiler_params=params(58),
        cost_estimate=cost,
        name="hold",
    )(*arrays)


def encode_kernel(
    place, feats, low, high, bias, index, cond, project, mix, pool, fence,
    encoded, first, last, residual, normed, again,
    rows, bias32, packed, mixed, ext,
):
    rows[0 : 2 * LOWER] = low[0 : 2 * LOWER].astype(F32)
    rows[2 * LOWER : 2 * (LOWER + ATOMS)] = feats[...].astype(F32)
    rows[2 * (LOWER + ATOMS) : 2 * EXT] = high[0 : 2 * MARGIN].astype(F32)
    bias32[0 : 4 * QB] = low[2 * LOWER : 2 * LOWER + 4 * QB].astype(F32)
    bias32[4 * QB :] = bias[...].astype(F32)
    for seed in range(SEEDS):
        values = rows[pl.ds(seed, EXT, stride=2), :]
        packed[seed] = dot(layer_norm(values).astype(BF16), project[...]).astype(BF16)
    window_blocks(packed, bias32, mixed, 33, place[0] * ATOMS - QB - MARGIN, 11)
    token = lax.broadcasted_iota(jnp.int32, (TOKS, CA), 0)
    below = low[2 * LOWER + 4 * QB :].astype(F32)[0:1].astype(jnp.int32)
    below = jnp.where(place[0] == 0, -1000, below)
    base = place[0] * TOKS
    chosen = jnp.concatenate(
        [(index[i : i + 1] - base == token).astype(F32) for i in range(8)]
        + [(below == token).astype(F32)],
        axis=1,
    )
    counts = jnp.sum(chosen, axis=1, keepdims=True)
    chosen = chosen.astype(BF16)
    for seed in range(SEEDS):
        values = rows[pl.ds(2 * MARGIN + seed, QB + ATOMS, stride=2), :]
        result = (values + dot(mixed[seed], mix[...])).astype(BF16)
        ext[0:ATOMS] = result[QB:]
        ext[ATOMS : EXT - QB] = jnp.zeros((EXT - QB - ATOMS, CA), BF16)
        ext[EXT - QB :] = result[0:QB]
        encoded[seed] = ext[0:ATOMS]
        first[seed] = ext[0:MARGIN]
        last[seed] = ext[ATOMS - MARGIN : ATOMS]
        lifted = jnp.maximum(dot(ext[...], pool[...]), 0.0).astype(BF16)
        state = cond[...].astype(F32) + dot(chosen, lifted) / counts
        residual[seed] = state
        normed[seed] = layer_norm(state).astype(BF16)
        again[seed] = normed[seed]


def encode(*args):
    return pl.pallas_call(
        encode_kernel,
        out_shape=(
            jax.ShapeDtypeStruct((SEEDS, ATOMS, CA), BF16),
            jax.ShapeDtypeStruct((SEEDS, MARGIN, CA), BF16),
            jax.ShapeDtypeStruct((SEEDS, MARGIN, CA), BF16),
            jax.ShapeDtypeStruct((SEEDS, TOKS, CT), F32),
            jax.ShapeDtypeStruct((SEEDS, TOKS, CT), BF16),
            jax.ShapeDtypeStruct((SEEDS, TOKS, CT), BF16),
        ),
        in_specs=[pl.BlockSpec(memory_space=pltpu.SMEM)] + vmem(9) + anywhere(1),
        out_specs=tuple(vmem(6)),
        scratch_shapes=[
            pltpu.VMEM((2 * EXT, CA), F32),
            pltpu.VMEM((33 * 4 * QB, WIN), F32),
            pltpu.VMEM((SEEDS, EXT, 3 * CA), BF16),
            pltpu.VMEM((SEEDS, QB + ATOMS, CA), BF16),
            pltpu.VMEM((EXT, CA), BF16),
        ],
        compiler_params=params(58),
        cost_estimate=SMALL,
        name="encode",
    )(*args)


def decode_kernel(
    place, enc, enc_low, enc_high, spread, spread_low, spread_high, bias, index, low, high,
    project, mix,
    update,
    rows, bias32, packed, mixed, decoded, tokens, moved,
):
    bias32[...] = bias[...].astype(F32)
    token = lax.broadcasted_iota(jnp.int32, (TOKS + 2 * EDGE, CA), 0) - EDGE
    below = low[2 * LOWER + 4 * QB :].astype(F32)[0:1].astype(jnp.int32)
    above = high[2 * MARGIN :].astype(F32)[0:1].astype(jnp.int32) + TOKS
    base = place[0] * TOKS
    chosen = jnp.concatenate(
        [(index[i : i + 1] - base == token).astype(F32) for i in range(8)]
        + [(below == token).astype(F32), (above == token).astype(F32)],
        axis=1,
    ).astype(BF16)
    end = MARGIN + ATOMS
    for seed in range(SEEDS):
        tokens[0:EDGE] = spread_low[seed]
        tokens[EDGE : EDGE + TOKS] = spread[seed]
        tokens[EDGE + TOKS :] = spread_high[seed]
        moved[...] = lax.dot_general(
            chosen, tokens[...], (((0,), (0,)), ((), ())), preferred_element_type=F32
        )
        decoded[0:MARGIN] = enc_low[seed].astype(F32) + moved[ATOMS + CA - MARGIN : ATOMS + CA]
        decoded[MARGIN:end] = enc[seed].astype(F32) + moved[0:ATOMS]
        decoded[end : end + MARGIN] = (
            enc_high[seed].astype(F32) + moved[ATOMS + CA : ATOMS + CA + MARGIN]
        )
        decoded[end + MARGIN :] = jnp.zeros((EXT - end - MARGIN, CA), F32)
        values = decoded[...].astype(BF16).astype(F32)
        rows[pl.ds(seed, EXT, stride=2), :] = values
        packed[seed] = dot(layer_norm(values).astype(BF16), project[...]).astype(BF16)
    window_blocks(packed, bias32, mixed, 32, place[0] * ATOMS - MARGIN, 8)
    for seed in range(SEEDS):
        at = pl.ds(2 * MARGIN + seed, ATOMS, stride=2)
        rows[at, :] = rows[at, :] + dot(mixed[seed], mix[...])
    update[...] = rows[2 * MARGIN : 2 * (MARGIN + ATOMS)].astype(BF16)


def decode(*args):
    return pl.pallas_call(
        decode_kernel,
        out_shape=jax.ShapeDtypeStruct((SEEDS * ATOMS, CA), BF16),
        in_specs=[pl.BlockSpec(memory_space=pltpu.SMEM)] + vmem(12),
        out_specs=vmem(1)[0],
        scratch_shapes=[
            pltpu.VMEM((2 * EXT, CA), F32),
            pltpu.VMEM((32 * 4 * QB, WIN), F32),
            pltpu.VMEM((SEEDS, EXT, 3 * CA), BF16),
            pltpu.VMEM((SEEDS, ATOMS, CA), BF16),
            pltpu.VMEM((EXT, CA), F32),
            pltpu.VMEM((TOKS + 2 * EDGE, CA), BF16),
            pltpu.VMEM((ATOMS + 2 * CA, CA), F32),
        ],
        compiler_params=params(58),
        cost_estimate=SMALL,
        name="decode",
    )(*args)


def spaced_kernel(place, first, second, fence, out):
    core = place[1]
    for group in range(4):
        start = PAIR * group // 128 * 128
        shift = PAIR * group - start + HEAD * core
        width = min(256, 384 - start)
        row = lax.broadcasted_iota(jnp.int32, (width, 128), 0) - shift
        lane = lax.broadcasted_iota(jnp.int32, (width, 128), 1)

        def pick(side):
            at = lane - HEAD * side
            return ((row == at) & (at >= 0) & (at < HEAD)).astype(F32).astype(BF16)

        block = dot(first[:, start : start + width], pick(1 - core)) + dot(
            second[:, start : start + width], pick(core)
        )
        out[0, group // 2, :, group % 2 * 128 : group % 2 * 128 + 128] = block.astype(BF16)


def spaced(place, weight, fence):
    return pl.pallas_call(
        spaced_kernel,
        grid=(4,),
        out_shape=jax.ShapeDtypeStruct((2, GROUPS // 2, CT, 256), BF16),
        in_specs=[
            pl.BlockSpec(memory_space=pltpu.SMEM),
            pl.BlockSpec((CT, 384), lambda i: (0, i)),
            pl.BlockSpec((CT, 384), lambda i: (0, jnp.where(i < 2, 6 + i, 2 + i))),
        ]
        + anywhere(1),
        out_specs=pl.BlockSpec((1, 2, CT, 256), lambda i: (i // 2, i % 2, 0, 0)),
        compiler_params=params(58),
        cost_estimate=LARGE,
        name="spaced",
    )(place, weight, weight, fence)


def queries_kernel(place, normed, other, weight, fence, query, gate):
    core = place[1]
    lane = lax.broadcasted_iota(jnp.int32, (1, 128), 1)
    in_query = (lane // HEAD == 1 - core) & (lane < PAIR)
    in_gate = (lane // HEAD == core) & (lane < PAIR)
    values = jnp.concatenate([normed[0], other[0], normed[1], other[1]], axis=0)
    for pair in range(GROUPS // 2):
        product = dot(values, weight[0, pair])
        for side in range(2):
            part = product[:, side * 128 : side * 128 + 128]
            group = 2 * pair + side
            queried = jnp.where(in_query, part * (HEAD**-0.5), 0.0).astype(BF16)
            opened = jnp.where(in_gate, jax.nn.sigmoid(part), 0.0)
            for seed in range(SEEDS):
                at = slice(seed * 2 * TOKS, (seed + 1) * 2 * TOKS)
                query[group, seed] = queried[at]
                gate[group, seed] = opened[at]


def queries(place, normed, other, weight, fence):
    return pl.pallas_call(
        queries_kernel,
        grid=(1,),
        out_shape=(
            jax.ShapeDtypeStruct((GROUPS, SEEDS, 2 * TOKS, 128), BF16),
            jax.ShapeDtypeStruct((GROUPS, SEEDS, 2 * TOKS, 128), F32),
        ),
        in_specs=[pl.BlockSpec(memory_space=pltpu.SMEM)]
        + vmem(2)
        + [pl.BlockSpec((1, GROUPS // 2, CT, 256), lambda i: (0, 0, 0, 0))]
        + anywhere(1),
        out_specs=tuple(vmem(2)),
        compiler_params=params(50),
        cost_estimate=SMALL,
        name="queries",
    )(place, normed, other, weight, fence)


def stack_kernel(*refs):
    for i, ref in enumerate(refs[:-1]):
        refs[-1][i] = ref[...]


def stack(*chunks):
    return pl.pallas_call(
        stack_kernel,
        out_shape=jax.ShapeDtypeStruct((len(chunks),) + chunks[0].shape, BF16),
        in_specs=vmem(len(chunks)),
        out_specs=vmem(1)[0],
        compiler_params=params(50),
        cost_estimate=SMALL,
        name="stack",
    )(*chunks)


def keys_kernel(place, own, received, weight, *rest):
    out, tiles, sems = rest[-3:]
    chunks = [ref.at[i] for ref in (own, received) for i in range(ref.shape[0])]
    values = jnp.concatenate([chunk[...].reshape(SEEDS * TOKS, CT) for chunk in chunks], axis=0)
    ones = (lax.broadcasted_iota(jnp.int32, (1, 256), 1) % 128 == PAIR).astype(F32)
    copies = []
    for pair in range(GROUPS // 2):
        product = (dot(values, weight[0, pair]) + ones).astype(BF16)
        for i in range(len(chunks)):
            for side in range(2):
                for seed in range(SEEDS):
                    start = (i * SEEDS + seed) * TOKS
                    tiles[i, 2 * pair + side, seed] = product[
                        start : start + TOKS, side * 128 : side * 128 + 128
                    ]
            rows = pl.ds(pl.multiple_of(place[2 + i] * TOKS, TOKS), TOKS)
            copies.append(
                pltpu.make_async_copy(
                    tiles.at[i, pl.ds(2 * pair, 2)],
                    out.at[pl.ds(2 * pair, 2), :, rows],
                    sems.at[pair, i],
                )
            )
            copies[-1].start()
    for copy in copies:
        copy.wait()


def keys(place, ids, own, received, weight, before=None, fences=()):
    more = ([] if before is None else [before]) + list(fences)
    count = own.shape[0] + received.shape[0]
    return pl.pallas_call(
        keys_kernel,
        grid=(1,),
        out_shape=jax.ShapeDtypeStruct((GROUPS, SEEDS, ALL_TOKS, 128), BF16),
        in_specs=[pl.BlockSpec(memory_space=pltpu.SMEM)]
        + vmem(2)
        + [pl.BlockSpec((1, GROUPS // 2, CT, 256), lambda i: (1, 0, 0, 0))]
        + anywhere(len(more)),
        out_specs=anywhere(1)[0],
        scratch_shapes=[
            pltpu.VMEM((count, GROUPS, SEEDS, TOKS, 128), BF16),
            pltpu.SemaphoreType.DMA((GROUPS // 2, count)),
        ],
        input_output_aliases={} if before is None else {4: 0},
        compiler_params=params(50),
        cost_estimate=SMALL,
        name="keys",
    )(jnp.concatenate([place, ids]), own, received, weight, *more)


def attend_kernel(count, extra, group_ids, query, gate, key_value, *rest):
    biases = rest[:count]
    own, sent, slots, scores, sems = rest[count + extra :]
    step = pl.program_id(0)

    def load(i):
        return pltpu.make_async_copy(biases[i], slots.at[i % 2], sems.at[i % 2])

    for i in range(count):

        @pl.when(step == i)
        def _(i=i):
            if i == 0:
                load(0).start()
            if i + 1 < count:
                load(i + 1).start()
            load(i).wait()

    bias = slots.at[step % 2]
    width = 512
    tops = []
    for seed in range(SEEDS):
        peak = None
        for c in range(ALL_TOKS // width):
            cols = slice(c * width, (c + 1) * width)
            part = dot_t(query[0, seed], key_value[0, seed, cols, :]) + bias[:, cols].astype(F32)
            scores[seed, :, cols] = part
            for w in range(width // 128):
                tile = part[:, w * 128 : (w + 1) * 128]
                peak = tile if peak is None else jnp.maximum(peak, tile)
        tops.append(jnp.max(peak, axis=-1, keepdims=True))
    for seed in range(SEEDS):
        total = None
        for c in range(ALL_TOKS // width):
            cols = slice(c * width, (c + 1) * width)
            part = dot(
                jnp.exp(scores[seed, :, cols] - tops[seed]).astype(BF16), key_value[0, seed, cols, :]
            )
            total = part if total is None else total + part
        gated = (total / total[:, PAIR : PAIR + 1] * gate[0, seed]).astype(BF16)
        own[0, seed] = gated[:TOKS]
        sent[0, seed] = gated[TOKS:]


def attend(group_ids, query, gate, key_value, before, biases):
    count = len(biases)
    shape = jax.ShapeDtypeStruct((GROUPS, SEEDS, TOKS, 128), BF16)

    def by_group(*block):
        return pl.BlockSpec((1,) + block, lambda i, ids: (ids[i],) + (0,) * len(block))

    grid_spec = pltpu.PrefetchScalarGridSpec(
        num_scalar_prefetch=1,
        grid=(count,),
        in_specs=[
            by_group(SEEDS, 2 * TOKS, 128),
            by_group(SEEDS, 2 * TOKS, 128),
            by_group(SEEDS, ALL_TOKS, 128),
        ]
        + anywhere(count + len(before)),
        out_specs=(by_group(SEEDS, TOKS, 128),) * 2,
        scratch_shapes=[
            pltpu.VMEM((2, 2 * TOKS, ALL_TOKS), BF16),
            pltpu.VMEM((SEEDS, 2 * TOKS, ALL_TOKS), F32),
            pltpu.SemaphoreType.DMA((2,)),
        ],
    )
    return pl.pallas_call(
        functools.partial(attend_kernel, count, len(before)),
        grid_spec=grid_spec,
        out_shape=(shape, shape),
        input_output_aliases={4 + count + i: i for i in range(len(before))},
        compiler_params=params(50),
        cost_estimate=SMALL,
        name="attend",
    )(group_ids, query, gate, key_value, *biases, *before)


def finish_kernel(
    residual, own, received, mix, wide_hbm, narrow_hbm, spread_weight,
    state, spread, first, last,
    wide, narrow, mix_tile, total, hidden, sems,
):
    step = 512
    count = TRANS // step
    copies = []
    for c in range(count):
        gate_cols = pl.ds(c * step, step)
        up_cols = pl.ds(TRANS + c * step, step)
        copies.append(
            [
                pltpu.make_async_copy(wide_hbm.at[:, gate_cols], wide.at[:, gate_cols], sems.at[c, 0]),
                pltpu.make_async_copy(wide_hbm.at[:, up_cols], wide.at[:, up_cols], sems.at[c, 1]),
                pltpu.make_async_copy(narrow_hbm.at[gate_cols], narrow.at[gate_cols], sems.at[c, 2]),
            ]
        )
    for group in copies:
        for copy in group:
            copy.start()
    values = residual[...].reshape(SEEDS * TOKS, CT)
    for group in range(GROUPS):
        gated = (own[group] + received[group]).reshape(SEEDS * TOKS, 128)
        mix_tile[group, 0:PAIR] = mix[group]
        mix_tile[group, PAIR:128] = jnp.zeros((128 - PAIR, CT), BF16)
        values = values + dot(gated, mix_tile[group])
    total[...] = values
    normed = layer_norm(values).astype(BF16)
    for c in range(count):
        for copy in copies[c]:
            copy.wait()
        gate = dot(normed, wide[:, c * step : (c + 1) * step])
        up = dot(normed, wide[:, TRANS + c * step : TRANS + (c + 1) * step])
        hidden[:, c * step : (c + 1) * step] = (jax.nn.silu(gate) * up).astype(BF16)
    rounded = (total[...] + dot(hidden[...], narrow[...])).astype(BF16)
    state[...] = rounded.reshape(SEEDS, TOKS, CT)
    carried = dot(rounded, spread_weight[...]).astype(BF16).reshape(SEEDS, TOKS, CA)
    spread[...] = carried
    first[...] = carried[:, :EDGE]
    last[...] = carried[:, TOKS - EDGE :]


def finish(residual, own, received, mix, wide, narrow, spread_weight):
    return pl.pallas_call(
        finish_kernel,
        out_shape=(
            jax.ShapeDtypeStruct((SEEDS, TOKS, CT), BF16),
            jax.ShapeDtypeStruct((SEEDS, TOKS, CA), BF16),
            jax.ShapeDtypeStruct((SEEDS, EDGE, CA), BF16),
            jax.ShapeDtypeStruct((SEEDS, EDGE, CA), BF16),
        ),
        in_specs=vmem(4) + anywhere(2) + vmem(1),
        out_specs=tuple(vmem(4)),
        scratch_shapes=[
            pltpu.VMEM((CT, 2 * TRANS), BF16),
            pltpu.VMEM((TRANS, CT), BF16),
            pltpu.VMEM((GROUPS, 128, CT), BF16),
            pltpu.VMEM((SEEDS * TOKS, CT), F32),
            pltpu.VMEM((SEEDS * TOKS, TRANS), BF16),
            pltpu.SemaphoreType.DMA((3, 3)),
        ],
        compiler_params=params(58),
        cost_estimate=SMALL,
        name="finish",
    )(residual, own, received, mix, wide, narrow, spread_weight)


def along_tok(values, by):
    return lax.ppermute(values, "tok", [(i, (i + by) % 16) for i in range(16)])


def across_core(values):
    return lax.ppermute(values, "tok", [(i, i ^ 1) for i in range(16)])


def along_x(values, by):
    return lax.ppermute(values, "tok", [(i, i // 8 * 8 + (i + 2 * by) % 8) for i in range(16)])


def across_floor(values):
    return lax.ppermute(values, "tok", [(i, i ^ 8) for i in range(16)])


def along_y(values, by):
    return lax.ppermute(values, "seed", [(i, (i + 2 * by) % 8) for i in range(8)])


def along_z(values):
    return lax.ppermute(values, "seed", [(i, i ^ 1) for i in range(8)])


def per_device(
    atom_feats, atom_index, token_cond, pair_bias, atom_bias_enc, atom_bias_dec,
    enc_project, enc_mix, pool_weight, token_project, token_mix, swiglu_in, swiglu_out,
    spread_weight, dec_project, dec_mix,
):
    tok = lax.axis_index("tok")
    seed = lax.axis_index("seed")
    place = jnp.stack([tok, tok % 2]).astype(jnp.int32)
    feats = atom_feats.reshape(SEEDS * ATOMS, CA)
    bias_enc = atom_bias_enc.reshape(4 * ATOMS, WIN)
    bias_dec = atom_bias_dec.reshape(4 * ATOMS, WIN)
    index = atom_index.reshape(8, CA)

    up, down, send, joined = pack(place, feats, bias_enc, index, pair_bias)
    low = along_tok(up, 1)
    high = along_tok(down, -1)
    mine = join(joined, across_core(send), low, high)
    below = along_y(mine, 1)
    above = along_y(mine, -1)
    other = along_z(mine)

    encoded, first, last, residual, normed, again = encode(
        place, feats, low, high, bias_enc, index, token_cond, enc_project, enc_mix, pool_weight,
        mine,
    )
    x_below = along_x(normed, 1)
    x_above = along_x(normed, -1)
    below, above, other, first, last, again, mine = hold(
        below, above, other, first, last, again, mine
    )
    far = along_y(mine, 2)
    z_own = across_floor(again)
    mate = across_core(again)
    x_far = along_x(again, 2)
    weights = spaced(place, token_project, below)
    z_own, x_below, x_above, x_far, weights = hold(z_own, x_below, x_above, x_far, weights)
    z_below = along_x(z_own, 1)
    z_above = along_x(z_own, -1)
    z_far = across_floor(x_far)
    near = stack(again, x_below, x_above, z_own)
    near_mate = across_core(near)
    query, gate = queries(place, again, mate, weights, z_own)
    enc_low = along_tok(last, 1)
    enc_high = along_tok(first, -1)
    far, other, z_below, z_above, query = hold(far, other, z_below, z_above, query)
    other_below = along_y(other, 1)
    other_above = along_y(other, -1)
    other_far = along_z(far)
    rest = stack(x_far, z_below, z_above, z_far)
    rest_mate = across_core(rest)

    column, floor, core = tok // 2 % 4, tok // 8, tok % 2

    def shards(*offsets):
        return jnp.stack(
            [
                (floor ^ dz) * 8 + (column + dx) % 4 * 2 + (core ^ side)
                for side in (0, 1)
                for dx, dz in offsets
            ]
        ).astype(jnp.int32)

    key_value = keys(
        place, shards((0, 0), (3, 0), (1, 0), (0, 1)), near, near_mate, weights
    )
    key_value = keys(
        place, shards((2, 0), (3, 1), (1, 1), (2, 1)), rest, rest_mate, weights, key_value,
        (enc_low, enc_high),
    )

    level, side = seed // 2, seed % 2

    def ids(*offsets):
        return jnp.stack([(level + dy) % 4 * 2 + (side ^ dz) for dy, dz in offsets]).astype(jnp.int32)

    done = attend(
        ids((0, 0), (3, 0), (1, 0), (2, 0), (0, 1)), query, gate, key_value, (),
        (mine, below, above, far, other),
    )
    own, sent = attend(
        ids((3, 1), (1, 1), (2, 1)), query, gate, key_value, done,
        (other_below, other_above, other_far),
    )

    state, spread, spread_first, spread_last = finish(
        residual, own, across_core(sent), token_mix.reshape(GROUPS, PAIR, CT), swiglu_in,
        swiglu_out, spread_weight,
    )
    update = decode(
        place, encoded, enc_low, enc_high, spread, along_tok(spread_last, 1),
        along_tok(spread_first, -1), bias_dec, index, low, high, dec_project, dec_mix,
    )
    return state.transpose(1, 0, 2), update.reshape(ATOMS, SEEDS, CA)


def solution(mesh):
    placed = (
        P("tok", "seed", None),
        P("tok"),
        P("tok", None),
        P("seed", "tok", None),
        P("tok", None, None),
        P("tok", None, None),
    ) + (P(),) * 10
    return jax.shard_map(
        per_device,
        mesh=mesh,
        in_specs=placed,
        out_specs=(P("tok", "seed", None), P("tok", "seed", None)),
        check_vma=False,
    )
```

```python
import functools

import jax
import jax.numpy as jnp
from jax import lax
from jax.experimental import pallas as pl
from jax.experimental.pallas import tpu as pltpu
from jax.sharding import PartitionSpec as P

EPS = 1e-05
NEG = -1000000000.0
F32 = jnp.float32
BF16 = jnp.bfloat16

SEEDS = 2
ATOMS = 1024
TOKS = 128
CA = 128
CT = 768
HEADS = 16
HEAD = 48
PAIR = 96
GROUPS = 8
QB = 32
WIN = 128
MARGIN = 48
LOWER = 80
EXT = 1152
EDGE = 16
TRANS = 1536
ALL_TOKS = 2048
ALL_ATOMS = 16384
UP_ROWS = 2 * LOWER + 4 * QB + 16
DOWN_ROWS = 2 * MARGIN + 16


SMALL = pl.CostEstimate(flops=10**6, bytes_accessed=10**4, transcendentals=0)
LARGE = pl.CostEstimate(flops=7 * 10**10, bytes_accessed=10**4, transcendentals=0)


def params(limit_mb, **more):
    return pltpu.CompilerParams(vmem_limit_bytes=limit_mb * 1024 * 1024, **more)


def vmem(n):
    return [pl.BlockSpec(memory_space=pltpu.VMEM)] * n


def anywhere(n):
    return [pl.BlockSpec(memory_space=pltpu.HBM)] * n


def layer_norm(values):
    centre = values - jnp.mean(values, axis=-1, keepdims=True)
    variance = jnp.mean(centre * centre, axis=-1, keepdims=True)
    return centre * lax.rsqrt(variance + EPS)


def dot(a, b):
    return jnp.dot(a, b, preferred_element_type=F32)


def dot_t(a, b):
    return lax.dot_general(a, b, (((1,), (1,)), ((), ())), preferred_element_type=F32)


def window_blocks(packed, bias, mixed, blocks, first_atom, unroll):
    lane_head = lax.broadcasted_iota(jnp.int32, (QB, CA), 1) // 32
    head_mask = [(lane_head == h).astype(BF16) for h in range(4)]
    lane = lax.broadcasted_iota(jnp.int32, (1, WIN), 1)
    ones = jnp.ones((WIN, CA), BF16)
    for b in (0, 1, 2, blocks - 2, blocks - 1):
        position = lane + (first_atom + b * QB)
        inside = (position >= 0) & (position < ALL_ATOMS)
        place = slice(b * 4 * QB, (b + 1) * 4 * QB)
        bias[place] = jnp.where(inside, bias[place], NEG)

    def body(i, carry):
        work = []
        for u in range(unroll):
            b = i * unroll + u
            rows = pl.multiple_of(b * QB, QB)
            query_rows = pl.multiple_of(b * QB + MARGIN, 16)
            bias_rows = pl.multiple_of(b * 4 * QB, 4 * QB)
            added = jnp.concatenate(
                [bias[pl.ds(bias_rows + h, QB, stride=4), :] for h in range(4)], axis=0
            )
            for seed in range(SEEDS):
                work.append((rows, query_rows, added, seed))
        scores = []
        for rows, query_rows, added, seed in work:
            query = packed[seed, pl.ds(query_rows, QB), 0:CA]
            key = packed[seed, pl.ds(rows, WIN), CA : 2 * CA]
            stacked = jnp.concatenate([query * head_mask[h] for h in range(4)], axis=0)
            scores.append(dot_t(stacked, key) * (32**-0.5) + added)
        weights = [jnp.exp(s - jnp.max(s, axis=-1, keepdims=True)).astype(BF16) for s in scores]
        for (rows, _, _, seed), w in zip(work, weights):
            value = jnp.concatenate([packed[seed, pl.ds(rows, WIN), 2 * CA : 3 * CA], ones], axis=1)
            out = dot(w, value)
            joined = out[3 * QB :]
            for h in range(3):
                joined = jnp.where(jnp.concatenate([lane_head, lane_head], axis=1) == h, out[h * QB : (h + 1) * QB], joined)
            mixed[seed, pl.ds(rows, QB), :] = (joined[:, :CA] / joined[:, CA:]).astype(BF16)
        return carry

    lax.fori_loop(0, blocks // unroll, body, 0)


def pack_kernel(place, feats, bias, index, pair_bias, up, down, send, joined, heads, rows, sems):
    base, core = place[0] * TOKS, place[1]
    low_rows, high_rows = UP_ROWS - 16, DOWN_ROWS - 16
    loads = (
        (pair_bias, heads),
        (feats.at[pl.ds(2 * (ATOMS - LOWER), 2 * LOWER)], rows.at[pl.ds(0, 2 * LOWER)]),
        (bias.at[pl.ds(4 * (ATOMS - QB), 4 * QB)], rows.at[pl.ds(2 * LOWER, 4 * QB)]),
        (feats.at[pl.ds(0, 2 * MARGIN)], rows.at[pl.ds(UP_ROWS, 2 * MARGIN)]),
    )
    loads = [pltpu.make_async_copy(a, b, sems.at[i]) for i, (a, b) in enumerate(loads)]
    for copy in loads:
        copy.start()
    tail = (index[7:8] - (base + TOKS)).astype(F32)
    head = (index[0:1] - base).astype(F32)
    rows[low_rows:UP_ROWS] = jnp.broadcast_to(tail, (16, CA)).astype(BF16)
    rows[UP_ROWS + high_rows :] = jnp.broadcast_to(head, (16, CA)).astype(BF16)
    for copy in loads:
        copy.wait()
    stores = (
        (rows.at[pl.ds(0, UP_ROWS)], up),
        (rows.at[pl.ds(UP_ROWS, DOWN_ROWS)], down),
        (heads.at[1 - core], send),
        (heads.at[core], joined.at[pl.ds(0, TOKS)]),
    )
    stores = [pltpu.make_async_copy(a, b, sems.at[4 + i]) for i, (a, b) in enumerate(stores)]
    for copy in stores:
        copy.start()
    for copy in stores:
        copy.wait()


def pack(place, feats, bias, index, pair_bias):
    return pl.pallas_call(
        pack_kernel,
        out_shape=(
            jax.ShapeDtypeStruct((UP_ROWS, CA), BF16),
            jax.ShapeDtypeStruct((DOWN_ROWS, CA), BF16),
            jax.ShapeDtypeStruct((TOKS, ALL_TOKS), BF16),
            jax.ShapeDtypeStruct((2 * TOKS, ALL_TOKS), BF16),
        ),
        in_specs=[pl.BlockSpec(memory_space=pltpu.SMEM)] + anywhere(2) + vmem(1) + anywhere(1),
        out_specs=tuple(anywhere(4)),
        scratch_shapes=[
            pltpu.VMEM((2, TOKS, ALL_TOKS), BF16),
            pltpu.VMEM((UP_ROWS + DOWN_ROWS, CA), BF16),
            pltpu.SemaphoreType.DMA((8,)),
        ],
        compiler_params=params(58),
        cost_estimate=SMALL,
        name="pack",
    )(place, feats, bias, index, pair_bias)


def join_kernel(joined, received, low, high, out, rows, sems):
    load = pltpu.make_async_copy(received, rows, sems.at[0])
    load.start()
    load.wait()
    store = pltpu.make_async_copy(rows, out.at[pl.ds(TOKS, TOKS)], sems.at[1])
    store.start()
    store.wait()


def join(joined, received, low, high):
    return pl.pallas_call(
        join_kernel,
        out_shape=jax.ShapeDtypeStruct(joined.shape, BF16),
        in_specs=anywhere(4),
        out_specs=anywhere(1)[0],
        input_output_aliases={0: 0},
        scratch_shapes=[pltpu.VMEM((TOKS, ALL_TOKS), BF16), pltpu.SemaphoreType.DMA((2,))],
        compiler_params=params(58),
        cost_estimate=SMALL,
        name="join",
    )(joined, received, low, high)


def hold_kernel(*refs):
    del refs


def hold(*arrays, cost=SMALL):
    return pl.pallas_call(
        hold_kernel,
        out_shape=tuple(jax.ShapeDtypeStruct(array.shape, array.dtype) for array in arrays),
        in_specs=anywhere(len(arrays)),
        out_specs=tuple(anywhere(len(arrays))),
        input_output_aliases={i: i for i in range(len(arrays))},
        compiler_params=params(58),
        cost_estimate=cost,
        name="hold",
    )(*arrays)


def encode_kernel(
    place, feats, low, high, bias, index, cond, project, mix, pool, fence,
    encoded, first, last, residual, normed, again,
    rows, bias32, packed, mixed, ext,
):
    rows[0 : 2 * LOWER] = low[0 : 2 * LOWER].astype(F32)
    rows[2 * LOWER : 2 * (LOWER + ATOMS)] = feats[...].astype(F32)
    rows[2 * (LOWER + ATOMS) : 2 * EXT] = high[0 : 2 * MARGIN].astype(F32)
    bias32[0 : 4 * QB] = low[2 * LOWER : 2 * LOWER + 4 * QB].astype(F32)
    bias32[4 * QB :] = bias[...].astype(F32)
    for seed in range(SEEDS):
        values = rows[pl.ds(seed, EXT, stride=2), :]
        packed[seed] = dot(layer_norm(values).astype(BF16), project[...]).astype(BF16)
    window_blocks(packed, bias32, mixed, 33, place[0] * ATOMS - QB - MARGIN, 11)
    token = lax.broadcasted_iota(jnp.int32, (TOKS, CA), 0)
    below = low[2 * LOWER + 4 * QB :].astype(F32)[0:1].astype(jnp.int32)
    below = jnp.where(place[0] == 0, -1000, below)
    base = place[0] * TOKS
    chosen = jnp.concatenate(
        [(index[i : i + 1] - base == token).astype(F32) for i in range(8)]
        + [(below == token).astype(F32)],
        axis=1,
    )
    counts = jnp.sum(chosen, axis=1, keepdims=True)
    chosen = chosen.astype(BF16)
    for seed in range(SEEDS):
        values = rows[pl.ds(2 * MARGIN + seed, QB + ATOMS, stride=2), :]
        result = (values + dot(mixed[seed], mix[...])).astype(BF16)
        ext[0:ATOMS] = result[QB:]
        ext[ATOMS : EXT - QB] = jnp.zeros((EXT - QB - ATOMS, CA), BF16)
        ext[EXT - QB :] = result[0:QB]
        encoded[seed] = ext[0:ATOMS]
        first[seed] = ext[0:MARGIN]
        last[seed] = ext[ATOMS - MARGIN : ATOMS]
        lifted = jnp.maximum(dot(ext[...], pool[...]), 0.0).astype(BF16)
        state = cond[...].astype(F32) + dot(chosen, lifted) / counts
        residual[seed] = state
        normed[seed] = layer_norm(state).astype(BF16)
        again[seed] = normed[seed]


def encode(*args):
    return pl.pallas_call(
        encode_kernel,
        out_shape=(
            jax.ShapeDtypeStruct((SEEDS, ATOMS, CA), BF16),
            jax.ShapeDtypeStruct((SEEDS, MARGIN, CA), BF16),
            jax.ShapeDtypeStruct((SEEDS, MARGIN, CA), BF16),
            jax.ShapeDtypeStruct((SEEDS, TOKS, CT), F32),
            jax.ShapeDtypeStruct((SEEDS, TOKS, CT), BF16),
            jax.ShapeDtypeStruct((SEEDS, TOKS, CT), BF16),
        ),
        in_specs=[pl.BlockSpec(memory_space=pltpu.SMEM)] + vmem(9) + anywhere(1),
        out_specs=tuple(vmem(6)),
        scratch_shapes=[
            pltpu.VMEM((2 * EXT, CA), F32),
            pltpu.VMEM((33 * 4 * QB, WIN), F32),
            pltpu.VMEM((SEEDS, EXT, 3 * CA), BF16),
            pltpu.VMEM((SEEDS, QB + ATOMS, CA), BF16),
            pltpu.VMEM((EXT, CA), BF16),
        ],
        compiler_params=params(58),
        cost_estimate=SMALL,
        name="encode",
    )(*args)


def decode_kernel(
    place, enc, enc_low, enc_high, spread, spread_low, spread_high, bias, index, low, high,
    project, mix,
    update,
    rows, bias32, packed, mixed, decoded, tokens, moved,
):
    bias32[...] = bias[...].astype(F32)
    token = lax.broadcasted_iota(jnp.int32, (TOKS + 2 * EDGE, CA), 0) - EDGE
    below = low[2 * LOWER + 4 * QB :].astype(F32)[0:1].astype(jnp.int32)
    above = high[2 * MARGIN :].astype(F32)[0:1].astype(jnp.int32) + TOKS
    base = place[0] * TOKS
    chosen = jnp.concatenate(
        [(index[i : i + 1] - base == token).astype(F32) for i in range(8)]
        + [(below == token).astype(F32), (above == token).astype(F32)],
        axis=1,
    ).astype(BF16)
    end = MARGIN + ATOMS
    for seed in range(SEEDS):
        tokens[0:EDGE] = spread_low[seed]
        tokens[EDGE : EDGE + TOKS] = spread[seed]
        tokens[EDGE + TOKS :] = spread_high[seed]
        moved[...] = lax.dot_general(
            chosen, tokens[...], (((0,), (0,)), ((), ())), preferred_element_type=F32
        )
        decoded[0:MARGIN] = enc_low[seed].astype(F32) + moved[ATOMS + CA - MARGIN : ATOMS + CA]
        decoded[MARGIN:end] = enc[seed].astype(F32) + moved[0:ATOMS]
        decoded[end : end + MARGIN] = (
            enc_high[seed].astype(F32) + moved[ATOMS + CA : ATOMS + CA + MARGIN]
        )
        decoded[end + MARGIN :] = jnp.zeros((EXT - end - MARGIN, CA), F32)
        values = decoded[...].astype(BF16).astype(F32)
        rows[pl.ds(seed, EXT, stride=2), :] = values
        packed[seed] = dot(layer_norm(values).astype(BF16), project[...]).astype(BF16)
    window_blocks(packed, bias32, mixed, 32, place[0] * ATOMS - MARGIN, 8)
    for seed in range(SEEDS):
        at = pl.ds(2 * MARGIN + seed, ATOMS, stride=2)
        rows[at, :] = rows[at, :] + dot(mixed[seed], mix[...])
    update[...] = rows[2 * MARGIN : 2 * (MARGIN + ATOMS)].astype(BF16)


def decode(*args):
    return pl.pallas_call(
        decode_kernel,
        out_shape=jax.ShapeDtypeStruct((SEEDS * ATOMS, CA), BF16),
        in_specs=[pl.BlockSpec(memory_space=pltpu.SMEM)] + vmem(12),
        out_specs=vmem(1)[0],
        scratch_shapes=[
            pltpu.VMEM((2 * EXT, CA), F32),
            pltpu.VMEM((32 * 4 * QB, WIN), F32),
            pltpu.VMEM((SEEDS, EXT, 3 * CA), BF16),
            pltpu.VMEM((SEEDS, ATOMS, CA), BF16),
            pltpu.VMEM((EXT, CA), F32),
            pltpu.VMEM((TOKS + 2 * EDGE, CA), BF16),
            pltpu.VMEM((ATOMS + 2 * CA, CA), F32),
        ],
        compiler_params=params(30),
        cost_estimate=SMALL,
        name="decode",
    )(*args)


def spaced_kernel(place, first, second, fence, out):
    core = place[1]
    for group in range(4):
        start = PAIR * group // 128 * 128
        shift = PAIR * group - start + HEAD * core
        width = min(256, 384 - start)
        row = lax.broadcasted_iota(jnp.int32, (width, 128), 0) - shift
        lane = lax.broadcasted_iota(jnp.int32, (width, 128), 1)

        def pick(side):
            at = lane - HEAD * side
            return ((row == at) & (at >= 0) & (at < HEAD)).astype(F32).astype(BF16)

        block = dot(first[:, start : start + width], pick(1 - core)) + dot(
            second[:, start : start + width], pick(core)
        )
        out[0, group // 2, :, group % 2 * 128 : group % 2 * 128 + 128] = block.astype(BF16)


def spaced(place, weight, fence):
    return pl.pallas_call(
        spaced_kernel,
        grid=(4,),
        out_shape=jax.ShapeDtypeStruct((2, GROUPS // 2, CT, 256), BF16),
        in_specs=[
            pl.BlockSpec(memory_space=pltpu.SMEM),
            pl.BlockSpec((CT, 384), lambda i: (0, i)),
            pl.BlockSpec((CT, 384), lambda i: (0, jnp.where(i < 2, 6 + i, 2 + i))),
        ]
        + anywhere(1),
        out_specs=pl.BlockSpec((1, 2, CT, 256), lambda i: (i // 2, i % 2, 0, 0)),
        compiler_params=params(58),
        cost_estimate=LARGE,
        name="spaced",
    )(place, weight, weight, fence)


def queries_kernel(place, normed, other, weight, fence, query, gate):
    core = place[1]
    lane = lax.broadcasted_iota(jnp.int32, (1, 128), 1)
    in_query = (lane // HEAD == 1 - core) & (lane < PAIR)
    in_gate = (lane // HEAD == core) & (lane < PAIR)
    values = jnp.concatenate([normed[0], other[0], normed[1], other[1]], axis=0)
    for pair in range(GROUPS // 2):
        product = dot(values, weight[0, pair])
        for side in range(2):
            part = product[:, side * 128 : side * 128 + 128]
            group = 2 * pair + side
            queried = jnp.where(in_query, part * (HEAD**-0.5), 0.0).astype(BF16)
            opened = jnp.where(in_gate, jax.nn.sigmoid(part), 0.0)
            for seed in range(SEEDS):
                at = slice(seed * 2 * TOKS, (seed + 1) * 2 * TOKS)
                query[group, seed] = queried[at]
                gate[group, seed] = opened[at]


def queries(place, normed, other, weight, fence):
    return pl.pallas_call(
        queries_kernel,
        grid=(1,),
        out_shape=(
            jax.ShapeDtypeStruct((GROUPS, SEEDS, 2 * TOKS, 128), BF16),
            jax.ShapeDtypeStruct((GROUPS, SEEDS, 2 * TOKS, 128), F32),
        ),
        in_specs=[pl.BlockSpec(memory_space=pltpu.SMEM)]
        + vmem(2)
        + [pl.BlockSpec((1, GROUPS // 2, CT, 256), lambda i: (0, 0, 0, 0))]
        + anywhere(1),
        out_specs=tuple(vmem(2)),
        compiler_params=params(50),
        cost_estimate=SMALL,
        name="queries",
    )(place, normed, other, weight, fence)


def stack_kernel(*refs):
    for i, ref in enumerate(refs[:-1]):
        refs[-1][i] = ref[...]


def stack(*chunks):
    return pl.pallas_call(
        stack_kernel,
        out_shape=jax.ShapeDtypeStruct((len(chunks),) + chunks[0].shape, BF16),
        in_specs=vmem(len(chunks)),
        out_specs=vmem(1)[0],
        compiler_params=params(50),
        cost_estimate=SMALL,
        name="stack",
    )(*chunks)


def keys_kernel(place, own, received, weight, *rest):
    out, tiles, sems = rest[-3:]
    chunks = [ref.at[i] for ref in (own, received) for i in range(ref.shape[0])]
    values = jnp.concatenate([chunk[...].reshape(SEEDS * TOKS, CT) for chunk in chunks], axis=0)
    ones = (lax.broadcasted_iota(jnp.int32, (1, 256), 1) % 128 == PAIR).astype(F32)
    copies = []
    for pair in range(GROUPS // 2):
        product = (dot(values, weight[0, pair]) + ones).astype(BF16)
        for i in range(len(chunks)):
            for side in range(2):
                for seed in range(SEEDS):
                    start = (i * SEEDS + seed) * TOKS
                    tiles[i, 2 * pair + side, seed] = product[
                        start : start + TOKS, side * 128 : side * 128 + 128
                    ]
            rows = pl.ds(pl.multiple_of(place[2 + i] * TOKS, TOKS), TOKS)
            copies.append(
                pltpu.make_async_copy(
                    tiles.at[i, pl.ds(2 * pair, 2)],
                    out.at[pl.ds(2 * pair, 2), :, rows],
                    sems.at[pair, i],
                )
            )
            copies[-1].start()
    for copy in copies:
        copy.wait()


def keys(place, ids, own, received, weight, before=None, fences=()):
    more = ([] if before is None else [before]) + list(fences)
    count = own.shape[0] + received.shape[0]
    return pl.pallas_call(
        keys_kernel,
        grid=(1,),
        out_shape=jax.ShapeDtypeStruct((GROUPS, SEEDS, ALL_TOKS, 128), BF16),
        in_specs=[pl.BlockSpec(memory_space=pltpu.SMEM)]
        + vmem(2)
        + [pl.BlockSpec((1, GROUPS // 2, CT, 256), lambda i: (1, 0, 0, 0))]
        + anywhere(len(more)),
        out_specs=anywhere(1)[0],
        scratch_shapes=[
            pltpu.VMEM((count, GROUPS, SEEDS, TOKS, 128), BF16),
            pltpu.SemaphoreType.DMA((GROUPS // 2, count)),
        ],
        input_output_aliases={} if before is None else {4: 0},
        compiler_params=params(50),
        cost_estimate=SMALL,
        name="keys",
    )(jnp.concatenate([place, ids]), own, received, weight, *more)


def attend_kernel(count, extra, group_ids, query, gate, key_value, *rest):
    biases = rest[:count]
    own, sent, slots, scores, sems = rest[count + extra :]
    step = pl.program_id(0)

    def load(i):
        return pltpu.make_async_copy(biases[i], slots.at[i % 2], sems.at[i % 2])

    for i in range(count):

        @pl.when(step == i)
        def _(i=i):
            if i == 0:
                load(0).start()
            if i + 1 < count:
                load(i + 1).start()
            load(i).wait()

    bias = slots.at[step % 2]
    width = 512
    tops = []
    for seed in range(SEEDS):
        peak = None
        for c in range(ALL_TOKS // width):
            cols = slice(c * width, (c + 1) * width)
            part = dot_t(query[0, seed], key_value[0, seed, cols, :]) + bias[:, cols].astype(F32)
            scores[seed, :, cols] = part
            for w in range(width // 128):
                tile = part[:, w * 128 : (w + 1) * 128]
                peak = tile if peak is None else jnp.maximum(peak, tile)
        tops.append(jnp.max(peak, axis=-1, keepdims=True))
    for seed in range(SEEDS):
        total = None
        for c in range(ALL_TOKS // width):
            cols = slice(c * width, (c + 1) * width)
            part = dot(
                jnp.exp(scores[seed, :, cols] - tops[seed]).astype(BF16), key_value[0, seed, cols, :]
            )
            total = part if total is None else total + part
        gated = (total / total[:, PAIR : PAIR + 1] * gate[0, seed]).astype(BF16)
        own[0, seed] = gated[:TOKS]
        sent[0, seed] = gated[TOKS:]


def attend(group_ids, query, gate, key_value, before, biases):
    count = len(biases)
    shape = jax.ShapeDtypeStruct((GROUPS, SEEDS, TOKS, 128), BF16)

    def by_group(*block):
        return pl.BlockSpec((1,) + block, lambda i, ids: (ids[i],) + (0,) * len(block))

    grid_spec = pltpu.PrefetchScalarGridSpec(
        num_scalar_prefetch=1,
        grid=(count,),
        in_specs=[
            by_group(SEEDS, 2 * TOKS, 128),
            by_group(SEEDS, 2 * TOKS, 128),
            by_group(SEEDS, ALL_TOKS, 128),
        ]
        + anywhere(count + len(before)),
        out_specs=(by_group(SEEDS, TOKS, 128),) * 2,
        scratch_shapes=[
            pltpu.VMEM((2, 2 * TOKS, ALL_TOKS), BF16),
            pltpu.VMEM((SEEDS, 2 * TOKS, ALL_TOKS), F32),
            pltpu.SemaphoreType.DMA((2,)),
        ],
    )
    return pl.pallas_call(
        functools.partial(attend_kernel, count, len(before)),
        grid_spec=grid_spec,
        out_shape=(shape, shape),
        input_output_aliases={4 + count + i: i for i in range(len(before))},
        compiler_params=params(50),
        cost_estimate=SMALL,
        name="attend",
    )(group_ids, query, gate, key_value, *biases, *before)


def finish_kernel(
    residual, own, received, mix, wide_hbm, narrow_hbm, spread_weight,
    state, spread, first, last,
    wide, narrow, mix_tile, total, hidden, sems,
):
    step = 512
    count = TRANS // step
    copies = []
    for c in range(count):
        gate_cols = pl.ds(c * step, step)
        up_cols = pl.ds(TRANS + c * step, step)
        copies.append(
            [
                pltpu.make_async_copy(wide_hbm.at[:, gate_cols], wide.at[:, gate_cols], sems.at[c, 0]),
                pltpu.make_async_copy(wide_hbm.at[:, up_cols], wide.at[:, up_cols], sems.at[c, 1]),
                pltpu.make_async_copy(narrow_hbm.at[gate_cols], narrow.at[gate_cols], sems.at[c, 2]),
            ]
        )
    for group in copies:
        for copy in group:
            copy.start()
    values = residual[...].reshape(SEEDS * TOKS, CT)
    for group in range(GROUPS):
        gated = (own[group] + received[group]).reshape(SEEDS * TOKS, 128)
        mix_tile[group, 0:PAIR] = mix[group]
        mix_tile[group, PAIR:128] = jnp.zeros((128 - PAIR, CT), BF16)
        values = values + dot(gated, mix_tile[group])
    total[...] = values
    normed = layer_norm(values).astype(BF16)
    for c in range(count):
        for copy in copies[c]:
            copy.wait()
        gate = dot(normed, wide[:, c * step : (c + 1) * step])
        up = dot(normed, wide[:, TRANS + c * step : TRANS + (c + 1) * step])
        hidden[:, c * step : (c + 1) * step] = (jax.nn.silu(gate) * up).astype(BF16)
    rounded = (total[...] + dot(hidden[...], narrow[...])).astype(BF16)
    state[...] = rounded.reshape(SEEDS, TOKS, CT)
    carried = dot(rounded, spread_weight[...]).astype(BF16).reshape(SEEDS, TOKS, CA)
    spread[...] = carried
    first[...] = carried[:, :EDGE]
    last[...] = carried[:, TOKS - EDGE :]


def finish(residual, own, received, mix, wide, narrow, spread_weight):
    return pl.pallas_call(
        finish_kernel,
        out_shape=(
            jax.ShapeDtypeStruct((SEEDS, TOKS, CT), BF16),
            jax.ShapeDtypeStruct((SEEDS, TOKS, CA), BF16),
            jax.ShapeDtypeStruct((SEEDS, EDGE, CA), BF16),
            jax.ShapeDtypeStruct((SEEDS, EDGE, CA), BF16),
        ),
        in_specs=vmem(4) + anywhere(2) + vmem(1),
        out_specs=tuple(vmem(4)),
        scratch_shapes=[
            pltpu.VMEM((CT, 2 * TRANS), BF16),
            pltpu.VMEM((TRANS, CT), BF16),
            pltpu.VMEM((GROUPS, 128, CT), BF16),
            pltpu.VMEM((SEEDS * TOKS, CT), F32),
            pltpu.VMEM((SEEDS * TOKS, TRANS), BF16),
            pltpu.SemaphoreType.DMA((3, 3)),
        ],
        compiler_params=params(40),
        cost_estimate=SMALL,
        name="finish",
    )(residual, own, received, mix, wide, narrow, spread_weight)


def along_tok(values, by):
    return lax.ppermute(values, "tok", [(i, (i + by) % 16) for i in range(16)])


def across_core(values):
    return lax.ppermute(values, "tok", [(i, i ^ 1) for i in range(16)])


def along_x(values, by):
    return lax.ppermute(values, "tok", [(i, i // 8 * 8 + (i + 2 * by) % 8) for i in range(16)])


def across_floor(values):
    return lax.ppermute(values, "tok", [(i, i ^ 8) for i in range(16)])


def along_y(values, by):
    return lax.ppermute(values, "seed", [(i, (i + 2 * by) % 8) for i in range(8)])


def along_z(values):
    return lax.ppermute(values, "seed", [(i, i ^ 1) for i in range(8)])


def per_device(
    atom_feats, atom_index, token_cond, pair_bias, atom_bias_enc, atom_bias_dec,
    enc_project, enc_mix, pool_weight, token_project, token_mix, swiglu_in, swiglu_out,
    spread_weight, dec_project, dec_mix,
):
    tok = lax.axis_index("tok")
    seed = lax.axis_index("seed")
    place = jnp.stack([tok, tok % 2]).astype(jnp.int32)
    feats = atom_feats.reshape(SEEDS * ATOMS, CA)
    bias_enc = atom_bias_enc.reshape(4 * ATOMS, WIN)
    bias_dec = atom_bias_dec.reshape(4 * ATOMS, WIN)
    index = atom_index.reshape(8, CA)

    up, down, send, joined = pack(place, feats, bias_enc, index, pair_bias)
    low = along_tok(up, 1)
    high = along_tok(down, -1)
    mine = join(joined, across_core(send), low, high)
    below = along_y(mine, 1)
    above = along_y(mine, -1)
    other = along_z(mine)

    encoded, first, last, residual, normed, again = encode(
        place, feats, low, high, bias_enc, index, token_cond, enc_project, enc_mix, pool_weight,
        mine,
    )
    x_below = along_x(normed, 1)
    x_above = along_x(normed, -1)
    below, above, first, last, again, mine = hold(
        below, above, first, last, again, mine
    )
    far = along_y(mine, 2)
    z_own = across_floor(again)
    mate = across_core(again)
    x_far = along_x(again, 2)
    weights = spaced(place, token_project, below)
    z_own, x_below, x_above, x_far, weights, other = hold(
        z_own, x_below, x_above, x_far, weights, other
    )
    z_below = along_x(z_own, 1)
    z_above = along_x(z_own, -1)
    z_far = across_floor(x_far)
    near = stack(again, x_below, x_above, z_own)
    near_mate = across_core(near)
    query, gate = queries(place, again, mate, weights, z_own)
    enc_low = along_tok(last, 1)
    enc_high = along_tok(first, -1)
    far, other, z_below, z_above, query = hold(far, other, z_below, z_above, query)
    other_below = along_y(other, 1)
    other_above = along_y(other, -1)
    other_far = along_z(far)
    rest = stack(x_far, z_below, z_above, z_far)
    rest_mate = across_core(rest)

    column, floor, core = tok // 2 % 4, tok // 8, tok % 2

    def shards(*offsets):
        return jnp.stack(
            [
                (floor ^ dz) * 8 + (column + dx) % 4 * 2 + (core ^ side)
                for side in (0, 1)
                for dx, dz in offsets
            ]
        ).astype(jnp.int32)

    key_value = keys(
        place, shards((0, 0), (3, 0), (1, 0), (0, 1)), near, near_mate, weights
    )
    key_value = keys(
        place, shards((2, 0), (3, 1), (1, 1), (2, 1)), rest, rest_mate, weights, key_value,
        (enc_low, enc_high),
    )

    level, side = seed // 2, seed % 2

    def ids(*offsets):
        return jnp.stack([(level + dy) % 4 * 2 + (side ^ dz) for dy, dz in offsets]).astype(jnp.int32)

    done = attend(
        ids((0, 0), (3, 0), (1, 0), (2, 0), (0, 1)), query, gate, key_value, (),
        (mine, below, above, far, other),
    )
    own, sent = attend(
        ids((3, 1), (1, 1), (2, 1)), query, gate, key_value, done,
        (other_below, other_above, other_far),
    )

    state, spread, spread_first, spread_last = finish(
        residual, own, across_core(sent), token_mix.reshape(GROUPS, PAIR, CT), swiglu_in,
        swiglu_out, spread_weight,
    )
    update = decode(
        place, encoded, enc_low, enc_high, spread, along_tok(spread_last, 1),
        along_tok(spread_first, -1), bias_dec, index, low, high, dec_project, dec_mix,
    )
    return state.transpose(1, 0, 2), update.reshape(ATOMS, SEEDS, CA)


def solution(mesh):
    placed = (
        P("tok", "seed", None),
        P("tok"),
        P("tok", None),
        P("seed", "tok", None),
        P("tok", None, None),
        P("tok", None, None),
    ) + (P(),) * 10
    return jax.shard_map(
        per_device,
        mesh=mesh,
        in_specs=placed,
        out_specs=(P("tok", "seed", None), P("tok", "seed", None)),
        check_vma=False,
    )
```

```python
import functools

import jax
import jax.numpy as jnp
from jax import lax
from jax.experimental import pallas as pl
from jax.experimental.pallas import tpu as pltpu
from jax.sharding import PartitionSpec as P

EPS = 1e-05
NEG = -1000000000.0
F32 = jnp.float32
BF16 = jnp.bfloat16

SEEDS = 2
ATOMS = 1024
TOKS = 128
CA = 128
CT = 768
HEADS = 16
HEAD = 48
PAIR = 96
GROUPS = 8
QB = 32
WIN = 128
MARGIN = 48
LOWER = 80
EXT = 1152
EDGE = 16
TRANS = 1536
ALL_TOKS = 2048
ALL_ATOMS = 16384
UP_ROWS = 2 * LOWER + 4 * QB + 16
DOWN_ROWS = 2 * MARGIN + 16


SMALL = pl.CostEstimate(flops=10**6, bytes_accessed=10**4, transcendentals=0)
LARGE = pl.CostEstimate(flops=7 * 10**10, bytes_accessed=10**4, transcendentals=0)


def params(limit_mb, **more):
    return pltpu.CompilerParams(vmem_limit_bytes=limit_mb * 1024 * 1024, **more)


def vmem(n):
    return [pl.BlockSpec(memory_space=pltpu.VMEM)] * n


def anywhere(n):
    return [pl.BlockSpec(memory_space=pltpu.HBM)] * n


def layer_norm(values):
    centre = values - jnp.mean(values, axis=-1, keepdims=True)
    variance = jnp.mean(centre * centre, axis=-1, keepdims=True)
    return centre * lax.rsqrt(variance + EPS)


def dot(a, b):
    return jnp.dot(a, b, preferred_element_type=F32)


def dot_t(a, b):
    return lax.dot_general(a, b, (((1,), (1,)), ((), ())), preferred_element_type=F32)


def window_blocks(packed, bias, mixed, blocks, first_atom, unroll):
    lane_head = lax.broadcasted_iota(jnp.int32, (QB, CA), 1) // 32
    head_mask = [(lane_head == h).astype(BF16) for h in range(4)]
    lane = lax.broadcasted_iota(jnp.int32, (1, WIN), 1)
    ones = jnp.ones((WIN, CA), BF16)
    for b in (0, 1, 2, blocks - 2, blocks - 1):
        position = lane + (first_atom + b * QB)
        inside = (position >= 0) & (position < ALL_ATOMS)
        place = slice(b * 4 * QB, (b + 1) * 4 * QB)
        bias[place] = jnp.where(inside, bias[place], NEG)

    def body(i, carry):
        work = []
        for u in range(unroll):
            b = i * unroll + u
            rows = pl.multiple_of(b * QB, QB)
            query_rows = pl.multiple_of(b * QB + MARGIN, 16)
            bias_rows = pl.multiple_of(b * 4 * QB, 4 * QB)
            added = jnp.concatenate(
                [bias[pl.ds(bias_rows + h, QB, stride=4), :] for h in range(4)], axis=0
            )
            for seed in range(SEEDS):
                work.append((rows, query_rows, added, seed))
        scores = []
        for rows, query_rows, added, seed in work:
            query = packed[seed, pl.ds(query_rows, QB), 0:CA]
            key = packed[seed, pl.ds(rows, WIN), CA : 2 * CA]
            stacked = jnp.concatenate([query * head_mask[h] for h in range(4)], axis=0)
            scores.append(dot_t(stacked, key) * (32**-0.5) + added)
        weights = [jnp.exp(s - jnp.max(s, axis=-1, keepdims=True)).astype(BF16) for s in scores]
        for (rows, _, _, seed), w in zip(work, weights):
            value = jnp.concatenate([packed[seed, pl.ds(rows, WIN), 2 * CA : 3 * CA], ones], axis=1)
            out = dot(w, value)
            joined = out[3 * QB :]
            for h in range(3):
                joined = jnp.where(jnp.concatenate([lane_head, lane_head], axis=1) == h, out[h * QB : (h + 1) * QB], joined)
            mixed[seed, pl.ds(rows, QB), :] = (joined[:, :CA] / joined[:, CA:]).astype(BF16)
        return carry

    lax.fori_loop(0, blocks // unroll, body, 0)


def pack_kernel(place, feats, bias, index, pair_bias, up, down, send, joined, heads, rows, sems):
    base, core = place[0] * TOKS, place[1]
    low_rows, high_rows = UP_ROWS - 16, DOWN_ROWS - 16
    loads = (
        (pair_bias, heads),
        (feats.at[pl.ds(2 * (ATOMS - LOWER), 2 * LOWER)], rows.at[pl.ds(0, 2 * LOWER)]),
        (bias.at[pl.ds(4 * (ATOMS - QB), 4 * QB)], rows.at[pl.ds(2 * LOWER, 4 * QB)]),
        (feats.at[pl.ds(0, 2 * MARGIN)], rows.at[pl.ds(UP_ROWS, 2 * MARGIN)]),
    )
    loads = [pltpu.make_async_copy(a, b, sems.at[i]) for i, (a, b) in enumerate(loads)]
    for copy in loads:
        copy.start()
    tail = (index[7:8] - (base + TOKS)).astype(F32)
    head = (index[0:1] - base).astype(F32)
    rows[low_rows:UP_ROWS] = jnp.broadcast_to(tail, (16, CA)).astype(BF16)
    rows[UP_ROWS + high_rows :] = jnp.broadcast_to(head, (16, CA)).astype(BF16)
    for copy in loads:
        copy.wait()
    stores = (
        (rows.at[pl.ds(0, UP_ROWS)], up),
        (rows.at[pl.ds(UP_ROWS, DOWN_ROWS)], down),
        (heads.at[1 - core], send),
        (heads.at[core], joined.at[pl.ds(0, TOKS)]),
    )
    stores = [pltpu.make_async_copy(a, b, sems.at[4 + i]) for i, (a, b) in enumerate(stores)]
    for copy in stores:
        copy.start()
    for copy in stores:
        copy.wait()


def pack(place, feats, bias, index, pair_bias):
    return pl.pallas_call(
        pack_kernel,
        out_shape=(
            jax.ShapeDtypeStruct((UP_ROWS, CA), BF16),
            jax.ShapeDtypeStruct((DOWN_ROWS, CA), BF16),
            jax.ShapeDtypeStruct((TOKS, ALL_TOKS), BF16),
            jax.ShapeDtypeStruct((2 * TOKS, ALL_TOKS), BF16),
        ),
        in_specs=[pl.BlockSpec(memory_space=pltpu.SMEM)] + anywhere(2) + vmem(1) + anywhere(1),
        out_specs=tuple(anywhere(4)),
        scratch_shapes=[
            pltpu.VMEM((2, TOKS, ALL_TOKS), BF16),
            pltpu.VMEM((UP_ROWS + DOWN_ROWS, CA), BF16),
            pltpu.SemaphoreType.DMA((8,)),
        ],
        compiler_params=params(58),
        cost_estimate=SMALL,
        name="pack",
    )(place, feats, bias, index, pair_bias)


def join_kernel(joined, received, low, high, out, rows, sems):
    load = pltpu.make_async_copy(received, rows, sems.at[0])
    load.start()
    load.wait()
    store = pltpu.make_async_copy(rows, out.at[pl.ds(TOKS, TOKS)], sems.at[1])
    store.start()
    store.wait()


def join(joined, received, low, high):
    return pl.pallas_call(
        join_kernel,
        out_shape=jax.ShapeDtypeStruct(joined.shape, BF16),
        in_specs=anywhere(4),
        out_specs=anywhere(1)[0],
        input_output_aliases={0: 0},
        scratch_shapes=[pltpu.VMEM((TOKS, ALL_TOKS), BF16), pltpu.SemaphoreType.DMA((2,))],
        compiler_params=params(58),
        cost_estimate=SMALL,
        name="join",
    )(joined, received, low, high)


def hold_kernel(*refs):
    del refs


def hold(*arrays, cost=SMALL):
    return pl.pallas_call(
        hold_kernel,
        out_shape=tuple(jax.ShapeDtypeStruct(array.shape, array.dtype) for array in arrays),
        in_specs=anywhere(len(arrays)),
        out_specs=tuple(anywhere(len(arrays))),
        input_output_aliases={i: i for i in range(len(arrays))},
        compiler_params=params(58),
        cost_estimate=cost,
        name="hold",
    )(*arrays)


def encode_kernel(
    place, feats, low, high, bias, index, cond, project, mix, pool, fence,
    encoded, first, last, residual, normed, again,
    rows, bias32, packed, mixed, ext,
):
    rows[0 : 2 * LOWER] = low[0 : 2 * LOWER].astype(F32)
    rows[2 * LOWER : 2 * (LOWER + ATOMS)] = feats[...].astype(F32)
    rows[2 * (LOWER + ATOMS) : 2 * EXT] = high[0 : 2 * MARGIN].astype(F32)
    bias32[0 : 4 * QB] = low[2 * LOWER : 2 * LOWER + 4 * QB].astype(F32)
    bias32[4 * QB :] = bias[...].astype(F32)
    for seed in range(SEEDS):
        values = rows[pl.ds(seed, EXT, stride=2), :]
        packed[seed] = dot(layer_norm(values).astype(BF16), project[...]).astype(BF16)
    window_blocks(packed, bias32, mixed, 33, place[0] * ATOMS - QB - MARGIN, 11)
    token = lax.broadcasted_iota(jnp.int32, (TOKS, CA), 0)
    below = low[2 * LOWER + 4 * QB :].astype(F32)[0:1].astype(jnp.int32)
    below = jnp.where(place[0] == 0, -1000, below)
    base = place[0] * TOKS
    chosen = jnp.concatenate(
        [(index[i : i + 1] - base == token).astype(F32) for i in range(8)]
        + [(below == token).astype(F32)],
        axis=1,
    )
    counts = jnp.sum(chosen, axis=1, keepdims=True)
    chosen = chosen.astype(BF16)
    for seed in range(SEEDS):
        values = rows[pl.ds(2 * MARGIN + seed, QB + ATOMS, stride=2), :]
        result = (values + dot(mixed[seed], mix[...])).astype(BF16)
        ext[0:ATOMS] = result[QB:]
        ext[ATOMS : EXT - QB] = jnp.zeros((EXT - QB - ATOMS, CA), BF16)
        ext[EXT - QB :] = result[0:QB]
        encoded[seed] = ext[0:ATOMS]
        first[seed] = ext[0:MARGIN]
        last[seed] = ext[ATOMS - MARGIN : ATOMS]
        lifted = jnp.maximum(dot(ext[...], pool[...]), 0.0).astype(BF16)
        state = cond[...].astype(F32) + dot(chosen, lifted) / counts
        residual[seed] = state
        normed[seed] = layer_norm(state).astype(BF16)
        again[seed] = normed[seed]


def encode(*args):
    return pl.pallas_call(
        encode_kernel,
        out_shape=(
            jax.ShapeDtypeStruct((SEEDS, ATOMS, CA), BF16),
            jax.ShapeDtypeStruct((SEEDS, MARGIN, CA), BF16),
            jax.ShapeDtypeStruct((SEEDS, MARGIN, CA), BF16),
            jax.ShapeDtypeStruct((SEEDS, TOKS, CT), F32),
            jax.ShapeDtypeStruct((SEEDS, TOKS, CT), BF16),
            jax.ShapeDtypeStruct((SEEDS, TOKS, CT), BF16),
        ),
        in_specs=[pl.BlockSpec(memory_space=pltpu.SMEM)] + vmem(9) + anywhere(1),
        out_specs=tuple(vmem(6)),
        scratch_shapes=[
            pltpu.VMEM((2 * EXT, CA), F32),
            pltpu.VMEM((33 * 4 * QB, WIN), F32),
            pltpu.VMEM((SEEDS, EXT, 3 * CA), BF16),
            pltpu.VMEM((SEEDS, QB + ATOMS, CA), BF16),
            pltpu.VMEM((EXT, CA), BF16),
        ],
        compiler_params=params(58),
        cost_estimate=SMALL,
        name="encode",
    )(*args)


def decode_kernel(
    place, enc, spread, edge_low, edge_high, bias, index, low, high,
    project, mix,
    update,
    rows, bias32, packed, mixed, decoded, tokens, moved,
):
    bias32[...] = bias[...].astype(F32)
    token = lax.broadcasted_iota(jnp.int32, (TOKS + 2 * EDGE, CA), 0) - EDGE
    below = low[2 * LOWER + 4 * QB :].astype(F32)[0:1].astype(jnp.int32)
    above = high[2 * MARGIN :].astype(F32)[0:1].astype(jnp.int32) + TOKS
    base = place[0] * TOKS
    chosen = jnp.concatenate(
        [(index[i : i + 1] - base == token).astype(F32) for i in range(8)]
        + [(below == token).astype(F32), (above == token).astype(F32)],
        axis=1,
    ).astype(BF16)
    end = MARGIN + ATOMS
    for seed in range(SEEDS):
        tokens[0:EDGE] = edge_low[seed, 0:EDGE]
        tokens[EDGE : EDGE + TOKS] = spread[seed]
        tokens[EDGE + TOKS :] = edge_high[seed, 0:EDGE]
        moved[...] = lax.dot_general(
            chosen, tokens[...], (((0,), (0,)), ((), ())), preferred_element_type=F32
        )
        decoded[0:MARGIN] = edge_low[seed, EDGE:].astype(F32) + moved[ATOMS + CA - MARGIN : ATOMS + CA]
        decoded[MARGIN:end] = enc[seed].astype(F32) + moved[0:ATOMS]
        decoded[end : end + MARGIN] = (
            edge_high[seed, EDGE:].astype(F32) + moved[ATOMS + CA : ATOMS + CA + MARGIN]
        )
        decoded[end + MARGIN :] = jnp.zeros((EXT - end - MARGIN, CA), F32)
        values = decoded[...].astype(BF16).astype(F32)
        rows[pl.ds(seed, EXT, stride=2), :] = values
        packed[seed] = dot(layer_norm(values).astype(BF16), project[...]).astype(BF16)
    window_blocks(packed, bias32, mixed, 32, place[0] * ATOMS - MARGIN, 8)
    for seed in range(SEEDS):
        at = pl.ds(2 * MARGIN + seed, ATOMS, stride=2)
        rows[at, :] = rows[at, :] + dot(mixed[seed], mix[...])
    update[...] = rows[2 * MARGIN : 2 * (MARGIN + ATOMS)].astype(BF16)


def decode(*args):
    return pl.pallas_call(
        decode_kernel,
        out_shape=jax.ShapeDtypeStruct((SEEDS * ATOMS, CA), BF16),
        in_specs=[pl.BlockSpec(memory_space=pltpu.SMEM)] + vmem(10),
        out_specs=vmem(1)[0],
        scratch_shapes=[
            pltpu.VMEM((2 * EXT, CA), F32),
            pltpu.VMEM((32 * 4 * QB, WIN), F32),
            pltpu.VMEM((SEEDS, EXT, 3 * CA), BF16),
            pltpu.VMEM((SEEDS, ATOMS, CA), BF16),
            pltpu.VMEM((EXT, CA), F32),
            pltpu.VMEM((TOKS + 2 * EDGE, CA), BF16),
            pltpu.VMEM((ATOMS + 2 * CA, CA), F32),
        ],
        compiler_params=params(30),
        cost_estimate=SMALL,
        name="decode",
    )(*args)


def spaced_kernel(place, first, second, fence, out):
    core = place[1]
    for group in range(4):
        start = PAIR * group // 128 * 128
        shift = PAIR * group - start + HEAD * core
        width = min(256, 384 - start)
        row = lax.broadcasted_iota(jnp.int32, (width, 128), 0) - shift
        lane = lax.broadcasted_iota(jnp.int32, (width, 128), 1)

        def pick(side):
            at = lane - HEAD * side
            return ((row == at) & (at >= 0) & (at < HEAD)).astype(F32).astype(BF16)

        block = dot(first[:, start : start + width], pick(1 - core)) + dot(
            second[:, start : start + width], pick(core)
        )
        out[0, group // 2, :, group % 2 * 128 : group % 2 * 128 + 128] = block.astype(BF16)


def spaced(place, weight, fence):
    return pl.pallas_call(
        spaced_kernel,
        grid=(4,),
        out_shape=jax.ShapeDtypeStruct((2, GROUPS // 2, CT, 256), BF16),
        in_specs=[
            pl.BlockSpec(memory_space=pltpu.SMEM),
            pl.BlockSpec((CT, 384), lambda i: (0, i)),
            pl.BlockSpec((CT, 384), lambda i: (0, jnp.where(i < 2, 6 + i, 2 + i))),
        ]
        + anywhere(1),
        out_specs=pl.BlockSpec((1, 2, CT, 256), lambda i: (i // 2, i % 2, 0, 0)),
        compiler_params=params(58),
        cost_estimate=LARGE,
        name="spaced",
    )(place, weight, weight, fence)


def queries_kernel(place, normed, other, weight, fence, query, gate):
    core = place[1]
    lane = lax.broadcasted_iota(jnp.int32, (1, 128), 1)
    in_query = (lane // HEAD == 1 - core) & (lane < PAIR)
    in_gate = (lane // HEAD == core) & (lane < PAIR)
    values = jnp.concatenate([normed[0], other[0], normed[1], other[1]], axis=0)
    for pair in range(GROUPS // 2):
        product = dot(values, weight[0, pair])
        for side in range(2):
            part = product[:, side * 128 : side * 128 + 128]
            group = 2 * pair + side
            queried = jnp.where(in_query, part * (HEAD**-0.5), 0.0).astype(BF16)
            opened = jnp.where(in_gate, jax.nn.sigmoid(part), 0.0)
            for seed in range(SEEDS):
                at = slice(seed * 2 * TOKS, (seed + 1) * 2 * TOKS)
                query[group, seed] = queried[at]
                gate[group, seed] = opened[at]


def queries(place, normed, other, weight, fence):
    return pl.pallas_call(
        queries_kernel,
        grid=(1,),
        out_shape=(
            jax.ShapeDtypeStruct((GROUPS, SEEDS, 2 * TOKS, 128), BF16),
            jax.ShapeDtypeStruct((GROUPS, SEEDS, 2 * TOKS, 128), F32),
        ),
        in_specs=[pl.BlockSpec(memory_space=pltpu.SMEM)]
        + vmem(2)
        + [pl.BlockSpec((1, GROUPS // 2, CT, 256), lambda i: (0, 0, 0, 0))]
        + anywhere(1),
        out_specs=tuple(vmem(2)),
        compiler_params=params(50),
        cost_estimate=SMALL,
        name="queries",
    )(place, normed, other, weight, fence)


def stack_kernel(*refs):
    for i, ref in enumerate(refs[:-1]):
        refs[-1][i] = ref[...]


def stack(*chunks):
    return pl.pallas_call(
        stack_kernel,
        out_shape=jax.ShapeDtypeStruct((len(chunks),) + chunks[0].shape, BF16),
        in_specs=vmem(len(chunks)),
        out_specs=vmem(1)[0],
        compiler_params=params(50),
        cost_estimate=SMALL,
        name="stack",
    )(*chunks)


def keys_kernel(place, own, received, weight, *rest):
    out, tiles, sems = rest[-3:]
    chunks = [ref.at[i] for ref in (own, received) for i in range(ref.shape[0])]
    values = jnp.concatenate([chunk[...].reshape(SEEDS * TOKS, CT) for chunk in chunks], axis=0)
    ones = (lax.broadcasted_iota(jnp.int32, (1, 256), 1) % 128 == PAIR).astype(F32)
    copies = []
    for pair in range(GROUPS // 2):
        product = (dot(values, weight[0, pair]) + ones).astype(BF16)
        for i in range(len(chunks)):
            for side in range(2):
                for seed in range(SEEDS):
                    start = (i * SEEDS + seed) * TOKS
                    tiles[i, 2 * pair + side, seed] = product[
                        start : start + TOKS, side * 128 : side * 128 + 128
                    ]
            rows = pl.ds(pl.multiple_of(place[2 + i] * TOKS, TOKS), TOKS)
            copies.append(
                pltpu.make_async_copy(
                    tiles.at[i, pl.ds(2 * pair, 2)],
                    out.at[pl.ds(2 * pair, 2), :, rows],
                    sems.at[pair, i],
                )
            )
            copies[-1].start()
    for copy in copies:
        copy.wait()


def keys(place, ids, own, received, weight, before=None, fences=()):
    more = ([] if before is None else [before]) + list(fences)
    count = own.shape[0] + received.shape[0]
    return pl.pallas_call(
        keys_kernel,
        grid=(1,),
        out_shape=jax.ShapeDtypeStruct((GROUPS, SEEDS, ALL_TOKS, 128), BF16),
        in_specs=[pl.BlockSpec(memory_space=pltpu.SMEM)]
        + vmem(2)
        + [pl.BlockSpec((1, GROUPS // 2, CT, 256), lambda i: (1, 0, 0, 0))]
        + anywhere(len(more)),
        out_specs=anywhere(1)[0],
        scratch_shapes=[
            pltpu.VMEM((count, GROUPS, SEEDS, TOKS, 128), BF16),
            pltpu.SemaphoreType.DMA((GROUPS // 2, count)),
        ],
        input_output_aliases={} if before is None else {4: 0},
        compiler_params=params(50),
        cost_estimate=SMALL,
        name="keys",
    )(jnp.concatenate([place, ids]), own, received, weight, *more)


def attend_kernel(count, extra, group_ids, query, gate, key_value, *rest):
    biases = rest[:count]
    own, sent, slots, scores, sems = rest[count + extra :]
    step = pl.program_id(0)

    def load(i):
        return pltpu.make_async_copy(biases[i], slots.at[i % 2], sems.at[i % 2])

    for i in range(count):

        @pl.when(step == i)
        def _(i=i):
            if i == 0:
                load(0).start()
            if i + 1 < count:
                load(i + 1).start()
            load(i).wait()

    bias = slots.at[step % 2]
    width = 512
    tops = []
    for seed in range(SEEDS):
        peak = None
        for c in range(ALL_TOKS // width):
            cols = slice(c * width, (c + 1) * width)
            part = dot_t(query[0, seed], key_value[0, seed, cols, :]) + bias[:, cols].astype(F32)
            scores[seed, :, cols] = part
            for w in range(width // 128):
                tile = part[:, w * 128 : (w + 1) * 128]
                peak = tile if peak is None else jnp.maximum(peak, tile)
        tops.append(jnp.max(peak, axis=-1, keepdims=True))
    for seed in range(SEEDS):
        total = None
        for c in range(ALL_TOKS // width):
            cols = slice(c * width, (c + 1) * width)
            part = dot(
                jnp.exp(scores[seed, :, cols] - tops[seed]).astype(BF16), key_value[0, seed, cols, :]
            )
            total = part if total is None else total + part
        gated = (total / total[:, PAIR : PAIR + 1] * gate[0, seed]).astype(BF16)
        own[0, seed] = gated[:TOKS]
        sent[0, seed] = gated[TOKS:]


def attend(group_ids, query, gate, key_value, before, biases):
    count = len(biases)
    shape = jax.ShapeDtypeStruct((GROUPS, SEEDS, TOKS, 128), BF16)

    def by_group(*block):
        return pl.BlockSpec((1,) + block, lambda i, ids: (ids[i],) + (0,) * len(block))

    grid_spec = pltpu.PrefetchScalarGridSpec(
        num_scalar_prefetch=1,
        grid=(count,),
        in_specs=[
            by_group(SEEDS, 2 * TOKS, 128),
            by_group(SEEDS, 2 * TOKS, 128),
            by_group(SEEDS, ALL_TOKS, 128),
        ]
        + anywhere(count + len(before)),
        out_specs=(by_group(SEEDS, TOKS, 128),) * 2,
        scratch_shapes=[
            pltpu.VMEM((2, 2 * TOKS, ALL_TOKS), BF16),
            pltpu.VMEM((SEEDS, 2 * TOKS, ALL_TOKS), F32),
            pltpu.SemaphoreType.DMA((2,)),
        ],
    )
    return pl.pallas_call(
        functools.partial(attend_kernel, count, len(before)),
        grid_spec=grid_spec,
        out_shape=(shape, shape),
        input_output_aliases={4 + count + i: i for i in range(len(before))},
        compiler_params=params(50),
        cost_estimate=SMALL,
        name="attend",
    )(group_ids, query, gate, key_value, *biases, *before)


def finish_kernel(
    residual, own, received, mix, wide_hbm, narrow_hbm, spread_weight, enc_first, enc_last,
    state, spread, first, last,
    wide, narrow, mix_tile, total, hidden, sems,
):
    step = 512
    count = TRANS // step
    copies = []
    for c in range(count):
        gate_cols = pl.ds(c * step, step)
        up_cols = pl.ds(TRANS + c * step, step)
        copies.append(
            [
                pltpu.make_async_copy(wide_hbm.at[:, gate_cols], wide.at[:, gate_cols], sems.at[c, 0]),
                pltpu.make_async_copy(wide_hbm.at[:, up_cols], wide.at[:, up_cols], sems.at[c, 1]),
                pltpu.make_async_copy(narrow_hbm.at[gate_cols], narrow.at[gate_cols], sems.at[c, 2]),
            ]
        )
    for group in copies:
        for copy in group:
            copy.start()
    values = residual[...].reshape(SEEDS * TOKS, CT)
    for group in range(GROUPS):
        gated = (own[group] + received[group]).reshape(SEEDS * TOKS, 128)
        mix_tile[group, 0:PAIR] = mix[group]
        mix_tile[group, PAIR:128] = jnp.zeros((128 - PAIR, CT), BF16)
        values = values + dot(gated, mix_tile[group])
    total[...] = values
    normed = layer_norm(values).astype(BF16)
    for c in range(count):
        for copy in copies[c]:
            copy.wait()
        gate = dot(normed, wide[:, c * step : (c + 1) * step])
        up = dot(normed, wide[:, TRANS + c * step : TRANS + (c + 1) * step])
        hidden[:, c * step : (c + 1) * step] = (jax.nn.silu(gate) * up).astype(BF16)
    rounded = (total[...] + dot(hidden[...], narrow[...])).astype(BF16)
    state[...] = rounded.reshape(SEEDS, TOKS, CT)
    carried = dot(rounded, spread_weight[...]).astype(BF16).reshape(SEEDS, TOKS, CA)
    spread[...] = carried
    first[:, :EDGE] = carried[:, :EDGE]
    first[:, EDGE:] = enc_first[...]
    last[:, :EDGE] = carried[:, TOKS - EDGE :]
    last[:, EDGE:] = enc_last[...]


def finish(residual, own, received, mix, wide, narrow, spread_weight, enc_first, enc_last):
    return pl.pallas_call(
        finish_kernel,
        out_shape=(
            jax.ShapeDtypeStruct((SEEDS, TOKS, CT), BF16),
            jax.ShapeDtypeStruct((SEEDS, TOKS, CA), BF16),
            jax.ShapeDtypeStruct((SEEDS, EDGE + MARGIN, CA), BF16),
            jax.ShapeDtypeStruct((SEEDS, EDGE + MARGIN, CA), BF16),
        ),
        in_specs=vmem(4) + anywhere(2) + vmem(3),
        out_specs=tuple(vmem(4)),
        scratch_shapes=[
            pltpu.VMEM((CT, 2 * TRANS), BF16),
            pltpu.VMEM((TRANS, CT), BF16),
            pltpu.VMEM((GROUPS, 128, CT), BF16),
            pltpu.VMEM((SEEDS * TOKS, CT), F32),
            pltpu.VMEM((SEEDS * TOKS, TRANS), BF16),
            pltpu.SemaphoreType.DMA((3, 3)),
        ],
        compiler_params=params(40),
        cost_estimate=SMALL,
        name="finish",
    )(residual, own, received, mix, wide, narrow, spread_weight, enc_first, enc_last)


def along_tok(values, by):
    return lax.ppermute(values, "tok", [(i, (i + by) % 16) for i in range(16)])


def across_core(values):
    return lax.ppermute(values, "tok", [(i, i ^ 1) for i in range(16)])


def along_x(values, by):
    return lax.ppermute(values, "tok", [(i, i // 8 * 8 + (i + 2 * by) % 8) for i in range(16)])


def across_floor(values):
    return lax.ppermute(values, "tok", [(i, i ^ 8) for i in range(16)])


def along_y(values, by):
    return lax.ppermute(values, "seed", [(i, (i + 2 * by) % 8) for i in range(8)])


def along_z(values):
    return lax.ppermute(values, "seed", [(i, i ^ 1) for i in range(8)])


def per_device(
    atom_feats, atom_index, token_cond, pair_bias, atom_bias_enc, atom_bias_dec,
    enc_project, enc_mix, pool_weight, token_project, token_mix, swiglu_in, swiglu_out,
    spread_weight, dec_project, dec_mix,
):
    tok = lax.axis_index("tok")
    seed = lax.axis_index("seed")
    place = jnp.stack([tok, tok % 2]).astype(jnp.int32)
    feats = atom_feats.reshape(SEEDS * ATOMS, CA)
    bias_enc = atom_bias_enc.reshape(4 * ATOMS, WIN)
    bias_dec = atom_bias_dec.reshape(4 * ATOMS, WIN)
    index = atom_index.reshape(8, CA)

    up, down, send, joined = pack(place, feats, bias_enc, index, pair_bias)
    low = along_tok(up, 1)
    high = along_tok(down, -1)
    mine = join(joined, across_core(send), low, high)
    below = along_y(mine, 1)
    above = along_y(mine, -1)
    other = along_z(mine)

    encoded, first, last, residual, normed, again = encode(
        place, feats, low, high, bias_enc, index, token_cond, enc_project, enc_mix, pool_weight,
        mine,
    )
    x_below = along_x(normed, 1)
    x_above = along_x(normed, -1)
    below, above, again, mine = hold(below, above, again, mine)
    far = along_y(mine, 2)
    z_own = across_floor(again)
    mate = across_core(again)
    x_far = along_x(again, 2)
    weights = spaced(place, token_project, below)
    z_own, x_below, x_above, x_far, weights, other = hold(
        z_own, x_below, x_above, x_far, weights, other
    )
    z_below = along_x(z_own, 1)
    z_above = along_x(z_own, -1)
    z_far = across_floor(x_far)
    near = stack(again, x_below, x_above, z_own)
    near_mate = across_core(near)
    query, gate = queries(place, again, mate, weights, z_own)
    far, other, z_below, z_above, query = hold(far, other, z_below, z_above, query)
    other_below = along_y(other, 1)
    other_above = along_y(other, -1)
    other_far = along_z(far)
    rest = stack(x_far, z_below, z_above, z_far)
    rest_mate = across_core(rest)

    column, floor, core = tok // 2 % 4, tok // 8, tok % 2

    def shards(*offsets):
        return jnp.stack(
            [
                (floor ^ dz) * 8 + (column + dx) % 4 * 2 + (core ^ side)
                for side in (0, 1)
                for dx, dz in offsets
            ]
        ).astype(jnp.int32)

    key_value = keys(
        place, shards((0, 0), (3, 0), (1, 0), (0, 1)), near, near_mate, weights
    )
    key_value = keys(
        place, shards((2, 0), (3, 1), (1, 1), (2, 1)), rest, rest_mate, weights, key_value
    )

    level, side = seed // 2, seed % 2

    def ids(*offsets):
        return jnp.stack([(level + dy) % 4 * 2 + (side ^ dz) for dy, dz in offsets]).astype(jnp.int32)

    done = attend(
        ids((0, 0), (3, 0), (1, 0), (2, 0), (0, 1)), query, gate, key_value, (),
        (mine, below, above, far, other),
    )
    own, sent = attend(
        ids((3, 1), (1, 1), (2, 1)), query, gate, key_value, done,
        (other_below, other_above, other_far),
    )

    state, spread, edge_first, edge_last = finish(
        residual, own, across_core(sent), token_mix.reshape(GROUPS, PAIR, CT), swiglu_in,
        swiglu_out, spread_weight, first, last,
    )
    update = decode(
        place, encoded, spread, along_tok(edge_last, 1), along_tok(edge_first, -1), bias_dec, index, low, high, dec_project, dec_mix,
    )
    return state.transpose(1, 0, 2), update.reshape(ATOMS, SEEDS, CA)


def solution(mesh):
    placed = (
        P("tok", "seed", None),
        P("tok"),
        P("tok", None),
        P("seed", "tok", None),
        P("tok", None, None),
        P("tok", None, None),
    ) + (P(),) * 10
    return jax.shard_map(
        per_device,
        mesh=mesh,
        in_specs=placed,
        out_specs=(P("tok", "seed", None), P("tok", "seed", None)),
        check_vma=False,
    )
```

```python
import functools

import jax
import jax.numpy as jnp
from jax import lax
from jax.experimental import pallas as pl
from jax.experimental.pallas import tpu as pltpu
from jax.sharding import PartitionSpec as P

EPS = 1e-05
NEG = -1000000000.0
F32 = jnp.float32
BF16 = jnp.bfloat16

SEEDS = 2
ATOMS = 1024
TOKS = 128
CA = 128
CT = 768
HEADS = 16
HEAD = 48
PAIR = 96
GROUPS = 8
QB = 32
WIN = 128
MARGIN = 48
LOWER = 80
EXT = 1152
EDGE = 16
TRANS = 1536
ALL_TOKS = 2048
ALL_ATOMS = 16384
UP_ROWS = 2 * LOWER + 4 * QB + 16
DOWN_ROWS = 2 * MARGIN + 16


SMALL = pl.CostEstimate(flops=10**6, bytes_accessed=10**4, transcendentals=0)
LARGE = pl.CostEstimate(flops=7 * 10**10, bytes_accessed=10**4, transcendentals=0)


def params(limit_mb, **more):
    return pltpu.CompilerParams(vmem_limit_bytes=limit_mb * 1024 * 1024, **more)


def vmem(n):
    return [pl.BlockSpec(memory_space=pltpu.VMEM)] * n


def anywhere(n):
    return [pl.BlockSpec(memory_space=pltpu.HBM)] * n


def layer_norm(values):
    centre = values - jnp.mean(values, axis=-1, keepdims=True)
    variance = jnp.mean(centre * centre, axis=-1, keepdims=True)
    return centre * lax.rsqrt(variance + EPS)


def dot(a, b):
    return jnp.dot(a, b, preferred_element_type=F32)


def dot_t(a, b):
    return lax.dot_general(a, b, (((1,), (1,)), ((), ())), preferred_element_type=F32)


def window_blocks(packed, bias, mixed, blocks, first_atom, unroll):
    lane_head = lax.broadcasted_iota(jnp.int32, (QB, CA), 1) // 32
    head_mask = [(lane_head == h).astype(BF16) for h in range(4)]
    lane = lax.broadcasted_iota(jnp.int32, (1, WIN), 1)
    ones = jnp.ones((WIN, CA), BF16)
    for b in (0, 1, 2, blocks - 2, blocks - 1):
        position = lane + (first_atom + b * QB)
        inside = (position >= 0) & (position < ALL_ATOMS)
        place = slice(b * 4 * QB, (b + 1) * 4 * QB)
        bias[place] = jnp.where(inside, bias[place], NEG)

    def body(i, carry):
        work = []
        for u in range(unroll):
            b = i * unroll + u
            rows = pl.multiple_of(b * QB, QB)
            query_rows = pl.multiple_of(b * QB + MARGIN, 16)
            bias_rows = pl.multiple_of(b * 4 * QB, 4 * QB)
            added = jnp.concatenate(
                [bias[pl.ds(bias_rows + h, QB, stride=4), :] for h in range(4)], axis=0
            )
            for seed in range(SEEDS):
                work.append((rows, query_rows, added, seed))
        scores = []
        for rows, query_rows, added, seed in work:
            query = packed[seed, pl.ds(query_rows, QB), 0:CA]
            key = packed[seed, pl.ds(rows, WIN), CA : 2 * CA]
            stacked = jnp.concatenate([query * head_mask[h] for h in range(4)], axis=0)
            scores.append(dot_t(stacked, key) * (32**-0.5) + added)
        weights = [jnp.exp(s - jnp.max(s, axis=-1, keepdims=True)).astype(BF16) for s in scores]
        for (rows, _, _, seed), w in zip(work, weights):
            value = jnp.concatenate([packed[seed, pl.ds(rows, WIN), 2 * CA : 3 * CA], ones], axis=1)
            out = dot(w, value)
            joined = out[3 * QB :]
            for h in range(3):
                joined = jnp.where(jnp.concatenate([lane_head, lane_head], axis=1) == h, out[h * QB : (h + 1) * QB], joined)
            mixed[seed, pl.ds(rows, QB), :] = (joined[:, :CA] / joined[:, CA:]).astype(BF16)
        return carry

    lax.fori_loop(0, blocks // unroll, body, 0)


def pack_kernel(place, feats, bias, index, pair_bias, up, down, send, joined, heads, rows, sems):
    base, core = place[0] * TOKS, place[1]
    low_rows, high_rows = UP_ROWS - 16, DOWN_ROWS - 16
    loads = (
        (pair_bias, heads),
        (feats.at[pl.ds(2 * (ATOMS - LOWER), 2 * LOWER)], rows.at[pl.ds(0, 2 * LOWER)]),
        (bias.at[pl.ds(4 * (ATOMS - QB), 4 * QB)], rows.at[pl.ds(2 * LOWER, 4 * QB)]),
        (feats.at[pl.ds(0, 2 * MARGIN)], rows.at[pl.ds(UP_ROWS, 2 * MARGIN)]),
    )
    loads = [pltpu.make_async_copy(a, b, sems.at[i]) for i, (a, b) in enumerate(loads)]
    for copy in loads:
        copy.start()
    tail = (index[7:8] - (base + TOKS)).astype(F32)
    head = (index[0:1] - base).astype(F32)
    rows[low_rows:UP_ROWS] = jnp.broadcast_to(tail, (16, CA)).astype(BF16)
    rows[UP_ROWS + high_rows :] = jnp.broadcast_to(head, (16, CA)).astype(BF16)
    stores = (
        (rows.at[pl.ds(0, UP_ROWS)], up),
        (rows.at[pl.ds(UP_ROWS, DOWN_ROWS)], down),
        (heads.at[1 - core], send),
        (heads.at[core], joined.at[pl.ds(0, TOKS)]),
    )
    stores = [pltpu.make_async_copy(a, b, sems.at[4 + i]) for i, (a, b) in enumerate(stores)]
    for copy in loads[1:]:
        copy.wait()
    stores[0].start()
    stores[1].start()
    loads[0].wait()
    stores[2].start()
    stores[3].start()
    for copy in stores:
        copy.wait()


def pack(place, feats, bias, index, pair_bias):
    return pl.pallas_call(
        pack_kernel,
        out_shape=(
            jax.ShapeDtypeStruct((UP_ROWS, CA), BF16),
            jax.ShapeDtypeStruct((DOWN_ROWS, CA), BF16),
            jax.ShapeDtypeStruct((TOKS, ALL_TOKS), BF16),
            jax.ShapeDtypeStruct((2 * TOKS, ALL_TOKS), BF16),
        ),
        in_specs=[pl.BlockSpec(memory_space=pltpu.SMEM)] + anywhere(2) + vmem(1) + anywhere(1),
        out_specs=tuple(anywhere(4)),
        scratch_shapes=[
            pltpu.VMEM((2, TOKS, ALL_TOKS), BF16),
            pltpu.VMEM((UP_ROWS + DOWN_ROWS, CA), BF16),
            pltpu.SemaphoreType.DMA((8,)),
        ],
        compiler_params=params(58),
        cost_estimate=SMALL,
        name="pack",
    )(place, feats, bias, index, pair_bias)


def join_kernel(joined, received, low, high, out, rows, sems):
    load = pltpu.make_async_copy(received, rows, sems.at[0])
    load.start()
    load.wait()
    store = pltpu.make_async_copy(rows, out.at[pl.ds(TOKS, TOKS)], sems.at[1])
    store.start()
    store.wait()


def join(joined, received, low, high):
    return pl.pallas_call(
        join_kernel,
        out_shape=jax.ShapeDtypeStruct(joined.shape, BF16),
        in_specs=anywhere(4),
        out_specs=anywhere(1)[0],
        input_output_aliases={0: 0},
        scratch_shapes=[pltpu.VMEM((TOKS, ALL_TOKS), BF16), pltpu.SemaphoreType.DMA((2,))],
        compiler_params=params(58),
        cost_estimate=SMALL,
        name="join",
    )(joined, received, low, high)


def hold_kernel(*refs):
    del refs


def hold(*arrays, cost=SMALL):
    return pl.pallas_call(
        hold_kernel,
        out_shape=tuple(jax.ShapeDtypeStruct(array.shape, array.dtype) for array in arrays),
        in_specs=anywhere(len(arrays)),
        out_specs=tuple(anywhere(len(arrays))),
        input_output_aliases={i: i for i in range(len(arrays))},
        compiler_params=params(58),
        cost_estimate=cost,
        name="hold",
    )(*arrays)


def encode_kernel(
    place, feats, low, high, bias, index, cond, project, mix, pool, fence,
    encoded, first, last, residual, normed, again,
    rows, bias32, packed, mixed, ext,
):
    rows[0 : 2 * LOWER] = low[0 : 2 * LOWER].astype(F32)
    rows[2 * LOWER : 2 * (LOWER + ATOMS)] = feats[...].astype(F32)
    rows[2 * (LOWER + ATOMS) : 2 * EXT] = high[0 : 2 * MARGIN].astype(F32)
    bias32[0 : 4 * QB] = low[2 * LOWER : 2 * LOWER + 4 * QB].astype(F32)
    bias32[4 * QB :] = bias[...].astype(F32)
    for seed in range(SEEDS):
        values = rows[pl.ds(seed, EXT, stride=2), :]
        packed[seed] = dot(layer_norm(values).astype(BF16), project[...]).astype(BF16)
    window_blocks(packed, bias32, mixed, 33, place[0] * ATOMS - QB - MARGIN, 11)
    token = lax.broadcasted_iota(jnp.int32, (TOKS, CA), 0)
    below = low[2 * LOWER + 4 * QB :].astype(F32)[0:1].astype(jnp.int32)
    below = jnp.where(place[0] == 0, -1000, below)
    base = place[0] * TOKS
    chosen = jnp.concatenate(
        [(index[i : i + 1] - base == token).astype(F32) for i in range(8)]
        + [(below == token).astype(F32)],
        axis=1,
    )
    counts = jnp.sum(chosen, axis=1, keepdims=True)
    chosen = chosen.astype(BF16)
    for seed in range(SEEDS):
        values = rows[pl.ds(2 * MARGIN + seed, QB + ATOMS, stride=2), :]
        result = (values + dot(mixed[seed], mix[...])).astype(BF16)
        ext[0:ATOMS] = result[QB:]
        ext[ATOMS : EXT - QB] = jnp.zeros((EXT - QB - ATOMS, CA), BF16)
        ext[EXT - QB :] = result[0:QB]
        encoded[seed] = ext[0:ATOMS]
        first[seed] = ext[0:MARGIN]
        last[seed] = ext[ATOMS - MARGIN : ATOMS]
        lifted = jnp.maximum(dot(ext[...], pool[...]), 0.0).astype(BF16)
        state = cond[...].astype(F32) + dot(chosen, lifted) / counts
        residual[seed] = state
        normed[seed] = layer_norm(state).astype(BF16)
        again[seed] = normed[seed]


def encode(*args):
    return pl.pallas_call(
        encode_kernel,
        out_shape=(
            jax.ShapeDtypeStruct((SEEDS, ATOMS, CA), BF16),
            jax.ShapeDtypeStruct((SEEDS, MARGIN, CA), BF16),
            jax.ShapeDtypeStruct((SEEDS, MARGIN, CA), BF16),
            jax.ShapeDtypeStruct((SEEDS, TOKS, CT), F32),
            jax.ShapeDtypeStruct((SEEDS, TOKS, CT), BF16),
            jax.ShapeDtypeStruct((SEEDS, TOKS, CT), BF16),
        ),
        in_specs=[pl.BlockSpec(memory_space=pltpu.SMEM)] + vmem(9) + anywhere(1),
        out_specs=tuple(vmem(6)),
        scratch_shapes=[
            pltpu.VMEM((2 * EXT, CA), F32),
            pltpu.VMEM((33 * 4 * QB, WIN), F32),
            pltpu.VMEM((SEEDS, EXT, 3 * CA), BF16),
            pltpu.VMEM((SEEDS, QB + ATOMS, CA), BF16),
            pltpu.VMEM((EXT, CA), BF16),
        ],
        compiler_params=params(58),
        cost_estimate=SMALL,
        name="encode",
    )(*args)


def decode_kernel(
    place, enc, spread, edge_low, edge_high, bias, index, low, high,
    project, mix,
    update,
    rows, bias32, packed, mixed, decoded, tokens, moved,
):
    bias32[...] = bias[...].astype(F32)
    token = lax.broadcasted_iota(jnp.int32, (TOKS + 2 * EDGE, CA), 0) - EDGE
    below = low[2 * LOWER + 4 * QB :].astype(F32)[0:1].astype(jnp.int32)
    above = high[2 * MARGIN :].astype(F32)[0:1].astype(jnp.int32) + TOKS
    base = place[0] * TOKS
    chosen = jnp.concatenate(
        [(index[i : i + 1] - base == token).astype(F32) for i in range(8)]
        + [(below == token).astype(F32), (above == token).astype(F32)],
        axis=1,
    ).astype(BF16)
    end = MARGIN + ATOMS
    for seed in range(SEEDS):
        tokens[0:EDGE] = edge_low[seed, 0:EDGE]
        tokens[EDGE : EDGE + TOKS] = spread[seed]
        tokens[EDGE + TOKS :] = edge_high[seed, 0:EDGE]
        moved[...] = lax.dot_general(
            chosen, tokens[...], (((0,), (0,)), ((), ())), preferred_element_type=F32
        )
        decoded[0:MARGIN] = edge_low[seed, EDGE:].astype(F32) + moved[ATOMS + CA - MARGIN : ATOMS + CA]
        decoded[MARGIN:end] = enc[seed].astype(F32) + moved[0:ATOMS]
        decoded[end : end + MARGIN] = (
            edge_high[seed, EDGE:].astype(F32) + moved[ATOMS + CA : ATOMS + CA + MARGIN]
        )
        decoded[end + MARGIN :] = jnp.zeros((EXT - end - MARGIN, CA), F32)
        values = decoded[...].astype(BF16).astype(F32)
        rows[pl.ds(seed, EXT, stride=2), :] = values
        packed[seed] = dot(layer_norm(values).astype(BF16), project[...]).astype(BF16)
    window_blocks(packed, bias32, mixed, 32, place[0] * ATOMS - MARGIN, 8)
    for seed in range(SEEDS):
        at = pl.ds(2 * MARGIN + seed, ATOMS, stride=2)
        rows[at, :] = rows[at, :] + dot(mixed[seed], mix[...])
    update[...] = rows[2 * MARGIN : 2 * (MARGIN + ATOMS)].astype(BF16)


def decode(*args):
    return pl.pallas_call(
        decode_kernel,
        out_shape=jax.ShapeDtypeStruct((SEEDS * ATOMS, CA), BF16),
        in_specs=[pl.BlockSpec(memory_space=pltpu.SMEM)] + vmem(10),
        out_specs=vmem(1)[0],
        scratch_shapes=[
            pltpu.VMEM((2 * EXT, CA), F32),
            pltpu.VMEM((32 * 4 * QB, WIN), F32),
            pltpu.VMEM((SEEDS, EXT, 3 * CA), BF16),
            pltpu.VMEM((SEEDS, ATOMS, CA), BF16),
            pltpu.VMEM((EXT, CA), F32),
            pltpu.VMEM((TOKS + 2 * EDGE, CA), BF16),
            pltpu.VMEM((ATOMS + 2 * CA, CA), F32),
        ],
        compiler_params=params(30),
        cost_estimate=SMALL,
        name="decode",
    )(*args)


def spaced_kernel(place, first, second, fence, out):
    core = place[1]
    for group in range(4):
        start = PAIR * group // 128 * 128
        shift = PAIR * group - start + HEAD * core
        width = min(256, 384 - start)
        row = lax.broadcasted_iota(jnp.int32, (width, 128), 0) - shift
        lane = lax.broadcasted_iota(jnp.int32, (width, 128), 1)

        def pick(side):
            at = lane - HEAD * side
            return ((row == at) & (at >= 0) & (at < HEAD)).astype(F32).astype(BF16)

        block = dot(first[:, start : start + width], pick(1 - core)) + dot(
            second[:, start : start + width], pick(core)
        )
        out[0, group // 2, :, group % 2 * 128 : group % 2 * 128 + 128] = block.astype(BF16)


def spaced(place, weight, fence):
    return pl.pallas_call(
        spaced_kernel,
        grid=(4,),
        out_shape=jax.ShapeDtypeStruct((2, GROUPS // 2, CT, 256), BF16),
        in_specs=[
            pl.BlockSpec(memory_space=pltpu.SMEM),
            pl.BlockSpec((CT, 384), lambda i: (0, i)),
            pl.BlockSpec((CT, 384), lambda i: (0, jnp.where(i < 2, 6 + i, 2 + i))),
        ]
        + anywhere(1),
        out_specs=pl.BlockSpec((1, 2, CT, 256), lambda i: (i // 2, i % 2, 0, 0)),
        compiler_params=params(58),
        cost_estimate=LARGE,
        name="spaced",
    )(place, weight, weight, fence)


def queries_kernel(place, normed, other, weight, fence, query, gate):
    core = place[1]
    lane = lax.broadcasted_iota(jnp.int32, (1, 128), 1)
    in_query = (lane // HEAD == 1 - core) & (lane < PAIR)
    in_gate = (lane // HEAD == core) & (lane < PAIR)
    values = jnp.concatenate([normed[0], other[0], normed[1], other[1]], axis=0)
    for pair in range(GROUPS // 2):
        product = dot(values, weight[0, pair])
        for side in range(2):
            part = product[:, side * 128 : side * 128 + 128]
            group = 2 * pair + side
            queried = jnp.where(in_query, part * (HEAD**-0.5), 0.0).astype(BF16)
            opened = jnp.where(in_gate, jax.nn.sigmoid(part), 0.0).astype(BF16)
            for seed in range(SEEDS):
                at = slice(seed * 2 * TOKS, (seed + 1) * 2 * TOKS)
                query[group, seed] = queried[at]
                gate[group, seed] = opened[at]


def queries(place, normed, other, weight, fence):
    return pl.pallas_call(
        queries_kernel,
        grid=(1,),
        out_shape=(
            jax.ShapeDtypeStruct((GROUPS, SEEDS, 2 * TOKS, 128), BF16),
            jax.ShapeDtypeStruct((GROUPS, SEEDS, 2 * TOKS, 128), BF16),
        ),
        in_specs=[pl.BlockSpec(memory_space=pltpu.SMEM)]
        + vmem(2)
        + [pl.BlockSpec((1, GROUPS // 2, CT, 256), lambda i: (0, 0, 0, 0))]
        + anywhere(1),
        out_specs=tuple(vmem(2)),
        compiler_params=params(50),
        cost_estimate=SMALL,
        name="queries",
    )(place, normed, other, weight, fence)


def stack_kernel(*refs):
    for i, ref in enumerate(refs[:-1]):
        refs[-1][i] = ref[...]


def stack(*chunks):
    return pl.pallas_call(
        stack_kernel,
        out_shape=jax.ShapeDtypeStruct((len(chunks),) + chunks[0].shape, BF16),
        in_specs=vmem(len(chunks)),
        out_specs=vmem(1)[0],
        compiler_params=params(50),
        cost_estimate=SMALL,
        name="stack",
    )(*chunks)


def keys_kernel(place, own, received, weight, *rest):
    out, tiles, sems = rest[-3:]
    chunks = [ref.at[i] for ref in (own, received) for i in range(ref.shape[0])]
    values = jnp.concatenate([chunk[...].reshape(SEEDS * TOKS, CT) for chunk in chunks], axis=0)
    ones = (lax.broadcasted_iota(jnp.int32, (1, 256), 1) % 128 == PAIR).astype(F32)
    copies = []
    for pair in range(GROUPS // 2):
        product = (dot(values, weight[0, pair]) + ones).astype(BF16)
        for i in range(len(chunks)):
            for side in range(2):
                for seed in range(SEEDS):
                    start = (i * SEEDS + seed) * TOKS
                    tiles[i, 2 * pair + side, seed] = product[
                        start : start + TOKS, side * 128 : side * 128 + 128
                    ]
            rows = pl.ds(pl.multiple_of(place[2 + i] * TOKS, TOKS), TOKS)
            copies.append(
                pltpu.make_async_copy(
                    tiles.at[i, pl.ds(2 * pair, 2)],
                    out.at[pl.ds(2 * pair, 2), :, rows],
                    sems.at[pair, i],
                )
            )
            copies[-1].start()
    for copy in copies:
        copy.wait()


def keys(place, ids, own, received, weight, before=None, fences=()):
    more = ([] if before is None else [before]) + list(fences)
    count = own.shape[0] + received.shape[0]
    return pl.pallas_call(
        keys_kernel,
        grid=(1,),
        out_shape=jax.ShapeDtypeStruct((GROUPS, SEEDS, ALL_TOKS, 128), BF16),
        in_specs=[pl.BlockSpec(memory_space=pltpu.SMEM)]
        + vmem(2)
        + [pl.BlockSpec((1, GROUPS // 2, CT, 256), lambda i: (1, 0, 0, 0))]
        + anywhere(len(more)),
        out_specs=anywhere(1)[0],
        scratch_shapes=[
            pltpu.VMEM((count, GROUPS, SEEDS, TOKS, 128), BF16),
            pltpu.SemaphoreType.DMA((GROUPS // 2, count)),
        ],
        input_output_aliases={} if before is None else {4: 0},
        compiler_params=params(50),
        cost_estimate=SMALL,
        name="keys",
    )(jnp.concatenate([place, ids]), own, received, weight, *more)


def attend_kernel(count, extra, group_ids, query, gate, key_value, *rest):
    biases = rest[:count]
    own, sent, slots, scores, sems = rest[count + extra :]
    step = pl.program_id(0)

    def load(i):
        return pltpu.make_async_copy(biases[i], slots.at[i % 2], sems.at[i % 2])

    for i in range(count):

        @pl.when(step == i)
        def _(i=i):
            if i == 0:
                load(0).start()
            if i + 1 < count:
                load(i + 1).start()
            load(i).wait()

    bias = slots.at[step % 2]
    width = 512
    tops = []
    for seed in range(SEEDS):
        peak = None
        for c in range(ALL_TOKS // width):
            cols = slice(c * width, (c + 1) * width)
            part = dot_t(query[0, seed], key_value[0, seed, cols, :]) + bias[:, cols].astype(F32)
            scores[seed, :, cols] = part
            for w in range(width // 128):
                tile = part[:, w * 128 : (w + 1) * 128]
                peak = tile if peak is None else jnp.maximum(peak, tile)
        tops.append(jnp.max(peak, axis=-1, keepdims=True))
    for seed in range(SEEDS):
        total = None
        for c in range(ALL_TOKS // width):
            cols = slice(c * width, (c + 1) * width)
            part = dot(
                jnp.exp(scores[seed, :, cols] - tops[seed]).astype(BF16), key_value[0, seed, cols, :]
            )
            total = part if total is None else total + part
        gated = (total / total[:, PAIR : PAIR + 1] * gate[0, seed].astype(F32)).astype(BF16)
        own[0, seed] = gated[:TOKS]
        sent[0, seed] = gated[TOKS:]


def attend(group_ids, query, gate, key_value, before, biases):
    count = len(biases)
    shape = jax.ShapeDtypeStruct((GROUPS, SEEDS, TOKS, 128), BF16)

    def by_group(*block):
        return pl.BlockSpec((1,) + block, lambda i, ids: (ids[i],) + (0,) * len(block))

    grid_spec = pltpu.PrefetchScalarGridSpec(
        num_scalar_prefetch=1,
        grid=(count,),
        in_specs=[
            by_group(SEEDS, 2 * TOKS, 128),
            by_group(SEEDS, 2 * TOKS, 128),
            by_group(SEEDS, ALL_TOKS, 128),
        ]
        + anywhere(count + len(before)),
        out_specs=(by_group(SEEDS, TOKS, 128),) * 2,
        scratch_shapes=[
            pltpu.VMEM((2, 2 * TOKS, ALL_TOKS), BF16),
            pltpu.VMEM((SEEDS, 2 * TOKS, ALL_TOKS), F32),
            pltpu.SemaphoreType.DMA((2,)),
        ],
    )
    return pl.pallas_call(
        functools.partial(attend_kernel, count, len(before)),
        grid_spec=grid_spec,
        out_shape=(shape, shape),
        input_output_aliases={4 + count + i: i for i in range(len(before))},
        compiler_params=params(50),
        cost_estimate=SMALL,
        name="attend",
    )(group_ids, query, gate, key_value, *biases, *before)


def finish_kernel(
    residual, own, received, mix, wide_hbm, narrow_hbm, spread_weight, enc_first, enc_last,
    state, spread, first, last,
    wide, narrow, mix_tile, total, hidden, sems,
):
    step = 512
    count = TRANS // step
    copies = []
    for c in range(count):
        gate_cols = pl.ds(c * step, step)
        up_cols = pl.ds(TRANS + c * step, step)
        copies.append(
            [
                pltpu.make_async_copy(wide_hbm.at[:, gate_cols], wide.at[:, gate_cols], sems.at[c, 0]),
                pltpu.make_async_copy(wide_hbm.at[:, up_cols], wide.at[:, up_cols], sems.at[c, 1]),
                pltpu.make_async_copy(narrow_hbm.at[gate_cols], narrow.at[gate_cols], sems.at[c, 2]),
            ]
        )
    for group in copies:
        for copy in group:
            copy.start()
    values = residual[...].reshape(SEEDS * TOKS, CT)
    for group in range(GROUPS):
        gated = (own[group] + received[group]).reshape(SEEDS * TOKS, 128)
        mix_tile[group, 0:PAIR] = mix[group]
        mix_tile[group, PAIR:128] = jnp.zeros((128 - PAIR, CT), BF16)
        values = values + dot(gated, mix_tile[group])
    total[...] = values
    normed = layer_norm(values).astype(BF16)
    for c in range(count):
        for copy in copies[c]:
            copy.wait()
        gate = dot(normed, wide[:, c * step : (c + 1) * step])
        up = dot(normed, wide[:, TRANS + c * step : TRANS + (c + 1) * step])
        hidden[:, c * step : (c + 1) * step] = (jax.nn.silu(gate) * up).astype(BF16)
    rounded = (total[...] + dot(hidden[...], narrow[...])).astype(BF16)
    state[...] = rounded.reshape(SEEDS, TOKS, CT)
    carried = dot(rounded, spread_weight[...]).astype(BF16).reshape(SEEDS, TOKS, CA)
    spread[...] = carried
    first[:, :EDGE] = carried[:, :EDGE]
    first[:, EDGE:] = enc_first[...]
    last[:, :EDGE] = carried[:, TOKS - EDGE :]
    last[:, EDGE:] = enc_last[...]


def finish(residual, own, received, mix, wide, narrow, spread_weight, enc_first, enc_last):
    return pl.pallas_call(
        finish_kernel,
        out_shape=(
            jax.ShapeDtypeStruct((SEEDS, TOKS, CT), BF16),
            jax.ShapeDtypeStruct((SEEDS, TOKS, CA), BF16),
            jax.ShapeDtypeStruct((SEEDS, EDGE + MARGIN, CA), BF16),
            jax.ShapeDtypeStruct((SEEDS, EDGE + MARGIN, CA), BF16),
        ),
        in_specs=vmem(4) + anywhere(2) + vmem(3),
        out_specs=tuple(vmem(4)),
        scratch_shapes=[
            pltpu.VMEM((CT, 2 * TRANS), BF16),
            pltpu.VMEM((TRANS, CT), BF16),
            pltpu.VMEM((GROUPS, 128, CT), BF16),
            pltpu.VMEM((SEEDS * TOKS, CT), F32),
            pltpu.VMEM((SEEDS * TOKS, TRANS), BF16),
            pltpu.SemaphoreType.DMA((3, 3)),
        ],
        compiler_params=params(40),
        cost_estimate=SMALL,
        name="finish",
    )(residual, own, received, mix, wide, narrow, spread_weight, enc_first, enc_last)


def along_tok(values, by):
    return lax.ppermute(values, "tok", [(i, (i + by) % 16) for i in range(16)])


def across_core(values):
    return lax.ppermute(values, "tok", [(i, i ^ 1) for i in range(16)])


def along_x(values, by):
    return lax.ppermute(values, "tok", [(i, i // 8 * 8 + (i + 2 * by) % 8) for i in range(16)])


def across_floor(values):
    return lax.ppermute(values, "tok", [(i, i ^ 8) for i in range(16)])


def along_y(values, by):
    return lax.ppermute(values, "seed", [(i, (i + 2 * by) % 8) for i in range(8)])


def along_z(values):
    return lax.ppermute(values, "seed", [(i, i ^ 1) for i in range(8)])


def per_device(
    atom_feats, atom_index, token_cond, pair_bias, atom_bias_enc, atom_bias_dec,
    enc_project, enc_mix, pool_weight, token_project, token_mix, swiglu_in, swiglu_out,
    spread_weight, dec_project, dec_mix,
):
    tok = lax.axis_index("tok")
    seed = lax.axis_index("seed")
    place = jnp.stack([tok, tok % 2]).astype(jnp.int32)
    feats = atom_feats.reshape(SEEDS * ATOMS, CA)
    bias_enc = atom_bias_enc.reshape(4 * ATOMS, WIN)
    bias_dec = atom_bias_dec.reshape(4 * ATOMS, WIN)
    index = atom_index.reshape(8, CA)

    up, down, send, joined = pack(place, feats, bias_enc, index, pair_bias)
    low = along_tok(up, 1)
    high = along_tok(down, -1)
    mine = join(joined, across_core(send), low, high)
    below = along_y(mine, 1)
    above = along_y(mine, -1)
    other = along_z(mine)

    encoded, first, last, residual, normed, again = encode(
        place, feats, low, high, bias_enc, index, token_cond, enc_project, enc_mix, pool_weight,
        mine,
    )
    x_below = along_x(normed, 1)
    x_above = along_x(normed, -1)
    below, above, again, mine = hold(below, above, again, mine)
    far = along_y(mine, 2)
    z_own = across_floor(again)
    mate = across_core(again)
    x_far = along_x(again, 2)
    weights = spaced(place, token_project, below)
    z_own, x_below, x_above, x_far, weights, other = hold(
        z_own, x_below, x_above, x_far, weights, other
    )
    z_below = along_x(z_own, 1)
    z_above = along_x(z_own, -1)
    z_far = across_floor(x_far)
    near = stack(again, x_below, x_above, z_own)
    near_mate = across_core(near)
    query, gate = queries(place, again, mate, weights, z_own)
    far, other, z_below, z_above, query = hold(far, other, z_below, z_above, query)
    other_below = along_y(other, 1)
    other_above = along_y(other, -1)
    other_far = along_z(far)
    rest = stack(x_far, z_below, z_above, z_far)
    rest_mate = across_core(rest)

    column, floor, core = tok // 2 % 4, tok // 8, tok % 2

    def shards(*offsets):
        return jnp.stack(
            [
                (floor ^ dz) * 8 + (column + dx) % 4 * 2 + (core ^ side)
                for side in (0, 1)
                for dx, dz in offsets
            ]
        ).astype(jnp.int32)

    key_value = keys(
        place, shards((0, 0), (3, 0), (1, 0), (0, 1)), near, near_mate, weights
    )
    key_value = keys(
        place, shards((2, 0), (3, 1), (1, 1), (2, 1)), rest, rest_mate, weights, key_value
    )

    level, side = seed // 2, seed % 2

    def ids(*offsets):
        return jnp.stack([(level + dy) % 4 * 2 + (side ^ dz) for dy, dz in offsets]).astype(jnp.int32)

    done = attend(
        ids((0, 0), (3, 0), (1, 0), (2, 0), (0, 1)), query, gate, key_value, (),
        (mine, below, above, far, other),
    )
    own, sent = attend(
        ids((3, 1), (1, 1), (2, 1)), query, gate, key_value, done,
        (other_below, other_above, other_far),
    )

    state, spread, edge_first, edge_last = finish(
        residual, own, across_core(sent), token_mix.reshape(GROUPS, PAIR, CT), swiglu_in,
        swiglu_out, spread_weight, first, last,
    )
    update = decode(
        place, encoded, spread, along_tok(edge_last, 1), along_tok(edge_first, -1), bias_dec, index, low, high, dec_project, dec_mix,
    )
    return state.transpose(1, 0, 2), update.reshape(ATOMS, SEEDS, CA)


def solution(mesh):
    placed = (
        P("tok", "seed", None),
        P("tok"),
        P("tok", None),
        P("seed", "tok", None),
        P("tok", None, None),
        P("tok", None, None),
    ) + (P(),) * 10
    return jax.shard_map(
        per_device,
        mesh=mesh,
        in_specs=placed,
        out_specs=(P("tok", "seed", None), P("tok", "seed", None)),
        check_vma=False,
    )
```
